128 devices in a mesh: dp: 16 (over y_hi, z, core), space: 8 (over x, y_lo).
Axes of the slice: x: 4, y: 4 (y_hi: 2, y_lo: 2; y = y_hi * 2 + y_lo), z: 4, core: 2. Of those that a mesh axis runs over, the one named last changes fastest.
Arguments:
- features: bfloat16 [16, 32, 128, 704], P('dp', 'space'), may hold values from -24 to 24
- kernel: float32 [7, 7, 704], replicated, may hold values from -0.875 to 0.875
- norm_gain: float32 [704], replicated, may hold values from 0.1 to 1.9
- w_up: bfloat16 [2816, 704], P('dp'), may hold values from -0.21875 to 0.21875
- grn_gamma: float32 [2816], replicated, may hold values from -2.5 to 2.5
- grn_beta: float32 [2816], replicated, may hold values from -3 to 3
- w_down: bfloat16 [2816, 704], P('dp'), may hold values from -0.109375 to 0.109375
- upstream: bfloat16 [16, 32, 128, 704], P('dp', 'space'), may hold values from -24 to 24
- labels: int32 [16, 32, 128], P('dp', 'space'), may hold values from 0 to 149
- class_weight: float32 [150], replicated, may hold values from 0.3 to 3
Outputs:
- grad_features: float32 [16, 32, 128, 704], P('dp', 'space')
- grad_kernel: float32 [7, 7, 704], replicated
- grad_gain: float32 [704], replicated
- grad_up: float32 [2816, 704], P('dp')
- grad_gamma: float32 [2816], replicated
- grad_beta: float32 [2816], replicated
- grad_down: float32 [2816, 704], P('dp')
The draws below stay inside these ranges and needn't reach their ends.
Inputs may be any that keep to these rules, and one draw needn't show every extreme that they name: `labels`: the class of each pixel.
All inputs are finite; a program needn't handle non-finite values.
Results may differ from the reference program's by a relative error of at most 0.0048.
Values may be sent and summed in bfloat16 or wider, within the bound.
No kernel may reach another device: no remote copies, remote signals or barrier semaphores. Data moves between devices by JAX's collectives and lax.ppermute only.
A program may use at most 128 MiB of HBM per device.

```python
import math
import jax
import jax.numpy as jnp
import numpy as np
from jax import lax

C = 704
HID = 2816
K = 150
COLS = 128
CROPS = 16
ROWS = 32


def draw_features(key, part):
    key = jax.random.fold_in(key, 1)
    noise_key, pattern_key = jax.random.split(key, 2)
    shape = (CROPS, ROWS, COLS, C)
    position = jnp.arange(ROWS, dtype=jnp.float32).reshape(1, ROWS, 1, 1) / (ROWS - 1)
    pattern = jax.random.normal(pattern_key, (CROPS, 1, 1, C), jnp.float32)
    noise = jax.random.normal(noise_key, shape, jnp.float32)
    return jnp.clip(noise + 3.0 * position * pattern, -24.0, 24.0).astype(jnp.bfloat16)


def draw_upstream(key, part):
    key = jax.random.fold_in(key, 2)
    noise_key = jax.random.fold_in(key, 0)
    shape = (CROPS, ROWS, COLS, C)
    position = jnp.arange(ROWS, dtype=jnp.float32).reshape(1, ROWS, 1, 1) / (ROWS - 1)
    rising = 1.0 + 2.0 * position
    noise = jax.random.normal(noise_key, shape, jnp.float32)
    return jnp.clip(noise * rising, -24.0, 24.0).astype(jnp.bfloat16)


def place_ends(entries, rng, low, top_value):
    longest = entries.shape.index(max(entries.shape))
    spots = []
    for shift in (0, 1):
        where = [jax.random.randint(jax.random.fold_in(rng, axis), (), 0, length) for axis, length in enumerate(entries.shape)]
        where[longest] = (where[longest] + shift) % entries.shape[longest]
        spots.append(tuple(where))
    return entries.at[spots[0]].set(low).at[spots[1]].set(top_value)


def level_of(rng, dims, shards, smallest, high):
    def one(axis_at, shards_of):
        steps = jax.random.uniform(jax.random.fold_in(jax.random.fold_in(rng, 6), axis_at), (shards_of,), jnp.float32, smallest / len(shards), high / len(shards))
        return jnp.repeat(jnp.exp(steps), dims[axis_at] // shards_of).reshape((-1,) + (1,) * (len(dims) - axis_at - 1))

    factor_of = one(*shards[0])
    for cut in shards[1:]:
        factor_of = factor_of * one(*cut)
    return factor_of


def rank_bounds(number_of, slope):
    weights = [(1 << 20) // math.isqrt(standing ** slope) + 1 for standing in range(1, number_of + 1)]
    deviation = 1 + sum(weights) // (1 << 30)
    return np.cumsum(np.array([max(1, weight // deviation) for weight in weights]))


def ranked_ids(own_key, shape, amount, slope):
    listing = rank_bounds(amount, slope)
    pick = jax.random.randint(jax.random.fold_in(own_key, 1), shape, 0, int(listing[amount - 1]))
    standing = jnp.searchsorted(jnp.asarray(listing, jnp.int32), pick, side="right")
    return jax.random.permutation(jax.random.fold_in(own_key, 2), amount)[standing].astype(jnp.int32)


def scatter_about(stream_key, extent, deviation, limit, cuts=(), kind=jnp.bfloat16):
    entries = jax.random.normal(stream_key, extent, jnp.float32) * deviation
    if len(cuts) > 0:
        entries = level_of(stream_key, extent, cuts, -0.22, 0.18) * entries
    return jnp.clip(entries, min=-limit, max=limit).astype(kind)


def setup_inputs(seed: int = 0) -> dict:
    splits = jax.random.split(jax.random.key(seed), 11)
    return {
        "features": draw_features(jax.random.fold_in(splits[10], 71), 0),
        "kernel": scatter_about(splits[1], (7, 7, C), 49 ** -0.5, 0.875, (), jnp.float32),
        "norm_gain": jnp.clip(1.0 + 0.18 * jax.random.normal(splits[2], (C,), jnp.float32), 0.1, 1.9),
        "w_up": scatter_about(splits[3], (HID, C), C ** -0.5, 0.21875, ((0, 16),)),
        "grn_gamma": scatter_about(splits[4], (HID,), 0.5, 2.5, (), jnp.float32),
        "grn_beta": scatter_about(splits[5], (HID,), 0.3, 3.0, (), jnp.float32),
        "w_down": scatter_about(splits[6], (HID, C), HID ** -0.5, 0.109375, ((0, 16),)),
        "upstream": draw_upstream(jax.random.fold_in(splits[10], 71), 0),
        "labels": place_ends(ranked_ids(splits[8], (CROPS, ROWS, COLS), K, 2), jax.random.fold_in(splits[8], 3), 0, K - 1).astype(jnp.int32),
        "class_weight": jnp.clip(jnp.exp(jax.random.uniform(splits[9], (K,), jnp.float32, math.log(0.3), math.log(3.0))), 0.3, 3.0),
    }


EPS_NORM = 1e-06

def depthwise(padded, kernel, rows, cols):
    total = jnp.zeros(padded.shape[:1] + (rows, cols, padded.shape[3]), jnp.float32)
    for down in range(7):
        for across in range(7):
            total = total + padded[:, down:down + rows, across:across + cols, :].astype(jnp.float32) * kernel[down, across]
    return total

def transpose_taps(grad_pad, kernel, rows, cols):
    total = jnp.zeros(grad_pad.shape[:1] + (rows, cols, grad_pad.shape[3]), jnp.float32)
    for down in range(7):
        for across in range(7):
            total = total + grad_pad[:, 6 - down:6 - down + rows, 6 - across:6 - across + cols, :] * kernel[down, across]
    return total

def kernel_terms(grad_conv, padded, rows, cols):
    lines = []
    for down in range(7):
        taps = []
        for across in range(7):
            window = padded[:, down:down + rows, across:across + cols, :].astype(jnp.float32)
            taps.append(lax.optimization_barrier(jnp.sum(grad_conv * window, axis=(0, 1, 2))))
        lines.append(jnp.stack(taps, axis=0))
    return jnp.stack(lines, axis=0)

def layer_norm(conv, gain):
    mean = lax.optimization_barrier(jnp.mean(conv, axis=-1, keepdims=True))
    centred = conv - mean
    var = lax.optimization_barrier(jnp.mean(centred * centred, axis=-1, keepdims=True))
    return centred * lax.rsqrt(var + EPS_NORM) * gain

def exact_gelu(value):
    return jax.nn.gelu(value, approximate=False)

def response_norm(act, total_sq, gamma, beta):
    energy = jnp.sqrt(total_sq)
    ratio = energy / (lax.optimization_barrier(jnp.mean(energy, axis=-1, keepdims=True)) + EPS_NORM)
    return gamma * act * ratio[:, None, :] + beta + act

def crop_terms(feat, upstream, labels, kernel, norm_gain, w_up, grn_gamma, grn_beta, w_down, class_weight):
    rows, cols, width = (feat.shape[1], feat.shape[2], feat.shape[3])
    padded = jnp.pad(feat, ((0, 0), (3, 3), (3, 3), (0, 0)))
    conv = depthwise(padded, kernel, rows, cols)
    normed_f, ln_back = jax.vjp(layer_norm, conv, norm_gain)
    normed = normed_f.astype(jnp.bfloat16).reshape(-1, width)
    hidden = lax.dot_general(normed, w_up, (((1,), (1,)), ((), ())), preferred_element_type=jnp.float32)
    act, gelu_back = jax.vjp(exact_gelu, hidden)
    act3 = act.reshape(1, rows * cols, act.shape[1])
    total_sq = lax.optimization_barrier(jnp.sum(act3 * act3, axis=1))
    mixed_f, grn_back = jax.vjp(response_norm, act3, total_sq, grn_gamma, grn_beta)
    mixed = mixed_f.astype(jnp.bfloat16).reshape(-1, act.shape[1])
    classes = jnp.arange(class_weight.shape[0], dtype=jnp.int32)
    pixel_weight = lax.optimization_barrier(jnp.sum(jnp.where(labels[..., None] == classes, class_weight, 0.0), axis=-1))
    pixel_grad = upstream.astype(jnp.float32) * pixel_weight[..., None]
    weighted = pixel_grad.astype(jnp.bfloat16).reshape(-1, width)
    grad_mixed = lax.dot_general(weighted, w_down, (((1,), (1,)), ((), ())), preferred_element_type=jnp.float32)
    grad_act, grad_sq, gamma_part, beta_part = grn_back(grad_mixed.reshape(act3.shape))
    grad_act = grad_act + 2.0 * act3 * grad_sq[:, None, :]
    grad_hidden = gelu_back(grad_act.reshape(act.shape))[0].astype(jnp.bfloat16)
    term_up = lax.dot_general(grad_hidden, normed, (((0,), (0,)), ((), ())), preferred_element_type=jnp.float32)
    term_down = lax.dot_general(mixed, weighted, (((0,), (0,)), ((), ())), preferred_element_type=jnp.float32)
    grad_normed = jnp.dot(grad_hidden, w_up, preferred_element_type=jnp.float32)
    grad_conv, gain_part = ln_back(grad_normed.reshape(1, rows, cols, width))
    grad_pad = jnp.pad(grad_conv, ((0, 0), (3, 3), (3, 3), (0, 0)))
    conv_back = transpose_taps(grad_pad, kernel, rows, cols)
    kernel_part = kernel_terms(grad_conv, padded, rows, cols)
    grad_feat = pixel_grad + conv_back
    return (grad_feat, (term_up, term_down, kernel_part, gain_part, gamma_part, beta_part))

def reference(features, kernel, norm_gain, w_up, grn_gamma, grn_beta, w_down, upstream, labels, class_weight):

    def one_step(carry, items):
        feat, grad_out, label_map = items
        grad_feat, terms = crop_terms(feat[None], grad_out[None], label_map[None], kernel, norm_gain, w_up, grn_gamma, grn_beta, w_down, class_weight)
        carry = tuple((total + term for total, term in zip(carry, terms)))
        return (carry, grad_feat[0])
    zeros = (jnp.zeros((HID, C), jnp.float32), jnp.zeros((HID, C), jnp.float32), jnp.zeros((7, 7, C), jnp.float32), jnp.zeros((C,), jnp.float32), jnp.zeros((HID,), jnp.float32), jnp.zeros((HID,), jnp.float32))
    sums, grad_features = lax.scan(one_step, zeros, (features, upstream, labels))
    scale = 1.0 / math.sqrt(CROPS * ROWS * COLS)
    term_up, term_down, kernel_sum, gain_sum, gamma_sum, beta_sum = sums
    return (grad_features, scale * kernel_sum, scale * gain_sum, scale * term_up, scale * gamma_sum, scale * beta_sum, scale * term_down)
```

```python
import functools
import math

import jax
import jax.numpy as jnp
from jax import lax
from jax.experimental import pallas as pl
from jax.experimental.pallas import tpu as pltpu
from jax.sharding import PartitionSpec as P

EPS_NORM = 1e-06
F32 = jnp.float32
BF16 = jnp.bfloat16
VMEM_LIMIT = 56 * 1024 * 1024
LANES = 128
PAD = 8
TILE = 8
GROUP = 4


def params(*semantics):
    return pltpu.CompilerParams(dimension_semantics=semantics, vmem_limit_bytes=VMEM_LIMIT)


def fill_padded(dst, src, first):
    rows, cols, lanes = src.shape
    zeros = jnp.zeros((rows, PAD, lanes), F32)
    dst[first : first + rows, 0:PAD, :] = zeros
    dst[first : first + rows, PAD + cols : PAD + cols + PAD, :] = zeros
    dst[first : first + rows, PAD : PAD + cols, :] = src[...].astype(F32)


def spread_taps(dst, k_ref, flip):
    for i in range(7):
        for j in range(7):
            tap = k_ref[6 - i, 6 - j : 7 - j, :] if flip else k_ref[i, j : j + 1, :]
            dst[i * 7 + j] = jnp.broadcast_to(tap, (TILE, LANES))


def taps_group(src, taps, pairs, start, acc):
    rows = sorted({r for r, _, _ in pairs})
    for j in range(7):
        for r in rows:
            todo = [(o, i) for rr, o, i in pairs if rr == r]
            xs = [src[r, start + TILE * b + PAD - 3 + j : start + TILE * b + PAD - 3 + j + TILE, :] for b in range(GROUP)]
            for o, i in todo:
                tap = taps[i * 7 + j]
                for b in range(GROUP):
                    acc[o][b] = acc[o][b] + xs[b] * tap
    return acc


def own_pairs():
    return [(s, o, s - o + 3) for s in range(4) for o in range(4)]


def halo_pairs():
    above = [(s, o, s - o) for s in range(3) for o in range(4) if 0 <= s - o <= 6]
    below = [(3 + s, o, s + 7 - o) for s in range(3) for o in range(4) if 0 <= s + 7 - o <= 6]
    return above + below


def conv_own_kernel(flip, feat, k_ref, out, xs, taps):
    fill_padded(xs, feat, 0)
    spread_taps(taps, k_ref, flip)
    cols = feat.shape[1]
    for start in range(0, cols, GROUP * TILE):
        acc = [[jnp.zeros((TILE, LANES), F32) for _ in range(GROUP)] for _ in range(4)]
        acc = taps_group(xs, taps, own_pairs(), start, acc)
        for o in range(4):
            for b in range(GROUP):
                out[o, start + TILE * b : start + TILE * (b + 1), :] = acc[o][b]


def conv_own(feat, kernel, flip):
    rows, cols, width = feat.shape
    chunks = pl.cdiv(width, LANES)
    return pl.pallas_call(
        functools.partial(conv_own_kernel, flip),
        grid=(chunks,),
        in_specs=[
            pl.BlockSpec((rows, cols, LANES), lambda c: (0, 0, c)),
            pl.BlockSpec((7, 7, LANES), lambda c: (0, 0, c)),
        ],
        out_specs=pl.BlockSpec((rows, cols, LANES), lambda c: (0, 0, c)),
        out_shape=jax.ShapeDtypeStruct((rows, cols, width), F32),
        scratch_shapes=[
            pltpu.VMEM((rows, cols + 2 * PAD, LANES), F32),
            pltpu.VMEM((49, TILE, LANES), F32),
        ],
        compiler_params=params("arbitrary"),
        name="conv_own",
    )(feat, kernel)


def conv_norm_kernel(width, chunks, part, above, below, k_ref, gain, normed, xhat, rstd, xs, taps, conv):
    c = pl.program_id(0)
    fill_padded(xs, above, 0)
    fill_padded(xs, below, 3)
    spread_taps(taps, k_ref, False)
    cols = part.shape[1]
    for start in range(0, cols, GROUP * TILE):
        acc = [
            [part[o, start + TILE * b : start + TILE * (b + 1), :] for b in range(GROUP)] for o in range(4)
        ]
        acc = taps_group(xs, taps, halo_pairs(), start, acc)
        for o in range(4):
            for b in range(GROUP):
                conv[c, o * cols + start + TILE * b : o * cols + start + TILE * (b + 1), :] = acc[o][b]

    @pl.when(c == chunks - 1)
    def _():
        last = width - (chunks - 1) * LANES
        block = 64

        def one(t, carry):
            at = pl.multiple_of(t * block, block)
            parts = [conv[n, pl.ds(at, block), :] for n in range(chunks)]
            lane = lax.broadcasted_iota(jnp.int32, (block, LANES), 1)
            inside = lane < last
            parts[-1] = jnp.where(inside, parts[-1], 0.0)
            mean = jnp.sum(sum(parts[1:], parts[0]), axis=-1, keepdims=True) / width
            centred = [p - mean for p in parts]
            centred[-1] = jnp.where(inside, centred[-1], 0.0)
            squares = [p * p for p in centred]
            var = jnp.sum(sum(squares[1:], squares[0]), axis=-1, keepdims=True) / width
            scale = lax.rsqrt(var + EPS_NORM)
            rstd[pl.ds(at, block), :] = jnp.broadcast_to(scale, (block, LANES))
            for n in range(chunks):
                w = min(LANES, width - n * LANES)
                hat = centred[n] * scale
                g = gain[:, n * LANES : n * LANES + w]
                xhat[pl.ds(at, block), n * LANES : n * LANES + w] = hat[:, :w]
                normed[pl.ds(at, block), n * LANES : n * LANES + w] = (hat[:, :w] * g).astype(BF16)
            return carry

        lax.fori_loop(0, (4 * cols) // block, one, 0)


def conv_norm(part, above, below, kernel, gain):
    rows, cols, width = part.shape
    chunks = pl.cdiv(width, LANES)
    pixels = rows * cols
    whole = lambda *s: pl.BlockSpec(s, lambda c: (0,) * len(s))
    return pl.pallas_call(
        functools.partial(conv_norm_kernel, width, chunks),
        grid=(chunks,),
        in_specs=[
            pl.BlockSpec((rows, cols, LANES), lambda c: (0, 0, c)),
            pl.BlockSpec((3, cols, LANES), lambda c: (0, 0, c)),
            pl.BlockSpec((3, cols, LANES), lambda c: (0, 0, c)),
            pl.BlockSpec((7, 7, LANES), lambda c: (0, 0, c)),
            whole(1, width),
        ],
        out_specs=[whole(pixels, width), whole(pixels, width), whole(pixels, LANES)],
        out_shape=[
            jax.ShapeDtypeStruct((pixels, width), BF16),
            jax.ShapeDtypeStruct((pixels, width), F32),
            jax.ShapeDtypeStruct((pixels, LANES), F32),
        ],
        scratch_shapes=[
            pltpu.VMEM((6, cols + 2 * PAD, LANES), F32),
            pltpu.VMEM((49, TILE, LANES), F32),
            pltpu.VMEM((chunks, pixels, LANES), F32),
        ],
        compiler_params=params("arbitrary"),
        name="conv_norm",
    )(part, above, below, kernel, gain.reshape(1, width))


def up_kernel(normed, weighted, w_up, w_down, act_ref, slope_ref, gm_ref, sums):
    nt = (((1,), (1,)), ((), ()))
    hidden = lax.dot_general(normed[...], w_up[...], nt, preferred_element_type=F32)
    gm = lax.dot_general(weighted[...], w_down[...], nt, preferred_element_type=F32)
    cdf = 0.5 * (1.0 + lax.erf(hidden * (2.0**-0.5)))
    act = hidden * cdf
    slope = cdf + hidden * (jnp.exp(hidden * hidden * -0.5) * (1.0 / math.sqrt(2.0 * math.pi)))
    act_ref[...] = act
    slope_ref[...] = slope
    gm_ref[...] = gm
    sums[0:1, :] = jnp.sum(act * act, axis=0, keepdims=True)
    sums[1:2, :] = jnp.sum(gm * act, axis=0, keepdims=True)
    sums[2:3, :] = jnp.sum(gm, axis=0, keepdims=True)
    sums[3:8, :] = jnp.zeros((5, sums.shape[1]), F32)


def up_project(normed, weighted, w_up, w_down, block=256):
    pixels, width = normed.shape
    hid = w_up.shape[0]
    whole = pl.BlockSpec((pixels, width), lambda h: (0, 0))
    rows = pl.BlockSpec((block, width), lambda h: (h, 0))
    cols = pl.BlockSpec((pixels, block), lambda h: (0, h))
    big = jax.ShapeDtypeStruct((pixels, hid), F32)
    return pl.pallas_call(
        up_kernel,
        grid=(hid // block,),
        in_specs=[whole, whole, rows, rows],
        out_specs=[cols, cols, cols, pl.BlockSpec((8, block), lambda h: (0, h))],
        out_shape=[big, big, big, jax.ShapeDtypeStruct((8, hid), F32)],
        compiler_params=params("arbitrary"),
        name="up_project",
    )(normed, weighted, w_up, w_down)


def ratio_of(sums, gamma):
    energy = jnp.sqrt(sums[0:1, :])
    hid = energy.shape[1]
    mean = jnp.sum(energy, axis=1, keepdims=True) / hid + EPS_NORM
    ratio = energy / mean
    grad_ratio = gamma * sums[1:2, :]
    shared = jnp.sum(grad_ratio * energy, axis=1, keepdims=True) / (mean * mean) / hid
    grad_energy = grad_ratio / mean - shared
    return ratio, grad_energy / energy


def down_kernel(act, weighted, sums, gamma, beta, down_term, ratio, twice, parts):
    h = pl.program_id(0)
    block = act.shape[1]

    @pl.when(h == 0)
    def _():
        r, t = ratio_of(sums, gamma[...])
        ratio[...] = r
        twice[...] = t
        parts[0:1, :] = sums[1:2, :] * r
        parts[1:2, :] = sums[2:3, :]
        parts[2:8, :] = jnp.zeros((6, r.shape[1]), F32)

    here = pl.ds(pl.multiple_of(h * block, block), block)
    a = act[...]
    mixed = (gamma[:, here] * a * ratio[:, here] + beta[:, here] + a).astype(BF16)
    down_term[...] = lax.dot_general(
        mixed, weighted[...], (((0,), (0,)), ((), ())), preferred_element_type=F32
    ).astype(BF16)


def down_grad(act, weighted, sums, gamma, beta, block=256):
    pixels, hid = act.shape
    width = weighted.shape[1]
    whole = lambda *s: pl.BlockSpec(s, lambda h: (0,) * len(s))
    return pl.pallas_call(
        down_kernel,
        grid=(hid // block,),
        in_specs=[
            pl.BlockSpec((pixels, block), lambda h: (0, h)),
            whole(pixels, width),
            whole(8, hid),
            whole(1, hid),
            whole(1, hid),
        ],
        out_specs=[
            pl.BlockSpec((block, width), lambda h: (h, 0)),
            whole(1, hid),
            whole(1, hid),
            whole(8, hid),
        ],
        out_shape=[
            jax.ShapeDtypeStruct((hid, width), BF16),
            jax.ShapeDtypeStruct((1, hid), F32),
            jax.ShapeDtypeStruct((1, hid), F32),
            jax.ShapeDtypeStruct((8, hid), F32),
        ],
        compiler_params=params("arbitrary"),
        name="down_grad",
    )(act, weighted, sums, gamma, beta)


def hidden_kernel(
    n, act, slope, gm, w_up, normed, ratio, twice, gamma, gain, xhat, rstd, up_term, grad_conv, ends, gain_part, total
):
    h = pl.program_id(0)
    a = act[...]
    grad_act = gm[...] * (gamma[...] * ratio[...] + 1.0) + a * twice[...]
    grad_hidden = (grad_act * slope[...]).astype(BF16)
    up_term[...] = lax.dot_general(
        grad_hidden, normed[...], (((0,), (0,)), ((), ())), preferred_element_type=F32
    ).astype(BF16)
    step = jnp.dot(grad_hidden, w_up[...], preferred_element_type=F32)

    @pl.when(h == 0)
    def _():
        total[...] = step

    @pl.when(h > 0)
    def _():
        total[...] += step

    @pl.when(h == n - 1)
    def _():
        pixels, width = total.shape
        block = 64

        def one(t, carry):
            at = pl.ds(pl.multiple_of(t * block, block), block)
            g = total[at, :]
            hat = xhat[at, :]
            carry = carry + jnp.sum((g * hat).reshape(block // 8, 8, width), axis=0)
            g = g * gain[...]
            mean_g = jnp.sum(g, axis=-1, keepdims=True) / width
            mean_gh = jnp.sum(g * hat, axis=-1, keepdims=True) / width
            out = rstd[at, 0:1] * (g - mean_g - hat * mean_gh)
            grad_conv[at, :] = out
            ends[at, :] = out.astype(BF16)
            return carry

        gain_part[...] = lax.fori_loop(0, pixels // block, one, jnp.zeros((8, width), F32))


def hidden_grad(act, slope, gm, w_up, normed, ratio, twice, gamma, gain, xhat, rstd, block=256):
    pixels, hid = act.shape
    width = normed.shape[1]
    n = hid // block
    whole = lambda *s: pl.BlockSpec(s, lambda h: (0,) * len(s))
    cols = pl.BlockSpec((pixels, block), lambda h: (0, h))
    vec = pl.BlockSpec((1, block), lambda h: (0, h))
    rows = pl.BlockSpec((block, width), lambda h: (h, 0))
    return pl.pallas_call(
        functools.partial(hidden_kernel, n),
        grid=(n,),
        in_specs=[
            cols, cols, cols, rows, whole(pixels, width), vec, vec, vec,
            whole(1, width), whole(pixels, width), whole(pixels, LANES),
        ],
        out_specs=[rows, whole(pixels, width), whole(pixels, width), whole(8, width)],
        out_shape=[
            jax.ShapeDtypeStruct((hid, width), BF16),
            jax.ShapeDtypeStruct((pixels, width), F32),
            jax.ShapeDtypeStruct((pixels, width), BF16),
            jax.ShapeDtypeStruct((8, width), F32),
        ],
        scratch_shapes=[pltpu.VMEM((pixels, width), F32)],
        compiler_params=params("arbitrary"),
        name="hidden_grad",
    )(act, slope, gm, w_up, normed, ratio, twice, gamma, gain.reshape(1, width), xhat, rstd)


def taps_grad_kernel(feat, above, below, grad, k_ref, ktaps, part, xs, gs, taps):
    fill_padded(xs, above, 0)
    fill_padded(xs, feat, 3)
    fill_padded(xs, below, 7)
    fill_padded(gs, grad, 0)
    spread_taps(taps, k_ref, True)
    cols = feat.shape[1]
    for start in range(0, cols, GROUP * TILE):
        acc = [[jnp.zeros((TILE, LANES), F32) for _ in range(GROUP)] for _ in range(4)]
        acc = taps_group(gs, taps, own_pairs(), start, acc)
        for o in range(4):
            for b in range(GROUP):
                part[o, start + TILE * b : start + TILE * (b + 1), :] = acc[o][b]
    for j in range(7):
        sums = [jnp.zeros((TILE, LANES), F32) for _ in range(7)]
        for start in range(0, cols, TILE):
            g = [gs[o, PAD + start : PAD + start + TILE, :] for o in range(4)]
            for r in range(10):
                x = xs[r, PAD - 3 + j + start : PAD - 3 + j + start + TILE, :]
                for o in range(4):
                    if 0 <= r - o <= 6:
                        sums[r - o] = sums[r - o] + x * g[o]
        for i in range(7):
            ktaps[i, j : j + 1, :] = jnp.sum(sums[i], axis=0, keepdims=True)


def taps_grad(feat, above, below, grad, kernel):
    rows, cols, width = feat.shape
    chunks = pl.cdiv(width, LANES)
    blk = lambda r: pl.BlockSpec((r, cols, LANES), lambda c: (0, 0, c))
    k = pl.BlockSpec((7, 7, LANES), lambda c: (0, 0, c))
    return pl.pallas_call(
        taps_grad_kernel,
        grid=(chunks,),
        in_specs=[blk(rows), blk(3), blk(3), blk(rows), k],
        out_specs=[k, blk(rows)],
        out_shape=[jax.ShapeDtypeStruct((7, 7, width), F32), jax.ShapeDtypeStruct((rows, cols, width), F32)],
        scratch_shapes=[
            pltpu.VMEM((rows + 6, cols + 2 * PAD, LANES), F32),
            pltpu.VMEM((rows, cols + 2 * PAD, LANES), F32),
            pltpu.VMEM((49, TILE, LANES), F32),
        ],
        compiler_params=params("arbitrary"),
        name="taps_grad",
    )(feat, above, below, grad, kernel)


def conv_back_kernel(part, above, below, k_ref, upstream, weight, out, xs, taps):
    fill_padded(xs, above, 0)
    fill_padded(xs, below, 3)
    spread_taps(taps, k_ref, True)
    cols = part.shape[1]
    for start in range(0, cols, GROUP * TILE):
        acc = [[None] * GROUP for _ in range(4)]
        for o in range(4):
            for b in range(GROUP):
                at = slice(start + TILE * b, start + TILE * (b + 1))
                acc[o][b] = part[o, at, :] + upstream[o, at, :].astype(F32) * weight[o, at, :]
        acc = taps_group(xs, taps, halo_pairs(), start, acc)
        for o in range(4):
            for b in range(GROUP):
                out[o, start + TILE * b : start + TILE * (b + 1), :] = acc[o][b]


def conv_back(part, above, below, kernel, upstream, weight):
    rows, cols, width = part.shape
    chunks = pl.cdiv(width, LANES)
    blk = lambda r: pl.BlockSpec((r, cols, LANES), lambda c: (0, 0, c))
    k = pl.BlockSpec((7, 7, LANES), lambda c: (0, 0, c))
    return pl.pallas_call(
        conv_back_kernel,
        grid=(chunks,),
        in_specs=[blk(rows), blk(3), blk(3), k, blk(rows), pl.BlockSpec((rows, cols, LANES), lambda c: (0, 0, 0))],
        out_specs=blk(rows),
        out_shape=jax.ShapeDtypeStruct((rows, cols, width), F32),
        scratch_shapes=[
            pltpu.VMEM((6, cols + 2 * PAD, LANES), F32),
            pltpu.VMEM((49, TILE, LANES), F32),
        ],
        compiler_params=params("arbitrary"),
        name="conv_back",
    )(part, above, below, kernel, upstream, weight)


def body(
    features, kernel, norm_gain, w_up, grn_gamma, grn_beta, w_down, upstream, labels, class_weight
):
    crops, rows, cols, width = features.shape
    feat, up = features[0], upstream[0]
    space = lax.axis_size("space")
    dp = lax.axis_size("dp")
    hid = w_up.shape[0] * dp
    pixels = rows * cols
    rising = [(i, i + 1) for i in range(space - 1)]
    falling = [(j, i) for i, j in rising]
    above = lax.ppermute(feat[rows - 3 :], "space", rising)
    below = lax.ppermute(feat[:3], "space", falling)
    w_up_all = lax.all_gather(w_up, "dp", axis=0, tiled=True)
    w_down_all = lax.all_gather(w_down, "dp", axis=0, tiled=True)

    classes = jnp.arange(class_weight.shape[0], dtype=jnp.int32)
    pixel_weight = jnp.sum(jnp.where(labels[0][..., None] == classes, class_weight, 0.0), axis=-1)
    weight = jnp.broadcast_to(pixel_weight[..., None], (rows, cols, LANES))
    weighted = (up.astype(F32) * pixel_weight[..., None]).astype(BF16).reshape(pixels, width)

    part = conv_own(feat, kernel, False)
    normed, xhat, rstd = conv_norm(part, above, below, kernel, norm_gain)
    act, slope, gm, local = up_project(normed, weighted, w_up_all, w_down_all)
    sums = lax.psum(local[:3], "space")
    sums = jnp.concatenate([sums, jnp.zeros((5, hid), F32)], axis=0)
    gamma, beta = grn_gamma.reshape(1, hid), grn_beta.reshape(1, hid)
    down_term, ratio, twice, parts = down_grad(act, weighted, sums, gamma, beta)
    up_term, grad_conv, grad_ends, gain_part = hidden_grad(
        act, slope, gm, w_up_all, normed, ratio, twice, gamma, norm_gain, xhat, rstd
    )
    grad_conv = grad_conv.reshape(rows, cols, width)
    ends = grad_ends.reshape(rows, cols, width)
    g_above = lax.ppermute(ends[rows - 3 :], "space", rising)
    g_below = lax.ppermute(ends[:3], "space", falling)
    kernel_part, back = taps_grad(feat, above, below, grad_conv, kernel)
    grad_features = conv_back(back, g_above, g_below, kernel, up, weight)

    scale = 1.0 / math.sqrt(dp * space * pixels)
    partial_rows = lax.psum_scatter(
        jnp.concatenate([up_term, down_term], axis=1), "dp", scatter_dimension=0, tiled=True
    )
    summed = lax.psum(partial_rows.astype(F32), "space")
    kernel_sum, gain_sum = lax.psum((kernel_part, jnp.sum(gain_part, axis=0)), ("dp", "space"))
    gamma_sum, beta_sum = lax.psum((parts[0], parts[1]), "dp")
    return (
        grad_features[None],
        scale * kernel_sum,
        scale * gain_sum,
        scale * summed[:, :width],
        scale * gamma_sum,
        scale * beta_sum,
        scale * summed[:, width:],
    )


def solution(mesh):
    return jax.shard_map(
        body,
        mesh=mesh,
        in_specs=(
            P("dp", "space", None, None),
            P(),
            P(),
            P("dp", None),
            P(),
            P(),
            P("dp", None),
            P("dp", "space", None, None),
            P("dp", "space", None),
            P(),
        ),
        out_specs=(P("dp", "space", None, None), P(), P(), P("dp", None), P(), P(), P("dp", None)),
        check_vma=False,
    )
```

```python
import functools
import math

import jax
import jax.numpy as jnp
from jax import lax
from jax.experimental import pallas as pl
from jax.experimental.pallas import tpu as pltpu
from jax.sharding import PartitionSpec as P

EPS_NORM = 1e-06
F32 = jnp.float32
BF16 = jnp.bfloat16
VMEM_LIMIT = 56 * 1024 * 1024
LANES = 128
PAD = 8
TILE = 8
GROUP = 4


def params(*semantics):
    return pltpu.CompilerParams(dimension_semantics=semantics, vmem_limit_bytes=VMEM_LIMIT)


def fill_padded(dst, src, first):
    rows, cols, lanes = src.shape
    zeros = jnp.zeros((rows, PAD, lanes), F32)
    dst[first : first + rows, 0:PAD, :] = zeros
    dst[first : first + rows, PAD + cols : PAD + cols + PAD, :] = zeros
    dst[first : first + rows, PAD : PAD + cols, :] = src[...].astype(F32)


def spread_taps(dst, k_ref, flip):
    for i in range(7):
        for j in range(7):
            tap = k_ref[6 - i, 6 - j : 7 - j, :] if flip else k_ref[i, j : j + 1, :]
            dst[i * 7 + j] = jnp.broadcast_to(tap, (TILE, LANES))


def taps_group(src, taps, pairs, start, acc):
    rows = sorted({r for r, _, _ in pairs})
    for j in range(7):
        for r in rows:
            todo = [(o, i) for rr, o, i in pairs if rr == r]
            xs = [src[r, start + TILE * b + PAD - 3 + j : start + TILE * b + PAD - 3 + j + TILE, :] for b in range(GROUP)]
            for o, i in todo:
                tap = taps[i * 7 + j]
                for b in range(GROUP):
                    acc[o][b] = acc[o][b] + xs[b] * tap
    return acc


def own_pairs():
    return [(s, o, s - o + 3) for s in range(4) for o in range(4)]


def halo_pairs():
    above = [(s, o, s - o) for s in range(3) for o in range(4) if 0 <= s - o <= 6]
    below = [(3 + s, o, s + 7 - o) for s in range(3) for o in range(4) if 0 <= s + 7 - o <= 6]
    return above + below


def conv_own_kernel(flip, feat, k_ref, out, xs, taps):
    fill_padded(xs, feat, 0)
    spread_taps(taps, k_ref, flip)
    cols = feat.shape[1]
    for start in range(0, cols, GROUP * TILE):
        acc = [[jnp.zeros((TILE, LANES), F32) for _ in range(GROUP)] for _ in range(4)]
        acc = taps_group(xs, taps, own_pairs(), start, acc)
        for o in range(4):
            for b in range(GROUP):
                out[o, start + TILE * b : start + TILE * (b + 1), :] = acc[o][b]


def conv_own(feat, kernel, flip):
    rows, cols, width = feat.shape
    chunks = pl.cdiv(width, LANES)
    return pl.pallas_call(
        functools.partial(conv_own_kernel, flip),
        grid=(chunks,),
        in_specs=[
            pl.BlockSpec((rows, cols, LANES), lambda c: (0, 0, c)),
            pl.BlockSpec((7, 7, LANES), lambda c: (0, 0, c)),
        ],
        out_specs=pl.BlockSpec((rows, cols, LANES), lambda c: (0, 0, c)),
        out_shape=jax.ShapeDtypeStruct((rows, cols, width), F32),
        scratch_shapes=[
            pltpu.VMEM((rows, cols + 2 * PAD, LANES), F32),
            pltpu.VMEM((49, TILE, LANES), F32),
        ],
        compiler_params=params("arbitrary"),
        name="conv_own",
    )(feat, kernel)


def conv_norm_kernel(width, chunks, part, above, below, k_ref, gain, normed, xhat, rstd, xs, taps, conv):
    c = pl.program_id(0)
    fill_padded(xs, above, 0)
    fill_padded(xs, below, 3)
    spread_taps(taps, k_ref, False)
    cols = part.shape[1]
    for start in range(0, cols, GROUP * TILE):
        acc = [
            [part[o, start + TILE * b : start + TILE * (b + 1), :] for b in range(GROUP)] for o in range(4)
        ]
        acc = taps_group(xs, taps, halo_pairs(), start, acc)
        for o in range(4):
            for b in range(GROUP):
                conv[c, o * cols + start + TILE * b : o * cols + start + TILE * (b + 1), :] = acc[o][b]

    @pl.when(c == chunks - 1)
    def _():
        last = width - (chunks - 1) * LANES
        block = 64

        def one(t, carry):
            at = pl.multiple_of(t * block, block)
            parts = [conv[n, pl.ds(at, block), :] for n in range(chunks)]
            lane = lax.broadcasted_iota(jnp.int32, (block, LANES), 1)
            inside = lane < last
            parts[-1] = jnp.where(inside, parts[-1], 0.0)
            mean = jnp.sum(sum(parts[1:], parts[0]), axis=-1, keepdims=True) / width
            centred = [p - mean for p in parts]
            centred[-1] = jnp.where(inside, centred[-1], 0.0)
            squares = [p * p for p in centred]
            var = jnp.sum(sum(squares[1:], squares[0]), axis=-1, keepdims=True) / width
            scale = lax.rsqrt(var + EPS_NORM)
            rstd[pl.ds(at, block), :] = jnp.broadcast_to(scale, (block, LANES))
            for n in range(chunks):
                w = min(LANES, width - n * LANES)
                hat = centred[n] * scale
                g = gain[:, n * LANES : n * LANES + w]
                xhat[pl.ds(at, block), n * LANES : n * LANES + w] = hat[:, :w]
                normed[pl.ds(at, block), n * LANES : n * LANES + w] = (hat[:, :w] * g).astype(BF16)
            return carry

        lax.fori_loop(0, (4 * cols) // block, one, 0)


def conv_norm(part, above, below, kernel, gain):
    rows, cols, width = part.shape
    chunks = pl.cdiv(width, LANES)
    pixels = rows * cols
    whole = lambda *s: pl.BlockSpec(s, lambda c: (0,) * len(s))
    return pl.pallas_call(
        functools.partial(conv_norm_kernel, width, chunks),
        grid=(chunks,),
        in_specs=[
            pl.BlockSpec((rows, cols, LANES), lambda c: (0, 0, c)),
            pl.BlockSpec((3, cols, LANES), lambda c: (0, 0, c)),
            pl.BlockSpec((3, cols, LANES), lambda c: (0, 0, c)),
            pl.BlockSpec((7, 7, LANES), lambda c: (0, 0, c)),
            whole(1, width),
        ],
        out_specs=[whole(pixels, width), whole(pixels, width), whole(pixels, LANES)],
        out_shape=[
            jax.ShapeDtypeStruct((pixels, width), BF16),
            jax.ShapeDtypeStruct((pixels, width), F32),
            jax.ShapeDtypeStruct((pixels, LANES), F32),
        ],
        scratch_shapes=[
            pltpu.VMEM((6, cols + 2 * PAD, LANES), F32),
            pltpu.VMEM((49, TILE, LANES), F32),
            pltpu.VMEM((chunks, pixels, LANES), F32),
        ],
        compiler_params=params("arbitrary"),
        name="conv_norm",
    )(part, above, below, kernel, gain.reshape(1, width))


def up_kernel(normed, w_up, act_ref, slope_ref, sums):
    nt = (((1,), (1,)), ((), ()))
    hidden = lax.dot_general(normed[...], w_up[...], nt, preferred_element_type=F32)
    cdf = 0.5 * (1.0 + lax.erf(hidden * (2.0**-0.5)))
    act = hidden * cdf
    slope = cdf + hidden * (jnp.exp(hidden * hidden * -0.5) * (1.0 / math.sqrt(2.0 * math.pi)))
    act_ref[...] = act
    slope_ref[...] = slope
    sums[...] = jnp.sum((act * act).reshape(-1, 8, act.shape[1]), axis=0)


def up_project(normed, w_up, block=256):
    pixels, width = normed.shape
    hid = w_up.shape[0]
    whole = pl.BlockSpec((pixels, width), lambda h: (0, 0))
    rows = pl.BlockSpec((block, width), lambda h: (h, 0))
    cols = pl.BlockSpec((pixels, block), lambda h: (0, h))
    big = jax.ShapeDtypeStruct((pixels, hid), F32)
    return pl.pallas_call(
        up_kernel,
        grid=(hid // block,),
        in_specs=[whole, rows],
        out_specs=[cols, cols, pl.BlockSpec((8, block), lambda h: (0, h))],
        out_shape=[big, big, jax.ShapeDtypeStruct((8, hid), F32)],
        compiler_params=params("arbitrary"),
        name="up_project",
    )(normed, w_up)


def mixed_kernel(weighted, w_down, act_ref, sq, gm_ref, sums):
    nt = (((1,), (1,)), ((), ()))
    gm = lax.dot_general(weighted[...], w_down[...], nt, preferred_element_type=F32)
    gm_ref[...] = gm
    act = act_ref[...]
    sums[0:1, :] = jnp.sum(sq[...], axis=0, keepdims=True)
    sums[1:2, :] = jnp.sum(gm * act, axis=0, keepdims=True)
    sums[2:3, :] = jnp.sum(gm, axis=0, keepdims=True)
    sums[3:4, :] = jnp.zeros((1, sums.shape[1]), F32)


def mixed_grad(weighted, w_down, act, sq, block=256):
    pixels, width = weighted.shape
    hid = w_down.shape[0]
    whole = pl.BlockSpec((pixels, width), lambda h: (0, 0))
    rows = pl.BlockSpec((block, width), lambda h: (h, 0))
    cols = pl.BlockSpec((pixels, block), lambda h: (0, h))
    return pl.pallas_call(
        mixed_kernel,
        grid=(hid // block,),
        in_specs=[whole, rows, cols, pl.BlockSpec((8, block), lambda h: (0, h))],
        out_specs=[cols, pl.BlockSpec((4, block), lambda h: (0, h))],
        out_shape=[jax.ShapeDtypeStruct((pixels, hid), F32), jax.ShapeDtypeStruct((4, hid), F32)],
        compiler_params=params("arbitrary"),
        name="mixed_grad",
    )(weighted, w_down, act, sq)


def ratio_of(sums, gamma):
    energy = jnp.sqrt(sums[0:1, :])
    hid = energy.shape[1]
    mean = jnp.sum(energy, axis=1, keepdims=True) / hid + EPS_NORM
    ratio = energy / mean
    grad_ratio = gamma * sums[1:2, :]
    shared = jnp.sum(grad_ratio * energy, axis=1, keepdims=True) / (mean * mean) / hid
    grad_energy = grad_ratio / mean - shared
    return ratio, grad_energy / energy


def down_kernel(act, weighted, sums, local, gamma, beta, down_term, ratio, twice, parts):
    h = pl.program_id(0)
    block = act.shape[1]

    @pl.when(h == 0)
    def _():
        r, t = ratio_of(jnp.sum(sums[...], axis=0), gamma[...])
        ratio[...] = r
        twice[...] = t
        parts[0:1, :] = local[1:2, :] * r
        parts[1:2, :] = local[2:3, :]

    here = pl.ds(pl.multiple_of(h * block, block), block)
    a = act[...]
    mixed = (gamma[:, here] * a * ratio[:, here] + beta[:, here] + a).astype(BF16)
    down_term[...] = lax.dot_general(
        mixed, weighted[...], (((0,), (0,)), ((), ())), preferred_element_type=F32
    ).astype(BF16)


def down_grad(act, weighted, sums, local, gamma, beta, block=256):
    pixels, hid = act.shape
    width = weighted.shape[1]
    whole = lambda *s: pl.BlockSpec(s, lambda h: (0,) * len(s))
    return pl.pallas_call(
        down_kernel,
        grid=(hid // block,),
        in_specs=[
            pl.BlockSpec((pixels, block), lambda h: (0, h)),
            whole(pixels, width),
            whole(*sums.shape),
            whole(4, hid),
            whole(1, hid),
            whole(1, hid),
        ],
        out_specs=[
            pl.BlockSpec((block, width), lambda h: (h, 0)),
            whole(1, hid),
            whole(1, hid),
            whole(2, hid),
        ],
        out_shape=[
            jax.ShapeDtypeStruct((hid, width), BF16),
            jax.ShapeDtypeStruct((1, hid), F32),
            jax.ShapeDtypeStruct((1, hid), F32),
            jax.ShapeDtypeStruct((2, hid), F32),
        ],
        compiler_params=params("arbitrary"),
        name="down_grad",
    )(act, weighted, sums, local, gamma, beta)


def hidden_kernel(
    n, act, slope, gm, w_up, normed, ratio, twice, gamma, gain, xhat, rstd, up_term, grad_conv, ends, gain_part, total
):
    h = pl.program_id(0)
    a = act[...]
    grad_act = gm[...] * (gamma[...] * ratio[...] + 1.0) + a * twice[...]
    grad_hidden = (grad_act * slope[...]).astype(BF16)
    up_term[...] = lax.dot_general(
        grad_hidden, normed[...], (((0,), (0,)), ((), ())), preferred_element_type=F32
    ).astype(BF16)
    step = jnp.dot(grad_hidden, w_up[...], preferred_element_type=F32)

    @pl.when(h == 0)
    def _():
        total[...] = step

    @pl.when(h > 0)
    def _():
        total[...] += step

    @pl.when(h == n - 1)
    def _():
        pixels, width = total.shape
        block = 64

        def one(t, carry):
            at = pl.ds(pl.multiple_of(t * block, block), block)
            g = total[at, :]
            hat = xhat[at, :]
            carry = carry + jnp.sum((g * hat).reshape(block // 8, 8, width), axis=0)
            g = g * gain[...]
            mean_g = jnp.sum(g, axis=-1, keepdims=True) / width
            mean_gh = jnp.sum(g * hat, axis=-1, keepdims=True) / width
            out = rstd[at, 0:1] * (g - mean_g - hat * mean_gh)
            grad_conv[at, :] = out
            ends[at, :] = out.astype(BF16)
            return carry

        gain_part[...] = lax.fori_loop(0, pixels // block, one, jnp.zeros((8, width), F32))


def hidden_grad(act, slope, gm, w_up, normed, ratio, twice, gamma, gain, xhat, rstd, block=256):
    pixels, hid = act.shape
    width = normed.shape[1]
    n = hid // block
    whole = lambda *s: pl.BlockSpec(s, lambda h: (0,) * len(s))
    cols = pl.BlockSpec((pixels, block), lambda h: (0, h))
    vec = pl.BlockSpec((1, block), lambda h: (0, h))
    rows = pl.BlockSpec((block, width), lambda h: (h, 0))
    return pl.pallas_call(
        functools.partial(hidden_kernel, n),
        grid=(n,),
        in_specs=[
            cols, cols, cols, rows, whole(pixels, width), vec, vec, vec,
            whole(1, width), whole(pixels, width), whole(pixels, LANES),
        ],
        out_specs=[rows, whole(pixels, width), whole(pixels, width), whole(8, width)],
        out_shape=[
            jax.ShapeDtypeStruct((hid, width), BF16),
            jax.ShapeDtypeStruct((pixels, width), F32),
            jax.ShapeDtypeStruct((pixels, width), BF16),
            jax.ShapeDtypeStruct((8, width), F32),
        ],
        scratch_shapes=[pltpu.VMEM((pixels, width), F32)],
        compiler_params=params("arbitrary"),
        name="hidden_grad",
    )(act, slope, gm, w_up, normed, ratio, twice, gamma, gain.reshape(1, width), xhat, rstd)


def taps_grad_kernel(feat, above, below, grad, k_ref, ktaps, part, xs, gs, taps):
    fill_padded(xs, above, 0)
    fill_padded(xs, feat, 3)
    fill_padded(xs, below, 7)
    fill_padded(gs, grad, 0)
    spread_taps(taps, k_ref, True)
    cols = feat.shape[1]
    for start in range(0, cols, GROUP * TILE):
        acc = [[jnp.zeros((TILE, LANES), F32) for _ in range(GROUP)] for _ in range(4)]
        acc = taps_group(gs, taps, own_pairs(), start, acc)
        for o in range(4):
            for b in range(GROUP):
                part[o, start + TILE * b : start + TILE * (b + 1), :] = acc[o][b]
    for j in range(7):
        sums = [jnp.zeros((TILE, LANES), F32) for _ in range(7)]
        for start in range(0, cols, TILE):
            g = [gs[o, PAD + start : PAD + start + TILE, :] for o in range(4)]
            for r in range(10):
                x = xs[r, PAD - 3 + j + start : PAD - 3 + j + start + TILE, :]
                for o in range(4):
                    if 0 <= r - o <= 6:
                        sums[r - o] = sums[r - o] + x * g[o]
        for i in range(7):
            ktaps[i, j : j + 1, :] = jnp.sum(sums[i], axis=0, keepdims=True)


def taps_grad(feat, above, below, grad, kernel):
    rows, cols, width = feat.shape
    chunks = pl.cdiv(width, LANES)
    blk = lambda r: pl.BlockSpec((r, cols, LANES), lambda c: (0, 0, c))
    k = pl.BlockSpec((7, 7, LANES), lambda c: (0, 0, c))
    return pl.pallas_call(
        taps_grad_kernel,
        grid=(chunks,),
        in_specs=[blk(rows), blk(3), blk(3), blk(rows), k],
        out_specs=[k, blk(rows)],
        out_shape=[jax.ShapeDtypeStruct((7, 7, width), F32), jax.ShapeDtypeStruct((rows, cols, width), F32)],
        scratch_shapes=[
            pltpu.VMEM((rows + 6, cols + 2 * PAD, LANES), F32),
            pltpu.VMEM((rows, cols + 2 * PAD, LANES), F32),
            pltpu.VMEM((49, TILE, LANES), F32),
        ],
        compiler_params=params("arbitrary"),
        name="taps_grad",
    )(feat, above, below, grad, kernel)


def conv_back_kernel(part, above, below, k_ref, upstream, weight, out, xs, taps):
    fill_padded(xs, above, 0)
    fill_padded(xs, below, 3)
    spread_taps(taps, k_ref, True)
    cols = part.shape[1]
    for start in range(0, cols, GROUP * TILE):
        acc = [[None] * GROUP for _ in range(4)]
        for o in range(4):
            for b in range(GROUP):
                at = slice(start + TILE * b, start + TILE * (b + 1))
                acc[o][b] = part[o, at, :] + upstream[o, at, :].astype(F32) * weight[o, at, :]
        acc = taps_group(xs, taps, halo_pairs(), start, acc)
        for o in range(4):
            for b in range(GROUP):
                out[o, start + TILE * b : start + TILE * (b + 1), :] = acc[o][b]


def conv_back(part, above, below, kernel, upstream, weight):
    rows, cols, width = part.shape
    chunks = pl.cdiv(width, LANES)
    blk = lambda r: pl.BlockSpec((r, cols, LANES), lambda c: (0, 0, c))
    k = pl.BlockSpec((7, 7, LANES), lambda c: (0, 0, c))
    return pl.pallas_call(
        conv_back_kernel,
        grid=(chunks,),
        in_specs=[blk(rows), blk(3), blk(3), k, blk(rows), pl.BlockSpec((rows, cols, LANES), lambda c: (0, 0, 0))],
        out_specs=blk(rows),
        out_shape=jax.ShapeDtypeStruct((rows, cols, width), F32),
        scratch_shapes=[
            pltpu.VMEM((6, cols + 2 * PAD, LANES), F32),
            pltpu.VMEM((49, TILE, LANES), F32),
        ],
        compiler_params=params("arbitrary"),
        name="conv_back",
    )(part, above, below, kernel, upstream, weight)


BOTH = ("dp", "space")
STEPS = ((1, 0), (3, 0), (0, 1), (2, 0), (1, 1), (3, 1), (2, 1))


def pairs_of(move):
    pairs = []
    for d in range(16):
        for s in range(8):
            y, z, c, x, low = move(d // 8, d // 2 % 4, d % 2, s // 2, s % 2)
            pairs.append((d * 8 + s, (y * 8 + z * 2 + c) * 8 + x * 2 + low))
    return pairs


def to_other_core(value):
    return lax.ppermute(value, BOTH, pairs_of(lambda y, z, c, x, low: (y, z, 1 - c, x, low)))


def by_step(value, dz, dy):
    return lax.ppermute(
        value, BOTH, pairs_of(lambda y, z, c, x, low: ((y + dy) % 2, (z + dz) % 4, c, x, (low + dy) % 2))
    )


def gather_rows(shard):
    mine = jnp.concatenate([shard] + [by_step(shard, dz, dy) for dz, dy in STEPS], axis=0)
    return jnp.concatenate([mine, to_other_core(mine)], axis=0)


def block_order():
    dp = lax.axis_index("dp")
    y, z, c = dp // 8, dp // 2 % 4, dp % 2
    owners = [
        ((y + dy) % 2) * 8 + ((z - dz) % 4) * 2 + core for core in (c, 1 - c) for dz, dy in ((0, 0),) + STEPS
    ]
    return jnp.stack(owners)


def reduce_rows(term):
    half = term.shape[0] // 2
    other = to_other_core(term[half:])
    chip = (term[:half].astype(F32) + other.astype(F32)).astype(BF16)
    rows = half // 8
    total = chip[:rows].astype(F32)
    for n, (dz, dy) in enumerate(STEPS, 1):
        total = total + by_step(chip[n * rows : (n + 1) * rows], -dz, dy).astype(F32)
    return total


def exchange(value, axis):
    return lax.all_to_all(value, axis, 0, 0)


def everyone(value, axis):
    return exchange(jnp.broadcast_to(value, (lax.axis_size(axis),) + value.shape), axis)


def body(
    features, kernel, norm_gain, w_up, grn_gamma, grn_beta, w_down, upstream, labels, class_weight
):
    crops, rows, cols, width = features.shape
    feat, up = features[0], upstream[0]
    space = lax.axis_size("space")
    dp = lax.axis_size("dp")
    owned = w_up.shape[0]
    hid = owned * dp
    pixels = rows * cols
    rising = [(i, i + 1) for i in range(space - 1)]
    falling = [(j, i) for i, j in rising]
    above = lax.ppermute(feat[rows - 3 :], "space", rising)
    below = lax.ppermute(feat[:3], "space", falling)
    w_up_all = gather_rows(w_up)
    w_down_all = gather_rows(w_down)
    order = block_order()
    gamma = jnp.take(grn_gamma.reshape(dp, owned), order, axis=0).reshape(1, hid)
    beta = jnp.take(grn_beta.reshape(dp, owned), order, axis=0).reshape(1, hid)

    classes = jnp.arange(class_weight.shape[0], dtype=jnp.int32)
    pixel_weight = jnp.sum(jnp.where(labels[0][..., None] == classes, class_weight, 0.0), axis=-1)
    weight = jnp.broadcast_to(pixel_weight[..., None], (rows, cols, LANES))
    weighted = (up.astype(F32) * pixel_weight[..., None]).astype(BF16).reshape(pixels, width)

    part = conv_own(feat, kernel, False)
    normed, xhat, rstd = conv_norm(part, above, below, kernel, norm_gain)
    act, slope, sq = up_project(normed, w_up_all)
    gm, local = mixed_grad(weighted, w_down_all, act, sq)
    sums = everyone(local, "space")
    down_term, ratio, twice, parts = down_grad(act, weighted, sums, local, gamma, beta)
    up_term, grad_conv, grad_ends, gain_part = hidden_grad(
        act, slope, gm, w_up_all, normed, ratio, twice, gamma, norm_gain, xhat, rstd
    )
    grad_conv = grad_conv.reshape(rows, cols, width)
    ends = grad_ends.reshape(rows, cols, width)
    g_above = lax.ppermute(ends[rows - 3 :], "space", rising)
    g_below = lax.ppermute(ends[:3], "space", falling)
    kernel_part, back = taps_grad(feat, above, below, grad_conv, kernel)
    grad_features = conv_back(back, g_above, g_below, kernel, up, weight)

    scale = 1.0 / math.sqrt(dp * space * pixels)
    down_rows = reduce_rows(down_term)
    up_rows = reduce_rows(up_term)

    places = jnp.arange(dp)
    place = jnp.sum(jnp.where(order[None, :] == places[:, None], places[None, :], 0), axis=1)
    spread = jnp.take(parts.reshape(2, dp, owned), place, axis=1)
    vector = jnp.concatenate(
        [kernel_part.reshape(49, width), jnp.sum(gain_part, axis=0, keepdims=True), spread.reshape(-1, width)], axis=0
    )
    lines = vector.shape[0]
    vector = jnp.pad(vector, ((0, -lines % (8 * space)), (0, 0)))
    piece = jnp.sum(exchange(vector.reshape(space, -1, width), "space"), axis=0)
    piece = jnp.sum(everyone(piece, "dp"), axis=0)
    vector = scale * everyone(piece, "space").reshape(-1, width)
    kernel_sum = vector[:49].reshape(7, 7, width)
    gain_sum = vector[49]
    gamma_sum, beta_sum = vector[50:lines].reshape(2, hid)

    block = jnp.concatenate([up_rows, down_rows], axis=1)
    block = block.reshape(space, owned // space, 2 * width).astype(BF16)
    block = scale * jnp.sum(exchange(block, "space").astype(F32), axis=0)
    block = everyone(block.astype(BF16), "space").astype(F32).reshape(owned, 2 * width)
    return (
        grad_features[None],
        kernel_sum,
        gain_sum,
        block[:, :width],
        gamma_sum,
        beta_sum,
        block[:, width:],
    )


def solution(mesh):
    return jax.shard_map(
        body,
        mesh=mesh,
        in_specs=(
            P("dp", "space", None, None),
            P(),
            P(),
            P("dp", None),
            P(),
            P(),
            P("dp", None),
            P("dp", "space", None, None),
            P("dp", "space", None),
            P(),
        ),
        out_specs=(P("dp", "space", None, None), P(), P(), P("dp", None), P(), P(), P("dp", None)),
        check_vma=False,
    )
```

```python
import functools
import math

import jax
import jax.numpy as jnp
from jax import lax
from jax.experimental import pallas as pl
from jax.experimental.pallas import tpu as pltpu
from jax.sharding import PartitionSpec as P

EPS_NORM = 1e-06
F32 = jnp.float32
BF16 = jnp.bfloat16
VMEM_LIMIT = 56 * 1024 * 1024
LANES = 128
PAD = 8
TILE = 8
GROUP = 4
CHUNKS = 3


def params(*semantics):
    return pltpu.CompilerParams(dimension_semantics=semantics, vmem_limit_bytes=VMEM_LIMIT)


def cost(micros):
    return pl.CostEstimate(flops=int(micros * 0.4e9), transcendentals=0, bytes_accessed=0)


def fill_padded(dst, src, first, lanes):
    rows, cols, _ = src.shape
    zeros = jnp.zeros((rows, PAD, LANES), F32)
    dst[first : first + rows, 0:PAD, :] = zeros
    dst[first : first + rows, PAD + cols : PAD + cols + PAD, :] = zeros
    dst[first : first + rows, PAD : PAD + cols, :] = src[:, :, lanes].astype(F32)


def spread_taps(dst, k_ref, flip, lanes):
    for i in range(7):
        for j in range(7):
            tap = k_ref[6 - i, 6 - j : 7 - j, lanes] if flip else k_ref[i, j : j + 1, lanes]
            dst[i * 7 + j] = jnp.broadcast_to(tap, (TILE, LANES))


def taps_group(src, taps, pairs, start, acc):
    rows = sorted({r for r, _, _ in pairs})
    for j in range(7):
        for r in rows:
            todo = [(o, i) for rr, o, i in pairs if rr == r]
            at = [start + TILE * b + PAD - 3 + j for b in range(GROUP)]
            xs = [src[r, p : p + TILE, :] for p in at]
            for o, i in todo:
                tap = taps[i * 7 + j]
                for b in range(GROUP):
                    acc[o][b] = acc[o][b] + xs[b] * tap
    return acc


def own_pairs():
    return [(s, o, s - o + 3) for s in range(4) for o in range(4)]


def halo_pairs():
    above = [(s, o, s - o) for s in range(3) for o in range(4) if 0 <= s - o <= 6]
    below = [(3 + s, o, s + 7 - o) for s in range(3) for o in range(4) if 0 <= s + 7 - o <= 6]
    return above + below


def each_chunk(body):
    def one(n, carry):
        body(n, pl.ds(pl.multiple_of(n * LANES, LANES), LANES))
        return carry

    lax.fori_loop(0, CHUNKS, one, 0)


def tile_rows(start, b):
    return slice(start + TILE * b, start + TILE * (b + 1))


def conv_own_kernel(feat, k_ref, out, xs, taps):
    cols = feat.shape[1]

    def chunk(n, lanes):
        fill_padded(xs, feat, 0, lanes)
        spread_taps(taps, k_ref, False, lanes)
        for start in range(0, cols, GROUP * TILE):
            acc = [[jnp.zeros((TILE, LANES), F32) for _ in range(GROUP)] for _ in range(4)]
            acc = taps_group(xs, taps, own_pairs(), start, acc)
            for o in range(4):
                for b in range(GROUP):
                    out[o, tile_rows(start, b), lanes] = acc[o][b]

    each_chunk(chunk)


def lane_blocks(rows, cols):
    return pl.BlockSpec((rows, cols, CHUNKS * LANES), lambda c: (0, 0, c))


def whole_block(*shape):
    return pl.BlockSpec(shape, lambda c: (0,) * len(shape))


def conv_own(feat, kernel):
    rows, cols, width = feat.shape
    return pl.pallas_call(
        conv_own_kernel,
        grid=(pl.cdiv(width, CHUNKS * LANES),),
        in_specs=[lane_blocks(rows, cols), lane_blocks(7, 7)],
        out_specs=lane_blocks(rows, cols),
        out_shape=jax.ShapeDtypeStruct((rows, cols, width), F32),
        scratch_shapes=[
            pltpu.VMEM((rows, cols + 2 * PAD, LANES), F32),
            pltpu.VMEM((49, TILE, LANES), F32),
        ],
        compiler_params=params("arbitrary"),
        cost_estimate=cost(5),
        name="conv_own",
    )(feat, kernel)


def conv_norm_kernel(width, steps, part, above, below, k_ref, gain, normed, xhat, rstd, xs, taps, conv):
    c = pl.program_id(0)
    cols = part.shape[1]

    def chunk(n, lanes):
        fill_padded(xs, above, 0, lanes)
        fill_padded(xs, below, 3, lanes)
        spread_taps(taps, k_ref, False, lanes)
        for start in range(0, cols, GROUP * TILE):
            acc = [[part[o, tile_rows(start, b), lanes] for b in range(GROUP)] for o in range(4)]
            acc = taps_group(xs, taps, halo_pairs(), start, acc)
            for o in range(4):
                for b in range(GROUP):
                    conv[c * CHUNKS + n, tile_rows(o * cols + start, b), :] = acc[o][b]

    each_chunk(chunk)

    @pl.when(c == steps - 1)
    def _():
        chunks = pl.cdiv(width, LANES)
        last = width - (chunks - 1) * LANES
        block = 64

        def one(t, carry):
            at = pl.multiple_of(t * block, block)
            parts = [conv[n, pl.ds(at, block), :] for n in range(chunks)]
            lane = lax.broadcasted_iota(jnp.int32, (block, LANES), 1)
            inside = lane < last
            parts[-1] = jnp.where(inside, parts[-1], 0.0)
            mean = jnp.sum(sum(parts[1:], parts[0]), axis=-1, keepdims=True) / width
            centred = [p - mean for p in parts]
            centred[-1] = jnp.where(inside, centred[-1], 0.0)
            squares = [p * p for p in centred]
            var = jnp.sum(sum(squares[1:], squares[0]), axis=-1, keepdims=True) / width
            scale = lax.rsqrt(var + EPS_NORM)
            rstd[pl.ds(at, block), :] = jnp.broadcast_to(scale, (block, LANES))
            for n in range(chunks):
                w = min(LANES, width - n * LANES)
                hat = centred[n] * scale
                g = gain[:, n * LANES : n * LANES + w]
                xhat[pl.ds(at, block), n * LANES : n * LANES + w] = hat[:, :w]
                normed[pl.ds(at, block), n * LANES : n * LANES + w] = (hat[:, :w] * g).astype(BF16)
            return carry

        lax.fori_loop(0, (4 * cols) // block, one, 0)


def conv_norm(part, above, below, kernel, gain):
    rows, cols, width = part.shape
    steps = pl.cdiv(width, CHUNKS * LANES)
    pixels = rows * cols
    return pl.pallas_call(
        functools.partial(conv_norm_kernel, width, steps),
        grid=(steps,),
        in_specs=[
            lane_blocks(rows, cols),
            lane_blocks(3, cols),
            lane_blocks(3, cols),
            lane_blocks(7, 7),
            whole_block(1, width),
        ],
        out_specs=[whole_block(pixels, width), whole_block(pixels, width), whole_block(pixels, LANES)],
        out_shape=[
            jax.ShapeDtypeStruct((pixels, width), BF16),
            jax.ShapeDtypeStruct((pixels, width), F32),
            jax.ShapeDtypeStruct((pixels, LANES), F32),
        ],
        scratch_shapes=[
            pltpu.VMEM((6, cols + 2 * PAD, LANES), F32),
            pltpu.VMEM((49, TILE, LANES), F32),
            pltpu.VMEM((steps * CHUNKS, pixels, LANES), F32),
        ],
        compiler_params=params("arbitrary"),
        cost_estimate=cost(7),
        name="conv_norm",
    )(part, above, below, kernel, gain.reshape(1, width))


def with_rows(h, mine, other, step):
    pl.when(h < 2)(lambda: step(mine))
    pl.when(h >= 2)(lambda: step(other))


def half_rows(block, width):
    mine = pl.BlockSpec((block, width), lambda h: (jnp.minimum(h, 1), 0))
    other = pl.BlockSpec((block, width), lambda h: (jnp.maximum(h - 2, 0), 0))
    return mine, other


def up_kernel(normed, w_mine, w_other, act_ref, slope_ref, sums):
    def step(w):
        nt = (((1,), (1,)), ((), ()))
        hidden = lax.dot_general(normed[...], w[...], nt, preferred_element_type=F32)
        cdf = 0.5 * (1.0 + lax.erf(hidden * (2.0**-0.5)))
        act = hidden * cdf
        slope_ref[0] = cdf + hidden * (jnp.exp(hidden * hidden * -0.5) * (1.0 / math.sqrt(2.0 * math.pi)))
        act_ref[0] = act
        sums[0] = jnp.sum((act * act).reshape(-1, 8, act.shape[1]), axis=0)

    with_rows(pl.program_id(0), w_mine, w_other, step)


def up_project(normed, w_up):
    pixels, width = normed.shape
    block = w_up[0].shape[0] // 2
    cols = pl.BlockSpec((1, pixels, block), lambda h: (h, 0, 0))
    big = jax.ShapeDtypeStruct((4, pixels, block), F32)
    return pl.pallas_call(
        up_kernel,
        grid=(4,),
        in_specs=[whole_block(pixels, width), *half_rows(block, width)],
        out_specs=[cols, cols, pl.BlockSpec((1, 8, block), lambda h: (h, 0, 0))],
        out_shape=[big, big, jax.ShapeDtypeStruct((4, 8, block), F32)],
        compiler_params=params("arbitrary"),
        cost_estimate=cost(9),
        name="up_project",
    )(normed, *w_up)


def mixed_kernel(weighted, w_mine, w_other, act_ref, sq, gm_ref, sums):
    def step(w):
        nt = (((1,), (1,)), ((), ()))
        gm = lax.dot_general(weighted[...], w[...], nt, preferred_element_type=F32)
        gm_ref[0] = gm
        act = act_ref[0]
        sums[0, 0:1, :] = jnp.sum(sq[0], axis=0, keepdims=True)
        sums[0, 1:2, :] = jnp.sum(gm * act, axis=0, keepdims=True)
        sums[0, 2:3, :] = jnp.sum(gm, axis=0, keepdims=True)
        sums[0, 3:4, :] = jnp.zeros((1, act.shape[1]), F32)

    with_rows(pl.program_id(0), w_mine, w_other, step)


def mixed_grad(weighted, w_down, act, sq):
    pixels, width = weighted.shape
    block = w_down[0].shape[0] // 2
    cols = pl.BlockSpec((1, pixels, block), lambda h: (h, 0, 0))
    return pl.pallas_call(
        mixed_kernel,
        grid=(4,),
        in_specs=[
            whole_block(pixels, width),
            *half_rows(block, width),
            cols,
            pl.BlockSpec((1, 8, block), lambda h: (h, 0, 0)),
        ],
        out_specs=[cols, pl.BlockSpec((1, 4, block), lambda h: (h, 0, 0))],
        out_shape=[jax.ShapeDtypeStruct((4, pixels, block), F32), jax.ShapeDtypeStruct((4, 4, block), F32)],
        compiler_params=params("arbitrary"),
        cost_estimate=cost(8),
        name="mixed_grad",
    )(weighted, *w_down, act, sq)


def ratio_of(sq, dot, gamma):
    energy = jnp.sqrt(sq)
    hid = energy.shape[0] * energy.shape[1]
    total = lambda x: jnp.sum(jnp.sum(x, axis=1, keepdims=True), axis=0, keepdims=True)
    mean = total(energy) / hid + EPS_NORM
    grad_ratio = gamma * dot
    shared = total(grad_ratio * energy) / (mean * mean) / hid
    return energy / mean, (grad_ratio / mean - shared) / energy


def outer(left, right):
    return lax.dot_general(left, right, (((0,), (0,)), ((), ())), preferred_element_type=F32).astype(BF16)


def mixed_of(a, gamma, ratio, beta):
    return (gamma * a * ratio + beta + a).astype(BF16)


def down_other_kernel(act, weighted, sums, local, gamma, beta, other, ratio, twice, parts):
    h = pl.program_id(0)

    @pl.when(h == 0)
    def _():
        crop = jnp.sum(sums[...], axis=0)
        sq = jnp.concatenate([crop[n, 0:1] for n in range(4)], axis=0)
        dot = jnp.concatenate([crop[n, 1:2] for n in range(4)], axis=0)
        r, t = ratio_of(sq, dot, gamma[...])
        ratio[...] = r
        twice[...] = t
        for n in range(4):
            parts[0, n : n + 1, :] = local[n, 1:2] * r[n : n + 1]
            parts[1, n : n + 1, :] = local[n, 2:3]

    row = pl.ds(h + 2, 1)
    other[...] = outer(mixed_of(act[0], gamma[row, :], ratio[row, :], beta[row, :]), weighted[...])


def down_other(act, weighted, sums, local, gamma, beta):
    _, pixels, block = act.shape
    width = weighted.shape[1]
    vec = jax.ShapeDtypeStruct((4, block), F32)
    return pl.pallas_call(
        down_other_kernel,
        grid=(2,),
        in_specs=[
            pl.BlockSpec((1, pixels, block), lambda h: (h + 2, 0, 0)),
            whole_block(pixels, width),
            whole_block(*sums.shape),
            whole_block(*local.shape),
            whole_block(4, block),
            whole_block(4, block),
        ],
        out_specs=[
            pl.BlockSpec((block, width), lambda h: (h, 0)),
            whole_block(4, block),
            whole_block(4, block),
            whole_block(2, 4, block),
        ],
        out_shape=[
            jax.ShapeDtypeStruct((2 * block, width), BF16),
            vec,
            vec,
            jax.ShapeDtypeStruct((2, 4, block), F32),
        ],
        compiler_params=params("arbitrary"),
        cost_estimate=cost(4),
        name="down_other",
    )(act, weighted, sums, local, gamma, beta)


def down_mine_kernel(act, weighted, ratio, gamma, beta, mine):
    row = pl.ds(pl.program_id(0), 1)
    mine[...] = outer(mixed_of(act[0], gamma[row, :], ratio[row, :], beta[row, :]), weighted[...])


def down_mine(act, weighted, ratio, gamma, beta):
    _, pixels, block = act.shape
    width = weighted.shape[1]
    return pl.pallas_call(
        down_mine_kernel,
        grid=(2,),
        in_specs=[
            pl.BlockSpec((1, pixels, block), lambda h: (h, 0, 0)),
            whole_block(pixels, width),
            whole_block(4, block),
            whole_block(4, block),
            whole_block(4, block),
        ],
        out_specs=pl.BlockSpec((block, width), lambda h: (h, 0)),
        out_shape=jax.ShapeDtypeStruct((2 * block, width), BF16),
        compiler_params=params("arbitrary"),
        cost_estimate=cost(4),
        name="down_mine",
    )(act, weighted, ratio, gamma, beta)


def hidden_kernel(
    act, slope, gm, w_mine, w_other, normed, ratio, twice, gamma, gain, xhat, rstd,
    mine, other, grad_conv, first, last, gain_part, total,
):
    h = pl.program_id(0)
    row = pl.ds(h, 1)
    grad_act = gm[0] * (gamma[row, :] * ratio[row, :] + 1.0) + act[0] * twice[row, :]
    grad_hidden = (grad_act * slope[0]).astype(BF16)
    term = outer(grad_hidden, normed[...])

    @pl.when(h == 0)
    def _():
        total[...] = jnp.dot(grad_hidden, w_mine[...], preferred_element_type=F32)
        mine[...] = term

    @pl.when(h == 1)
    def _():
        total[...] += jnp.dot(grad_hidden, w_mine[...], preferred_element_type=F32)
        mine[...] = term

    @pl.when(h >= 2)
    def _():
        total[...] += jnp.dot(grad_hidden, w_other[...], preferred_element_type=F32)
        other[...] = term

    @pl.when(h == 3)
    def _():
        pixels, width = total.shape
        block = 64

        def one(t, carry):
            at = pl.ds(pl.multiple_of(t * block, block), block)
            g = total[at, :]
            hat = xhat[at, :]
            carry = carry + jnp.sum((g * hat).reshape(block // 8, 8, width), axis=0)
            g = g * gain[...]
            mean_g = jnp.sum(g, axis=-1, keepdims=True) / width
            mean_gh = jnp.sum(g * hat, axis=-1, keepdims=True) / width
            out = rstd[at, 0:1] * (g - mean_g - hat * mean_gh)
            grad_conv[at, :] = out

            @pl.when(t * block < first.shape[0])
            def _():
                first[at, :] = out.astype(BF16)

            @pl.when(t * block >= pixels - last.shape[0])
            def _():
                last[pl.ds(pl.multiple_of(t * block - (pixels - last.shape[0]), block), block), :] = out.astype(BF16)

            return carry

        gain_part[...] = lax.fori_loop(0, pixels // block, one, jnp.zeros((8, width), F32))


def hidden_grad(act, slope, gm, w_up, normed, ratio, twice, gamma, gain, xhat, rstd, edge):
    _, pixels, block = act.shape
    width = normed.shape[1]
    cols = pl.BlockSpec((1, pixels, block), lambda h: (h, 0, 0))
    vec = whole_block(4, block)
    mine, other = half_rows(block, width)
    term = jax.ShapeDtypeStruct((2 * block, width), BF16)
    return pl.pallas_call(
        hidden_kernel,
        grid=(4,),
        in_specs=[
            cols, cols, cols, mine, other, whole_block(pixels, width), vec, vec, vec,
            whole_block(1, width), whole_block(pixels, width), whole_block(pixels, LANES),
        ],
        out_specs=[
            mine, other, whole_block(pixels, width), whole_block(edge, width), whole_block(edge, width),
            whole_block(8, width),
        ],
        out_shape=[
            term,
            term,
            jax.ShapeDtypeStruct((pixels, width), F32),
            jax.ShapeDtypeStruct((edge, width), BF16),
            jax.ShapeDtypeStruct((edge, width), BF16),
            jax.ShapeDtypeStruct((8, width), F32),
        ],
        scratch_shapes=[pltpu.VMEM((pixels, width), F32)],
        compiler_params=params("arbitrary"),
        cost_estimate=cost(14),
        name="hidden_grad",
    )(act, slope, gm, *w_up, normed, ratio, twice, gamma, gain.reshape(1, width), xhat, rstd)


def taps_grad_kernel(feat, above, below, grad, k_ref, ktaps, part, xs, gs, taps):
    cols = feat.shape[1]

    def chunk(n, lanes):
        fill_padded(xs, above, 0, lanes)
        fill_padded(xs, feat, 3, lanes)
        fill_padded(xs, below, 7, lanes)
        fill_padded(gs, grad, 0, lanes)
        spread_taps(taps, k_ref, True, lanes)
        for start in range(0, cols, GROUP * TILE):
            acc = [[jnp.zeros((TILE, LANES), F32) for _ in range(GROUP)] for _ in range(4)]
            acc = taps_group(gs, taps, own_pairs(), start, acc)
            for o in range(4):
                for b in range(GROUP):
                    part[o, tile_rows(start, b), lanes] = acc[o][b]
        for j in range(7):
            sums = [jnp.zeros((TILE, LANES), F32) for _ in range(7)]
            for start in range(0, cols, TILE):
                g = [gs[o, PAD + start : PAD + start + TILE, :] for o in range(4)]
                for r in range(10):
                    x = xs[r, PAD - 3 + j + start : PAD - 3 + j + start + TILE, :]
                    for o in range(4):
                        if 0 <= r - o <= 6:
                            sums[r - o] = sums[r - o] + x * g[o]
            for i in range(7):
                ktaps[i, j : j + 1, lanes] = jnp.sum(sums[i], axis=0, keepdims=True)

    each_chunk(chunk)


def taps_grad(feat, above, below, grad, kernel):
    rows, cols, width = feat.shape
    return pl.pallas_call(
        taps_grad_kernel,
        grid=(pl.cdiv(width, CHUNKS * LANES),),
        in_specs=[
            lane_blocks(rows, cols),
            lane_blocks(3, cols),
            lane_blocks(3, cols),
            lane_blocks(rows, cols),
            lane_blocks(7, 7),
        ],
        out_specs=[lane_blocks(7, 7), lane_blocks(rows, cols)],
        out_shape=[jax.ShapeDtypeStruct((7, 7, width), F32), jax.ShapeDtypeStruct((rows, cols, width), F32)],
        scratch_shapes=[
            pltpu.VMEM((rows + 6, cols + 2 * PAD, LANES), F32),
            pltpu.VMEM((rows, cols + 2 * PAD, LANES), F32),
            pltpu.VMEM((49, TILE, LANES), F32),
        ],
        compiler_params=params("arbitrary"),
        cost_estimate=cost(9),
        name="taps_grad",
    )(feat, above, below, grad, kernel)


def conv_back_kernel(part, above, below, k_ref, upstream, weight, out, xs, taps):
    cols = part.shape[1]

    def chunk(n, lanes):
        fill_padded(xs, above, 0, lanes)
        fill_padded(xs, below, 3, lanes)
        spread_taps(taps, k_ref, True, lanes)
        for start in range(0, cols, GROUP * TILE):
            acc = [[None] * GROUP for _ in range(4)]
            for o in range(4):
                for b in range(GROUP):
                    at = tile_rows(start, b)
                    acc[o][b] = part[o, at, lanes] + upstream[o, at, lanes].astype(F32) * weight[o, at, :]
            acc = taps_group(xs, taps, halo_pairs(), start, acc)
            for o in range(4):
                for b in range(GROUP):
                    out[o, tile_rows(start, b), lanes] = acc[o][b]

    each_chunk(chunk)


def conv_back(part, above, below, kernel, upstream, weight):
    rows, cols, width = part.shape
    return pl.pallas_call(
        conv_back_kernel,
        grid=(pl.cdiv(width, CHUNKS * LANES),),
        in_specs=[
            lane_blocks(rows, cols),
            lane_blocks(3, cols),
            lane_blocks(3, cols),
            lane_blocks(7, 7),
            lane_blocks(rows, cols),
            whole_block(rows, cols, LANES),
        ],
        out_specs=lane_blocks(rows, cols),
        out_shape=jax.ShapeDtypeStruct((rows, cols, width), F32),
        scratch_shapes=[
            pltpu.VMEM((6, cols + 2 * PAD, LANES), F32),
            pltpu.VMEM((49, TILE, LANES), F32),
        ],
        compiler_params=params("arbitrary"),
        cost_estimate=cost(5),
        name="conv_back",
    )(part, above, below, kernel, upstream, weight)


def chip_kernel(mine, other, vector, out):
    for q in range(mine.shape[0]):
        high = (mine[q, :128, :].astype(F32) + other[q, :128, :].astype(F32)).astype(BF16)
        low = mine[q, 128:, :].astype(F32) + other[q, 128:, :].astype(F32)
        for s in range(8):
            out[q * 8 + s, :16, :] = high[16 * s : 16 * (s + 1), :]
            rest = low[6 * s : 6 * (s + 1), :]
            if vector is not None:
                rest = jnp.concatenate([rest, vector[s]], axis=0)
            out[q * 8 + s, 16:, :] = rest.astype(BF16)


def chip_sum(mine, other, vector=None):
    owners, owned, width = mine.shape
    piece = owned // 8 + (0 if vector is None else vector.shape[1])
    rows = pl.BlockSpec((owners // 2, owned, width), lambda q: (q, 0, 0))
    given = [] if vector is None else [vector]
    kernel = chip_kernel if given else lambda mine, other, out: chip_kernel(mine, other, None, out)
    return pl.pallas_call(
        kernel,
        grid=(2,),
        in_specs=[rows, rows] + [whole_block(*v.shape) for v in given],
        out_specs=pl.BlockSpec((owners * 4, piece, width), lambda q: (q, 0, 0)),
        out_shape=jax.ShapeDtypeStruct((owners * 8, piece, width), BF16),
        compiler_params=params("arbitrary"),
        cost_estimate=cost(3),
        name="chip_sum",
    )(mine, other, *given)


BOTH = ("dp", "space")


def device(y, z, c, x, low):
    return (y * 8 + z * 2 + c) * 8 + x * 2 + low


OWNERS = [
    [device(y, z, c, x, low ^ y) for y in range(2) for z in range(4)]
    for c in range(2)
    for x in range(4)
    for low in range(2)
]
CORES = [
    [device(y, z, c, x, low) for y in range(2) for z in range(4) for x in range(4) for low in range(2)]
    for c in range(2)
]

SWAP = [
    (device(y, z, c, x, low), device(y, z, 1 - c, x, low))
    for y in range(2)
    for z in range(4)
    for c in range(2)
    for x in range(4)
    for low in range(2)
]


def to_other_core(value):
    return lax.ppermute(value, BOTH, SWAP)


def gather_mine(shard):
    return lax.all_to_all(jnp.broadcast_to(shard, (8,) + shard.shape), BOTH, 0, 0, axis_index_groups=OWNERS)


def with_other(mine):
    other = to_other_core(mine)
    return mine.reshape(-1, mine.shape[2]), other.reshape(-1, mine.shape[2])


def local_order(vector, owned):
    first, second = core_halves(vector.reshape(8, 2, owned), 1)
    return jnp.concatenate([first.reshape(2, -1), second.reshape(2, -1)], axis=0)


def core_halves(value, axis):
    c = lax.axis_index("dp") % 2
    low, high = lax.index_in_dim(value, 0, axis, False), lax.index_in_dim(value, 1, axis, False)
    return jnp.where(c == 0, low, high), jnp.where(c == 0, high, low)


def global_order(blocks, owned):
    n = blocks.shape[0]
    low, high = core_halves(blocks.reshape(n, 2, 8, owned), 1)
    return jnp.stack([low, high], axis=2).reshape(n, -1)


def sum_blocks(blocks):
    return jnp.sum(lax.all_to_all(blocks, BOTH, 0, 0, axis_index_groups=CORES).astype(F32), axis=0)


def exchange(value, axis):
    return lax.all_to_all(value, axis, 0, 0)


def everyone(value, axis):
    return exchange(jnp.broadcast_to(value, (lax.axis_size(axis),) + value.shape), axis)


def shift(rows, pairs):
    flat = rows.reshape(-1, 16, rows.shape[-1])
    return lax.ppermute(flat, "space", pairs).reshape(rows.shape)


def body(
    features, kernel, norm_gain, w_up, grn_gamma, grn_beta, w_down, upstream, labels, class_weight
):
    crops, rows, cols, width = features.shape
    feat, up = features[0], upstream[0]
    space = lax.axis_size("space")
    dp = lax.axis_size("dp")
    owned = w_up.shape[0]
    hid = owned * dp
    pixels = rows * cols
    rising = [(i, i + 1) for i in range(space - 1)]
    falling = [(j, i) for i, j in rising]
    above = shift(feat[rows - 3 :], rising)
    below = shift(feat[:3], falling)
    part = conv_own(feat, kernel)
    mine = gather_mine(jnp.concatenate([w_up, w_down], axis=0))
    w_up_mine, w_down_mine = mine[:, :owned], mine[:, owned:]
    gamma, beta = local_order(grn_gamma, owned), local_order(grn_beta, owned)

    classes = jnp.arange(class_weight.shape[0], dtype=jnp.int32)
    pixel_weight = jnp.sum(jnp.where(labels[0][..., None] == classes, class_weight, 0.0), axis=-1)
    weight = jnp.broadcast_to(pixel_weight[..., None], (rows, cols, LANES))
    weighted = (up.astype(F32) * pixel_weight[..., None]).astype(BF16).reshape(pixels, width)

    normed, xhat, rstd = conv_norm(part, above, below, kernel, norm_gain)
    w_up_mine, w_down_mine, rstd = lax.optimization_barrier((w_up_mine, w_down_mine, rstd))
    w_up_all = with_other(w_up_mine)
    act, slope, sq = up_project(normed, w_up_all)
    w_down_mine, sq = lax.optimization_barrier((w_down_mine, sq))
    w_down_all = with_other(w_down_mine)
    gm, local = mixed_grad(weighted, w_down_all, act, sq)
    sums = everyone(local, "space")
    down_other_term, ratio, twice, parts = down_other(act, weighted, sums, local, gamma, beta)
    by_owner = lambda rows: rows.reshape(8, owned, width)
    came = to_other_core(by_owner(down_other_term))
    down_blocks = chip_sum(by_owner(down_mine(act, weighted, ratio, gamma, beta)), came)
    ratio, down_blocks = lax.optimization_barrier((ratio, down_blocks))
    down_rows = sum_blocks(down_blocks)
    up_mine, up_other, grad_conv, g_first, g_last, gain_part = hidden_grad(
        act, slope, gm, w_up_all, normed, ratio, twice, gamma, norm_gain, xhat, rstd, 3 * cols
    )
    grad_conv = grad_conv.reshape(rows, cols, width)
    g_above = shift(g_last.reshape(3, cols, width), rising)
    g_below = shift(g_first.reshape(3, cols, width), falling)
    kernel_part, back = taps_grad(feat, above, below, grad_conv, kernel)

    scale = 1.0 / math.sqrt(dp * space * pixels)
    vector = jnp.concatenate(
        [
            kernel_part.reshape(49, width),
            jnp.sum(gain_part, axis=0, keepdims=True),
            global_order(parts, owned).reshape(-1, width),
        ],
        axis=0,
    )
    lines = vector.shape[0]
    vector = jnp.pad(vector, ((0, -lines % 64), (0, 0)))
    vector, g_above, g_below = lax.optimization_barrier((vector, g_above, g_below))
    vector = (vector + to_other_core(vector)).reshape(8, 8, width)
    up_blocks = chip_sum(by_owner(up_mine), to_other_core(by_owner(up_other)), vector)
    up_blocks, down_rows = lax.optimization_barrier((up_blocks, down_rows))
    up_rows = sum_blocks(up_blocks)
    grad_features = conv_back(back, g_above, g_below, kernel, up, weight)
    up_rows, grad_features = lax.optimization_barrier((up_rows, grad_features))

    piece = owned // space
    block = jnp.concatenate([up_rows[:piece], down_rows], axis=1)
    block = jnp.concatenate([block, up_rows[piece:].reshape(4, 2 * width)], axis=0)
    block = everyone((scale * block).astype(BF16), "space").astype(F32)
    vector = block[:, piece:].reshape(8 * space, width)
    kernel_sum = vector[:49].reshape(7, 7, width)
    gain_sum = vector[49]
    gamma_sum, beta_sum = vector[50:lines].reshape(2, hid)
    block = jnp.concatenate([block[:, :16].reshape(-1, 2 * width), block[:, 16:piece].reshape(-1, 2 * width)], axis=0)
    return (
        grad_features[None],
        kernel_sum,
        gain_sum,
        block[:, :width],
        gamma_sum,
        beta_sum,
        block[:, width:],
    )


def solution(mesh):
    return jax.shard_map(
        body,
        mesh=mesh,
        in_specs=(
            P("dp", "space", None, None),
            P(),
            P(),
            P("dp", None),
            P(),
            P(),
            P("dp", None),
            P("dp", "space", None, None),
            P("dp", "space", None),
            P(),
        ),
        out_specs=(P("dp", "space", None, None), P(), P(), P("dp", None), P(), P(), P("dp", None)),
        check_vma=False,
    )
```

```python
import functools
import math

import jax
import jax.numpy as jnp
from jax import lax
from jax.experimental import pallas as pl
from jax.experimental.pallas import tpu as pltpu
from jax.sharding import PartitionSpec as P

EPS_NORM = 1e-06
F32 = jnp.float32
BF16 = jnp.bfloat16
VMEM_LIMIT = 56 * 1024 * 1024
LANES = 128
PAD = 8
TILE = 8
GROUP = 4
CHUNKS = 3


def params(*semantics):
    return pltpu.CompilerParams(dimension_semantics=semantics, vmem_limit_bytes=VMEM_LIMIT)


def cost(micros):
    return pl.CostEstimate(flops=int(micros * 0.4e9), transcendentals=0, bytes_accessed=0)


def fill_padded(dst, src, first, lanes):
    rows, cols, _ = src.shape
    zeros = jnp.zeros((rows, PAD, LANES), F32)
    dst[first : first + rows, 0:PAD, :] = zeros
    dst[first : first + rows, PAD + cols : PAD + cols + PAD, :] = zeros
    dst[first : first + rows, PAD : PAD + cols, :] = src[:, :, lanes].astype(F32)


def spread_taps(dst, k_ref, flip, lanes):
    for i in range(7):
        for j in range(7):
            tap = k_ref[6 - i, 6 - j : 7 - j, lanes] if flip else k_ref[i, j : j + 1, lanes]
            dst[i * 7 + j] = jnp.broadcast_to(tap, (TILE, LANES))


def taps_group(src, taps, pairs, start, acc):
    rows = sorted({r for r, _, _ in pairs})
    for j in range(7):
        for r in rows:
            todo = [(o, i) for rr, o, i in pairs if rr == r]
            at = [start + TILE * b + PAD - 3 + j for b in range(GROUP)]
            xs = [src[r, p : p + TILE, :] for p in at]
            for o, i in todo:
                tap = taps[i * 7 + j]
                for b in range(GROUP):
                    acc[o][b] = acc[o][b] + xs[b] * tap
    return acc


def own_pairs():
    return [(s, o, s - o + 3) for s in range(4) for o in range(4)]


def halo_pairs():
    above = [(s, o, s - o) for s in range(3) for o in range(4) if 0 <= s - o <= 6]
    below = [(3 + s, o, s + 7 - o) for s in range(3) for o in range(4) if 0 <= s + 7 - o <= 6]
    return above + below


def each_chunk(body):
    def one(n, carry):
        body(n, pl.ds(pl.multiple_of(n * LANES, LANES), LANES))
        return carry

    lax.fori_loop(0, CHUNKS, one, 0)


def tile_rows(start, b):
    return slice(start + TILE * b, start + TILE * (b + 1))


def conv_own_kernel(feat, k_ref, out, xs, taps):
    cols = feat.shape[1]

    def chunk(n, lanes):
        fill_padded(xs, feat, 0, lanes)
        spread_taps(taps, k_ref, False, lanes)
        for start in range(0, cols, GROUP * TILE):
            acc = [[jnp.zeros((TILE, LANES), F32) for _ in range(GROUP)] for _ in range(4)]
            acc = taps_group(xs, taps, own_pairs(), start, acc)
            for o in range(4):
                for b in range(GROUP):
                    out[o, tile_rows(start, b), lanes] = acc[o][b]

    each_chunk(chunk)


def lane_blocks(rows, cols):
    return pl.BlockSpec((rows, cols, CHUNKS * LANES), lambda c: (0, 0, c))


def whole_block(*shape):
    return pl.BlockSpec(shape, lambda c: (0,) * len(shape))


def conv_own(feat, kernel):
    rows, cols, width = feat.shape
    return pl.pallas_call(
        conv_own_kernel,
        grid=(pl.cdiv(width, CHUNKS * LANES),),
        in_specs=[lane_blocks(rows, cols), lane_blocks(7, 7)],
        out_specs=lane_blocks(rows, cols),
        out_shape=jax.ShapeDtypeStruct((rows, cols, width), F32),
        scratch_shapes=[
            pltpu.VMEM((rows, cols + 2 * PAD, LANES), F32),
            pltpu.VMEM((49, TILE, LANES), F32),
        ],
        compiler_params=params("arbitrary"),
        cost_estimate=cost(5),
        name="conv_own",
    )(feat, kernel)


def conv_norm_kernel(width, steps, part, above, below, k_ref, gain, normed, xhat, rstd, xs, taps, conv):
    c = pl.program_id(0)
    cols = part.shape[1]

    def chunk(n, lanes):
        fill_padded(xs, above, 0, lanes)
        fill_padded(xs, below, 3, lanes)
        spread_taps(taps, k_ref, False, lanes)
        for start in range(0, cols, GROUP * TILE):
            acc = [[part[o, tile_rows(start, b), lanes] for b in range(GROUP)] for o in range(4)]
            acc = taps_group(xs, taps, halo_pairs(), start, acc)
            for o in range(4):
                for b in range(GROUP):
                    conv[c * CHUNKS + n, tile_rows(o * cols + start, b), :] = acc[o][b]

    each_chunk(chunk)

    @pl.when(c == steps - 1)
    def _():
        chunks = pl.cdiv(width, LANES)
        last = width - (chunks - 1) * LANES
        block = 64

        def one(t, carry):
            at = pl.multiple_of(t * block, block)
            parts = [conv[n, pl.ds(at, block), :] for n in range(chunks)]
            lane = lax.broadcasted_iota(jnp.int32, (block, LANES), 1)
            inside = lane < last
            parts[-1] = jnp.where(inside, parts[-1], 0.0)
            mean = jnp.sum(sum(parts[1:], parts[0]), axis=-1, keepdims=True) / width
            centred = [p - mean for p in parts]
            centred[-1] = jnp.where(inside, centred[-1], 0.0)
            squares = [p * p for p in centred]
            var = jnp.sum(sum(squares[1:], squares[0]), axis=-1, keepdims=True) / width
            scale = lax.rsqrt(var + EPS_NORM)
            rstd[pl.ds(at, block), :] = jnp.broadcast_to(scale, (block, LANES))
            for n in range(chunks):
                w = min(LANES, width - n * LANES)
                hat = centred[n] * scale
                g = gain[:, n * LANES : n * LANES + w]
                xhat[pl.ds(at, block), n * LANES : n * LANES + w] = hat[:, :w]
                normed[pl.ds(at, block), n * LANES : n * LANES + w] = (hat[:, :w] * g).astype(BF16)
            return carry

        lax.fori_loop(0, (4 * cols) // block, one, 0)


def conv_norm(part, above, below, kernel, gain):
    rows, cols, width = part.shape
    steps = pl.cdiv(width, CHUNKS * LANES)
    pixels = rows * cols
    return pl.pallas_call(
        functools.partial(conv_norm_kernel, width, steps),
        grid=(steps,),
        in_specs=[
            lane_blocks(rows, cols),
            lane_blocks(3, cols),
            lane_blocks(3, cols),
            lane_blocks(7, 7),
            whole_block(1, width),
        ],
        out_specs=[whole_block(pixels, width), whole_block(pixels, width), whole_block(pixels, LANES)],
        out_shape=[
            jax.ShapeDtypeStruct((pixels, width), BF16),
            jax.ShapeDtypeStruct((pixels, width), F32),
            jax.ShapeDtypeStruct((pixels, LANES), F32),
        ],
        scratch_shapes=[
            pltpu.VMEM((6, cols + 2 * PAD, LANES), F32),
            pltpu.VMEM((49, TILE, LANES), F32),
            pltpu.VMEM((steps * CHUNKS, pixels, LANES), F32),
        ],
        compiler_params=params("arbitrary"),
        cost_estimate=cost(7),
        name="conv_norm",
    )(part, above, below, kernel, gain.reshape(1, width))


def with_rows(h, mine, other, step):
    pl.when(h < 2)(lambda: step(mine))
    pl.when(h >= 2)(lambda: step(other))


def half_rows(block, width):
    mine = pl.BlockSpec((block, width), lambda h: (jnp.minimum(h, 1), 0))
    other = pl.BlockSpec((block, width), lambda h: (jnp.maximum(h - 2, 0), 0))
    return mine, other


def up_kernel(normed, w_mine, w_other, act_ref, slope_ref, sums):
    def step(w):
        nt = (((1,), (1,)), ((), ()))
        hidden = lax.dot_general(normed[...], w[...], nt, preferred_element_type=F32)
        cdf = 0.5 * (1.0 + lax.erf(hidden * (2.0**-0.5)))
        act = hidden * cdf
        slope_ref[0] = cdf + hidden * (jnp.exp(hidden * hidden * -0.5) * (1.0 / math.sqrt(2.0 * math.pi)))
        act_ref[0] = act
        sums[0] = jnp.sum((act * act).reshape(-1, 8, act.shape[1]), axis=0)

    with_rows(pl.program_id(0), w_mine, w_other, step)


def up_project(normed, w_up):
    pixels, width = normed.shape
    block = w_up[0].shape[0] // 2
    cols = pl.BlockSpec((1, pixels, block), lambda h: (h, 0, 0))
    big = jax.ShapeDtypeStruct((4, pixels, block), F32)
    return pl.pallas_call(
        up_kernel,
        grid=(4,),
        in_specs=[whole_block(pixels, width), *half_rows(block, width)],
        out_specs=[cols, cols, pl.BlockSpec((1, 8, block), lambda h: (h, 0, 0))],
        out_shape=[big, big, jax.ShapeDtypeStruct((4, 8, block), F32)],
        compiler_params=params("arbitrary"),
        cost_estimate=cost(9),
        name="up_project",
    )(normed, *w_up)


def mixed_kernel(weighted, w_mine, w_other, act_ref, sq, gm_ref, sums, gm_sum):
    def step(w):
        nt = (((1,), (1,)), ((), ()))
        gm = lax.dot_general(weighted[...], w[...], nt, preferred_element_type=F32)
        gm_ref[0] = gm
        act = act_ref[0]
        sums[0, 0:1, :] = jnp.sum(sq[0], axis=0, keepdims=True)
        sums[0, 1:2, :] = jnp.sum(gm * act, axis=0, keepdims=True)
        gm_sum[0] = jnp.sum(gm, axis=0, keepdims=True)

    with_rows(pl.program_id(0), w_mine, w_other, step)


def mixed_grad(weighted, w_down, act, sq):
    pixels, width = weighted.shape
    block = w_down[0].shape[0] // 2
    cols = pl.BlockSpec((1, pixels, block), lambda h: (h, 0, 0))
    return pl.pallas_call(
        mixed_kernel,
        grid=(4,),
        in_specs=[
            whole_block(pixels, width),
            *half_rows(block, width),
            cols,
            pl.BlockSpec((1, 8, block), lambda h: (h, 0, 0)),
        ],
        out_specs=[
            cols,
            pl.BlockSpec((1, 2, block), lambda h: (h, 0, 0)),
            pl.BlockSpec((1, 1, block), lambda h: (h, 0, 0)),
        ],
        out_shape=[
            jax.ShapeDtypeStruct((4, pixels, block), F32),
            jax.ShapeDtypeStruct((4, 2, block), F32),
            jax.ShapeDtypeStruct((4, 1, block), F32),
        ],
        compiler_params=params("arbitrary"),
        cost_estimate=cost(8),
        name="mixed_grad",
    )(weighted, *w_down, act, sq)


def ratio_of(sq, dot, gamma):
    energy = jnp.sqrt(sq)
    hid = energy.shape[0] * energy.shape[1]
    total = lambda x: jnp.sum(jnp.sum(x, axis=1, keepdims=True), axis=0, keepdims=True)
    mean = total(energy) / hid + EPS_NORM
    grad_ratio = gamma * dot
    shared = total(grad_ratio * energy) / (mean * mean) / hid
    return energy / mean, (grad_ratio / mean - shared) / energy


def outer(left, right):
    return lax.dot_general(left, right, (((0,), (0,)), ((), ())), preferred_element_type=F32).astype(BF16)


def mixed_of(a, gamma, ratio, beta):
    return (gamma * a * ratio + beta + a).astype(BF16)


def down_other_kernel(act, weighted, sums, local, gm_sum, gamma, beta, other, ratio, twice, parts):
    h = pl.program_id(0)

    @pl.when(h == 0)
    def _():
        crop = jnp.sum(sums[...], axis=0)
        sq = jnp.concatenate([crop[n, 0:1] for n in range(4)], axis=0)
        dot = jnp.concatenate([crop[n, 1:2] for n in range(4)], axis=0)
        r, t = ratio_of(sq, dot, gamma[...])
        ratio[...] = r
        twice[...] = t
        for n in range(4):
            parts[0, n : n + 1, :] = local[n, 1:2] * r[n : n + 1]
            parts[1, n : n + 1, :] = gm_sum[n]

    row = pl.ds(h + 2, 1)
    other[...] = outer(mixed_of(act[0], gamma[row, :], ratio[row, :], beta[row, :]), weighted[...])


def down_other(act, weighted, sums, local, gm_sum, gamma, beta):
    _, pixels, block = act.shape
    width = weighted.shape[1]
    vec = jax.ShapeDtypeStruct((4, block), F32)
    return pl.pallas_call(
        down_other_kernel,
        grid=(2,),
        in_specs=[
            pl.BlockSpec((1, pixels, block), lambda h: (h + 2, 0, 0)),
            whole_block(pixels, width),
            whole_block(*sums.shape),
            whole_block(*local.shape),
            whole_block(*gm_sum.shape),
            whole_block(4, block),
            whole_block(4, block),
        ],
        out_specs=[
            pl.BlockSpec((block, width), lambda h: (h, 0)),
            whole_block(4, block),
            whole_block(4, block),
            whole_block(2, 4, block),
        ],
        out_shape=[
            jax.ShapeDtypeStruct((2 * block, width), BF16),
            vec,
            vec,
            jax.ShapeDtypeStruct((2, 4, block), F32),
        ],
        compiler_params=params("arbitrary"),
        cost_estimate=cost(4),
        name="down_other",
    )(act, weighted, sums, local, gm_sum, gamma, beta)


def down_mine_kernel(act, weighted, ratio, gamma, beta, mine):
    row = pl.ds(pl.program_id(0), 1)
    mine[...] = outer(mixed_of(act[0], gamma[row, :], ratio[row, :], beta[row, :]), weighted[...])


def down_mine(act, weighted, ratio, gamma, beta):
    _, pixels, block = act.shape
    width = weighted.shape[1]
    return pl.pallas_call(
        down_mine_kernel,
        grid=(2,),
        in_specs=[
            pl.BlockSpec((1, pixels, block), lambda h: (h, 0, 0)),
            whole_block(pixels, width),
            whole_block(4, block),
            whole_block(4, block),
            whole_block(4, block),
        ],
        out_specs=pl.BlockSpec((block, width), lambda h: (h, 0)),
        out_shape=jax.ShapeDtypeStruct((2 * block, width), BF16),
        compiler_params=params("arbitrary"),
        cost_estimate=cost(4),
        name="down_mine",
    )(act, weighted, ratio, gamma, beta)


def hidden_kernel(
    act, slope, gm, w_mine, w_other, normed, ratio, twice, gamma, gain, xhat, rstd,
    mine, other, grad_conv, first, last, gain_part, total,
):
    h = pl.program_id(0)
    row = pl.ds(h, 1)
    grad_act = gm[0] * (gamma[row, :] * ratio[row, :] + 1.0) + act[0] * twice[row, :]
    grad_hidden = (grad_act * slope[0]).astype(BF16)
    term = outer(grad_hidden, normed[...])

    @pl.when(h == 0)
    def _():
        total[...] = jnp.dot(grad_hidden, w_mine[...], preferred_element_type=F32)
        mine[...] = term

    @pl.when(h == 1)
    def _():
        total[...] += jnp.dot(grad_hidden, w_mine[...], preferred_element_type=F32)
        mine[...] = term

    @pl.when(h >= 2)
    def _():
        total[...] += jnp.dot(grad_hidden, w_other[...], preferred_element_type=F32)
        other[...] = term

    @pl.when(h == 3)
    def _():
        pixels, width = total.shape
        block = 64

        def one(t, carry):
            at = pl.ds(pl.multiple_of(t * block, block), block)
            g = total[at, :]
            hat = xhat[at, :]
            carry = carry + jnp.sum((g * hat).reshape(block // 8, 8, width), axis=0)
            g = g * gain[...]
            mean_g = jnp.sum(g, axis=-1, keepdims=True) / width
            mean_gh = jnp.sum(g * hat, axis=-1, keepdims=True) / width
            out = rstd[at, 0:1] * (g - mean_g - hat * mean_gh)
            grad_conv[at, :] = out

            @pl.when(t * block < first.shape[0])
            def _():
                first[at, :] = out.astype(BF16)

            @pl.when(t * block >= pixels - last.shape[0])
            def _():
                last[pl.ds(pl.multiple_of(t * block - (pixels - last.shape[0]), block), block), :] = out.astype(BF16)

            return carry

        gain_part[...] = lax.fori_loop(0, pixels // block, one, jnp.zeros((8, width), F32))


def hidden_grad(act, slope, gm, w_up, normed, ratio, twice, gamma, gain, xhat, rstd, edge):
    _, pixels, block = act.shape
    width = normed.shape[1]
    cols = pl.BlockSpec((1, pixels, block), lambda h: (h, 0, 0))
    vec = whole_block(4, block)
    mine, other = half_rows(block, width)
    term = jax.ShapeDtypeStruct((2 * block, width), BF16)
    return pl.pallas_call(
        hidden_kernel,
        grid=(4,),
        in_specs=[
            cols, cols, cols, mine, other, whole_block(pixels, width), vec, vec, vec,
            whole_block(1, width), whole_block(pixels, width), whole_block(pixels, LANES),
        ],
        out_specs=[
            mine, other, whole_block(pixels, width), whole_block(edge, width), whole_block(edge, width),
            whole_block(8, width),
        ],
        out_shape=[
            term,
            term,
            jax.ShapeDtypeStruct((pixels, width), F32),
            jax.ShapeDtypeStruct((edge, width), BF16),
            jax.ShapeDtypeStruct((edge, width), BF16),
            jax.ShapeDtypeStruct((8, width), F32),
        ],
        scratch_shapes=[pltpu.VMEM((pixels, width), F32)],
        compiler_params=params("arbitrary"),
        cost_estimate=cost(14),
        name="hidden_grad",
    )(act, slope, gm, *w_up, normed, ratio, twice, gamma, gain.reshape(1, width), xhat, rstd)


def taps_grad_kernel(feat, above, below, grad, ktaps, xs, gs):
    cols = feat.shape[1]

    def chunk(n, lanes):
        fill_padded(xs, above, 0, lanes)
        fill_padded(xs, feat, 3, lanes)
        fill_padded(xs, below, 7, lanes)
        gs[...] = grad[:, :, lanes]
        for j in range(7):
            sums = [jnp.zeros((TILE, LANES), F32) for _ in range(7)]
            for start in range(0, cols, TILE):
                g = [gs[o, start : start + TILE, :] for o in range(4)]
                for r in range(10):
                    x = xs[r, PAD - 3 + j + start : PAD - 3 + j + start + TILE, :]
                    for o in range(4):
                        if 0 <= r - o <= 6:
                            sums[r - o] = sums[r - o] + x * g[o]
            for i in range(7):
                ktaps[i, j : j + 1, lanes] = jnp.sum(sums[i], axis=0, keepdims=True)

    each_chunk(chunk)


def taps_grad(feat, above, below, grad):
    rows, cols, width = feat.shape
    return pl.pallas_call(
        taps_grad_kernel,
        grid=(pl.cdiv(width, CHUNKS * LANES),),
        in_specs=[
            lane_blocks(rows, cols),
            lane_blocks(3, cols),
            lane_blocks(3, cols),
            lane_blocks(rows, cols),
        ],
        out_specs=lane_blocks(7, 7),
        out_shape=jax.ShapeDtypeStruct((7, 7, width), F32),
        scratch_shapes=[
            pltpu.VMEM((rows + 6, cols + 2 * PAD, LANES), F32),
            pltpu.VMEM((rows, cols, LANES), F32),
        ],
        compiler_params=params("arbitrary"),
        cost_estimate=cost(1),
        name="taps_grad",
    )(feat, above, below, grad)


def all_pairs():
    return [(r, o, r - o) for r in range(10) for o in range(4) if 0 <= r - o <= 6]


def conv_back_kernel(grad, above, below, k_ref, upstream, weight, out, xs, taps):
    cols = grad.shape[1]

    def chunk(n, lanes):
        fill_padded(xs, above, 0, lanes)
        fill_padded(xs, grad, 3, lanes)
        fill_padded(xs, below, 7, lanes)
        spread_taps(taps, k_ref, True, lanes)
        for start in range(0, cols, GROUP * TILE):
            acc = [[None] * GROUP for _ in range(4)]
            for o in range(4):
                for b in range(GROUP):
                    at = tile_rows(start, b)
                    acc[o][b] = upstream[o, at, lanes].astype(F32) * weight[o, at, :]
            acc = taps_group(xs, taps, all_pairs(), start, acc)
            for o in range(4):
                for b in range(GROUP):
                    out[o, tile_rows(start, b), lanes] = acc[o][b]

    each_chunk(chunk)


def conv_back(grad, above, below, kernel, upstream, weight):
    rows, cols, width = grad.shape
    return pl.pallas_call(
        conv_back_kernel,
        grid=(pl.cdiv(width, CHUNKS * LANES),),
        in_specs=[
            lane_blocks(rows, cols),
            lane_blocks(3, cols),
            lane_blocks(3, cols),
            lane_blocks(7, 7),
            lane_blocks(rows, cols),
            whole_block(rows, cols, LANES),
        ],
        out_specs=lane_blocks(rows, cols),
        out_shape=jax.ShapeDtypeStruct((rows, cols, width), F32),
        scratch_shapes=[
            pltpu.VMEM((rows + 6, cols + 2 * PAD, LANES), F32),
            pltpu.VMEM((49, TILE, LANES), F32),
        ],
        compiler_params=params("arbitrary"),
        cost_estimate=cost(60),
        name="conv_back",
    )(grad, above, below, kernel, upstream, weight)


def chip_kernel(mine, other, vector, out):
    for q in range(mine.shape[0]):
        high = (mine[q, :128, :].astype(F32) + other[q, :128, :].astype(F32)).astype(BF16)
        low = mine[q, 128:, :].astype(F32) + other[q, 128:, :].astype(F32)
        for s in range(8):
            out[q * 8 + s, :16, :] = high[16 * s : 16 * (s + 1), :]
            rest = low[6 * s : 6 * (s + 1), :]
            if vector is not None:
                rest = jnp.concatenate([rest, vector[s]], axis=0)
            out[q * 8 + s, 16:, :] = rest.astype(BF16)


def chip_sum(mine, other, vector=None):
    owners, owned, width = mine.shape
    piece = owned // 8 + (0 if vector is None else vector.shape[1])
    rows = pl.BlockSpec((owners // 2, owned, width), lambda q: (q, 0, 0))
    given = [] if vector is None else [vector]
    kernel = chip_kernel if given else lambda mine, other, out: chip_kernel(mine, other, None, out)
    return pl.pallas_call(
        kernel,
        grid=(2,),
        in_specs=[rows, rows] + [whole_block(*v.shape) for v in given],
        out_specs=pl.BlockSpec((owners * 4, piece, width), lambda q: (q, 0, 0)),
        out_shape=jax.ShapeDtypeStruct((owners * 8, piece, width), BF16),
        compiler_params=params("arbitrary"),
        cost_estimate=cost(0.3),
        name="chip_sum",
    )(mine, other, *given)


BOTH = ("dp", "space")


def device(y, z, c, x, low):
    return (y * 8 + z * 2 + c) * 8 + x * 2 + low


OWNERS = [
    [device(y, z, c, x, low ^ y) for y in range(2) for z in range(4)]
    for c in range(2)
    for x in range(4)
    for low in range(2)
]
CORES = [
    [device(y, z, c, x, low) for y in range(2) for z in range(4) for x in range(4) for low in range(2)]
    for c in range(2)
]

SWAP = [
    (device(y, z, c, x, low), device(y, z, 1 - c, x, low))
    for y in range(2)
    for z in range(4)
    for c in range(2)
    for x in range(4)
    for low in range(2)
]


def to_other_core(value):
    return lax.ppermute(value, BOTH, SWAP)


def gather_mine(shard):
    return lax.all_to_all(jnp.broadcast_to(shard, (8,) + shard.shape), BOTH, 0, 0, axis_index_groups=OWNERS)


def with_other(mine):
    other = to_other_core(mine)
    return mine.reshape(-1, mine.shape[2]), other.reshape(-1, mine.shape[2])


def local_order(vector, owned):
    first, second = core_halves(vector.reshape(8, 2, owned), 1)
    return jnp.concatenate([first.reshape(2, -1), second.reshape(2, -1)], axis=0)


def core_halves(value, axis):
    c = lax.axis_index("dp") % 2
    low, high = lax.index_in_dim(value, 0, axis, False), lax.index_in_dim(value, 1, axis, False)
    return jnp.where(c == 0, low, high), jnp.where(c == 0, high, low)


def global_order(blocks, owned):
    n = blocks.shape[0]
    low, high = core_halves(blocks.reshape(n, 2, 8, owned), 1)
    return jnp.stack([low, high], axis=2).reshape(n, -1)


def sum_blocks(blocks):
    return jnp.sum(lax.all_to_all(blocks, BOTH, 0, 0, axis_index_groups=CORES).astype(F32), axis=0)


def exchange(value, axis):
    return lax.all_to_all(value, axis, 0, 0)


def everyone(value, axis):
    return exchange(jnp.broadcast_to(value, (lax.axis_size(axis),) + value.shape), axis)


def shift(rows, pairs):
    flat = rows.reshape(-1, 16, rows.shape[-1])
    return lax.ppermute(flat, "space", pairs).reshape(rows.shape)


def body(
    features, kernel, norm_gain, w_up, grn_gamma, grn_beta, w_down, upstream, labels, class_weight
):
    crops, rows, cols, width = features.shape
    feat, up = features[0], upstream[0]
    space = lax.axis_size("space")
    dp = lax.axis_size("dp")
    owned = w_up.shape[0]
    hid = owned * dp
    pixels = rows * cols
    rising = [(i, i + 1) for i in range(space - 1)]
    falling = [(j, i) for i, j in rising]
    above = shift(feat[rows - 3 :], rising)
    below = shift(feat[:3], falling)
    part = conv_own(feat, kernel)
    w_up_mine = gather_mine(w_up)
    w_up_mine, w_down, part, above, below = lax.optimization_barrier((w_up_mine, w_down, part, above, below))
    w_down_mine = gather_mine(w_down)
    gamma, beta = local_order(grn_gamma, owned), local_order(grn_beta, owned)

    classes = jnp.arange(class_weight.shape[0], dtype=jnp.int32)
    pixel_weight = jnp.sum(jnp.where(labels[0][..., None] == classes, class_weight, 0.0), axis=-1)
    weight = jnp.broadcast_to(pixel_weight[..., None], (rows, cols, LANES))
    weighted = (up.astype(F32) * pixel_weight[..., None]).astype(BF16).reshape(pixels, width)

    normed, xhat, rstd = conv_norm(part, above, below, kernel, norm_gain)
    w_up_all = with_other(w_up_mine)
    act, slope, sq = up_project(normed, w_up_all)
    w_down_mine, sq = lax.optimization_barrier((w_down_mine, sq))
    w_down_all = with_other(w_down_mine)
    gm, local, gm_sum = mixed_grad(weighted, w_down_all, act, sq)
    sums = everyone(local, "space")
    down_other_term, ratio, twice, parts = down_other(act, weighted, sums, local, gm_sum, gamma, beta)
    by_owner = lambda rows: rows.reshape(8, owned, width)
    came = to_other_core(by_owner(down_other_term))
    down_blocks = chip_sum(by_owner(down_mine(act, weighted, ratio, gamma, beta)), came)
    ratio, down_blocks = lax.optimization_barrier((ratio, down_blocks))
    down_rows = sum_blocks(down_blocks)
    up_mine, up_other, grad_conv, g_first, g_last, gain_part = hidden_grad(
        act, slope, gm, w_up_all, normed, ratio, twice, gamma, norm_gain, xhat, rstd, 3 * cols
    )
    grad_conv = grad_conv.reshape(rows, cols, width)
    g_above = shift(g_last.reshape(3, cols, width), rising)
    g_below = shift(g_first.reshape(3, cols, width), falling)
    kernel_part = taps_grad(feat, above, below, grad_conv)

    scale = 1.0 / math.sqrt(dp * space * pixels)
    vector = jnp.concatenate(
        [
            kernel_part.reshape(49, width),
            jnp.sum(gain_part, axis=0, keepdims=True),
            global_order(parts, owned).reshape(-1, width),
        ],
        axis=0,
    )
    lines = vector.shape[0]
    vector = jnp.pad(vector, ((0, -lines % 64), (0, 0)))
    vector = (vector + to_other_core(vector)).reshape(8, 8, width)
    up_blocks = chip_sum(by_owner(up_mine), to_other_core(by_owner(up_other)), vector)
    up_blocks, down_rows = lax.optimization_barrier((up_blocks, down_rows))
    up_rows = sum_blocks(up_blocks)
    grad_features = conv_back(grad_conv, g_above, g_below, kernel, up, weight)
    up_rows, grad_features = lax.optimization_barrier((up_rows, grad_features))

    piece = owned // space
    block = jnp.concatenate([up_rows[:piece], down_rows], axis=1)
    block = jnp.concatenate([block, up_rows[piece:].reshape(4, 2 * width)], axis=0)
    block = everyone((scale * block).astype(BF16), "space").astype(F32)
    vector = block[:, piece:].reshape(8 * space, width)
    kernel_sum = vector[:49].reshape(7, 7, width)
    gain_sum = vector[49]
    gamma_sum, beta_sum = vector[50:lines].reshape(2, hid)
    block = jnp.concatenate([block[:, :16].reshape(-1, 2 * width), block[:, 16:piece].reshape(-1, 2 * width)], axis=0)
    return (
        grad_features[None],
        kernel_sum,
        gain_sum,
        block[:, :width],
        gamma_sum,
        beta_sum,
        block[:, width:],
    )


def solution(mesh):
    return jax.shard_map(
        body,
        mesh=mesh,
        in_specs=(
            P("dp", "space", None, None),
            P(),
            P(),
            P("dp", None),
            P(),
            P(),
            P("dp", None),
            P("dp", "space", None, None),
            P("dp", "space", None),
            P(),
        ),
        out_specs=(P("dp", "space", None, None), P(), P(), P("dp", None), P(), P(), P("dp", None)),
        check_vma=False,
    )
```

```python
import functools
import math

import jax
import jax.numpy as jnp
from jax import lax
from jax.experimental import pallas as pl
from jax.experimental.pallas import tpu as pltpu
from jax.sharding import PartitionSpec as P

EPS_NORM = 1e-06
F32 = jnp.float32
BF16 = jnp.bfloat16
VMEM_LIMIT = 56 * 1024 * 1024
LANES = 128
PAD = 8
TILE = 8
GROUP = 4
CHUNKS = 3


def params(*semantics):
    return pltpu.CompilerParams(dimension_semantics=semantics, vmem_limit_bytes=VMEM_LIMIT)


def cost(micros):
    return pl.CostEstimate(flops=int(micros * 0.4e9), transcendentals=0, bytes_accessed=0)


def fill_padded(dst, src, first, lanes):
    rows, cols, _ = src.shape
    zeros = jnp.zeros((rows, PAD, LANES), F32)
    dst[first : first + rows, 0:PAD, :] = zeros
    dst[first : first + rows, PAD + cols : PAD + cols + PAD, :] = zeros
    dst[first : first + rows, PAD : PAD + cols, :] = src[:, :, lanes].astype(F32)


def spread_taps(dst, k_ref, flip, lanes):
    for i in range(7):
        for j in range(7):
            tap = k_ref[6 - i, 6 - j : 7 - j, lanes] if flip else k_ref[i, j : j + 1, lanes]
            dst[i * 7 + j] = jnp.broadcast_to(tap, (TILE, LANES))


def taps_group(src, taps, pairs, start, acc):
    rows = sorted({r for r, _, _ in pairs})
    for j in range(7):
        for r in rows:
            todo = [(o, i) for rr, o, i in pairs if rr == r]
            at = [start + TILE * b + PAD - 3 + j for b in range(GROUP)]
            xs = [src[r, p : p + TILE, :] for p in at]
            for o, i in todo:
                tap = taps[i * 7 + j]
                for b in range(GROUP):
                    acc[o][b] = acc[o][b] + xs[b] * tap
    return acc


def own_pairs():
    return [(s, o, s - o + 3) for s in range(4) for o in range(4)]


def halo_pairs():
    above = [(s, o, s - o) for s in range(3) for o in range(4) if 0 <= s - o <= 6]
    below = [(3 + s, o, s + 7 - o) for s in range(3) for o in range(4) if 0 <= s + 7 - o <= 6]
    return above + below


def each_chunk(body):
    def one(n, carry):
        body(n, pl.ds(pl.multiple_of(n * LANES, LANES), LANES))
        return carry

    lax.fori_loop(0, CHUNKS, one, 0)


def tile_rows(start, b):
    return slice(start + TILE * b, start + TILE * (b + 1))


def conv_own_kernel(feat, k_ref, out, xs, taps):
    cols = feat.shape[1]

    def chunk(n, lanes):
        fill_padded(xs, feat, 0, lanes)
        spread_taps(taps, k_ref, False, lanes)
        for start in range(0, cols, GROUP * TILE):
            acc = [[jnp.zeros((TILE, LANES), F32) for _ in range(GROUP)] for _ in range(4)]
            acc = taps_group(xs, taps, own_pairs(), start, acc)
            for o in range(4):
                for b in range(GROUP):
                    out[o, tile_rows(start, b), lanes] = acc[o][b]

    each_chunk(chunk)


def lane_blocks(rows, cols):
    return pl.BlockSpec((rows, cols, CHUNKS * LANES), lambda c: (0, 0, c))


def whole_block(*shape):
    return pl.BlockSpec(shape, lambda c: (0,) * len(shape))


def conv_own(feat, kernel):
    rows, cols, width = feat.shape
    return pl.pallas_call(
        conv_own_kernel,
        grid=(pl.cdiv(width, CHUNKS * LANES),),
        in_specs=[lane_blocks(rows, cols), lane_blocks(7, 7)],
        out_specs=lane_blocks(rows, cols),
        out_shape=jax.ShapeDtypeStruct((rows, cols, width), F32),
        scratch_shapes=[
            pltpu.VMEM((rows, cols + 2 * PAD, LANES), F32),
            pltpu.VMEM((49, TILE, LANES), F32),
        ],
        compiler_params=params("arbitrary"),
        cost_estimate=cost(5),
        name="conv_own",
    )(feat, kernel)


def conv_norm_kernel(width, steps, part, above, below, k_ref, gain, normed, xhat, rstd, xs, taps, conv):
    c = pl.program_id(0)
    cols = part.shape[1]

    def chunk(n, lanes):
        fill_padded(xs, above, 0, lanes)
        fill_padded(xs, below, 3, lanes)
        spread_taps(taps, k_ref, False, lanes)
        for start in range(0, cols, GROUP * TILE):
            acc = [[part[o, tile_rows(start, b), lanes] for b in range(GROUP)] for o in range(4)]
            acc = taps_group(xs, taps, halo_pairs(), start, acc)
            for o in range(4):
                for b in range(GROUP):
                    conv[c * CHUNKS + n, tile_rows(o * cols + start, b), :] = acc[o][b]

    each_chunk(chunk)

    @pl.when(c == steps - 1)
    def _():
        chunks = pl.cdiv(width, LANES)
        last = width - (chunks - 1) * LANES
        block = 64

        def one(t, carry):
            at = pl.multiple_of(t * block, block)
            parts = [conv[n, pl.ds(at, block), :] for n in range(chunks)]
            lane = lax.broadcasted_iota(jnp.int32, (block, LANES), 1)
            inside = lane < last
            parts[-1] = jnp.where(inside, parts[-1], 0.0)
            mean = jnp.sum(sum(parts[1:], parts[0]), axis=-1, keepdims=True) / width
            centred = [p - mean for p in parts]
            centred[-1] = jnp.where(inside, centred[-1], 0.0)
            squares = [p * p for p in centred]
            var = jnp.sum(sum(squares[1:], squares[0]), axis=-1, keepdims=True) / width
            scale = lax.rsqrt(var + EPS_NORM)
            rstd[pl.ds(at, block), :] = jnp.broadcast_to(scale, (block, LANES))
            for n in range(chunks):
                w = min(LANES, width - n * LANES)
                hat = centred[n] * scale
                g = gain[:, n * LANES : n * LANES + w]
                xhat[pl.ds(at, block), n * LANES : n * LANES + w] = hat[:, :w]
                normed[pl.ds(at, block), n * LANES : n * LANES + w] = (hat[:, :w] * g).astype(BF16)
            return carry

        lax.fori_loop(0, (4 * cols) // block, one, 0)


def conv_norm(part, above, below, kernel, gain):
    rows, cols, width = part.shape
    steps = pl.cdiv(width, CHUNKS * LANES)
    pixels = rows * cols
    return pl.pallas_call(
        functools.partial(conv_norm_kernel, width, steps),
        grid=(steps,),
        in_specs=[
            lane_blocks(rows, cols),
            lane_blocks(3, cols),
            lane_blocks(3, cols),
            lane_blocks(7, 7),
            whole_block(1, width),
        ],
        out_specs=[whole_block(pixels, width), whole_block(pixels, width), whole_block(pixels, LANES)],
        out_shape=[
            jax.ShapeDtypeStruct((pixels, width), BF16),
            jax.ShapeDtypeStruct((pixels, width), F32),
            jax.ShapeDtypeStruct((pixels, LANES), F32),
        ],
        scratch_shapes=[
            pltpu.VMEM((6, cols + 2 * PAD, LANES), F32),
            pltpu.VMEM((49, TILE, LANES), F32),
            pltpu.VMEM((steps * CHUNKS, pixels, LANES), F32),
        ],
        compiler_params=params("arbitrary"),
        cost_estimate=cost(7),
        name="conv_norm",
    )(part, above, below, kernel, gain.reshape(1, width))


def with_rows(h, mine, other, step):
    pl.when(h < 2)(lambda: step(mine))
    pl.when(h >= 2)(lambda: step(other))


def half_rows(block, width):
    mine = pl.BlockSpec((block, width), lambda h: (jnp.minimum(h, 1), 0))
    other = pl.BlockSpec((block, width), lambda h: (jnp.maximum(h - 2, 0), 0))
    return mine, other


def up_kernel(normed, w_mine, w_other, act_ref, slope_ref, sums):
    def step(w):
        nt = (((1,), (1,)), ((), ()))
        hidden = lax.dot_general(normed[...], w[...], nt, preferred_element_type=F32)
        cdf = 0.5 * (1.0 + lax.erf(hidden * (2.0**-0.5)))
        act = hidden * cdf
        slope_ref[0] = cdf + hidden * (jnp.exp(hidden * hidden * -0.5) * (1.0 / math.sqrt(2.0 * math.pi)))
        act_ref[0] = act
        sums[0] = jnp.sum((act * act).reshape(-1, 8, act.shape[1]), axis=0)

    with_rows(pl.program_id(0), w_mine, w_other, step)


def up_project(normed, w_up):
    pixels, width = normed.shape
    block = w_up[0].shape[0] // 2
    cols = pl.BlockSpec((1, pixels, block), lambda h: (h, 0, 0))
    big = jax.ShapeDtypeStruct((4, pixels, block), F32)
    return pl.pallas_call(
        up_kernel,
        grid=(4,),
        in_specs=[whole_block(pixels, width), *half_rows(block, width)],
        out_specs=[cols, cols, pl.BlockSpec((1, 8, block), lambda h: (h, 0, 0))],
        out_shape=[big, big, jax.ShapeDtypeStruct((4, 8, block), F32)],
        compiler_params=params("arbitrary"),
        cost_estimate=cost(9),
        name="up_project",
    )(normed, *w_up)


def mixed_kernel(weighted, w_mine, w_other, act_ref, sq, gm_ref, sums, gm_sum):
    def step(w):
        nt = (((1,), (1,)), ((), ()))
        gm = lax.dot_general(weighted[...], w[...], nt, preferred_element_type=F32)
        gm_ref[0] = gm
        act = act_ref[0]
        sums[0, 0:1, :] = jnp.sum(sq[0], axis=0, keepdims=True)
        sums[0, 1:2, :] = jnp.sum(gm * act, axis=0, keepdims=True)
        gm_sum[0] = jnp.sum(gm, axis=0, keepdims=True)

    with_rows(pl.program_id(0), w_mine, w_other, step)


def mixed_grad(weighted, w_down, act, sq):
    pixels, width = weighted.shape
    block = w_down[0].shape[0] // 2
    cols = pl.BlockSpec((1, pixels, block), lambda h: (h, 0, 0))
    return pl.pallas_call(
        mixed_kernel,
        grid=(4,),
        in_specs=[
            whole_block(pixels, width),
            *half_rows(block, width),
            cols,
            pl.BlockSpec((1, 8, block), lambda h: (h, 0, 0)),
        ],
        out_specs=[
            cols,
            pl.BlockSpec((1, 2, block), lambda h: (h, 0, 0)),
            pl.BlockSpec((1, 1, block), lambda h: (h, 0, 0)),
        ],
        out_shape=[
            jax.ShapeDtypeStruct((4, pixels, block), F32),
            jax.ShapeDtypeStruct((4, 2, block), F32),
            jax.ShapeDtypeStruct((4, 1, block), F32),
        ],
        compiler_params=params("arbitrary"),
        cost_estimate=cost(8),
        name="mixed_grad",
    )(weighted, *w_down, act, sq)


def ratio_of(sq, dot, gamma):
    energy = jnp.sqrt(sq)
    hid = energy.shape[0] * energy.shape[1]
    total = lambda x: jnp.sum(jnp.sum(x, axis=1, keepdims=True), axis=0, keepdims=True)
    mean = total(energy) / hid + EPS_NORM
    grad_ratio = gamma * dot
    shared = total(grad_ratio * energy) / (mean * mean) / hid
    return energy / mean, (grad_ratio / mean - shared) / energy


def outer(left, right):
    return lax.dot_general(left, right, (((0,), (0,)), ((), ())), preferred_element_type=F32).astype(BF16)


def mixed_of(a, gamma, ratio, beta):
    return (gamma * a * ratio + beta + a).astype(BF16)


def down_other_kernel(act, weighted, sums, local, gm_sum, gamma, beta, other, ratio, twice, parts):
    h = pl.program_id(0)

    @pl.when(h == 0)
    def _():
        crop = jnp.sum(sums[...], axis=0)
        sq = jnp.concatenate([crop[n, 0:1] for n in range(4)], axis=0)
        dot = jnp.concatenate([crop[n, 1:2] for n in range(4)], axis=0)
        r, t = ratio_of(sq, dot, gamma[...])
        ratio[...] = r
        twice[...] = t
        for n in range(4):
            parts[0, n : n + 1, :] = local[n, 1:2] * r[n : n + 1]
            parts[1, n : n + 1, :] = gm_sum[n]

    row = pl.ds(h + 2, 1)
    other[...] = outer(mixed_of(act[0], gamma[row, :], ratio[row, :], beta[row, :]), weighted[...])


def down_other(act, weighted, sums, local, gm_sum, gamma, beta):
    _, pixels, block = act.shape
    width = weighted.shape[1]
    vec = jax.ShapeDtypeStruct((4, block), F32)
    return pl.pallas_call(
        down_other_kernel,
        grid=(2,),
        in_specs=[
            pl.BlockSpec((1, pixels, block), lambda h: (h + 2, 0, 0)),
            whole_block(pixels, width),
            whole_block(*sums.shape),
            whole_block(*local.shape),
            whole_block(*gm_sum.shape),
            whole_block(4, block),
            whole_block(4, block),
        ],
        out_specs=[
            pl.BlockSpec((block, width), lambda h: (h, 0)),
            whole_block(4, block),
            whole_block(4, block),
            whole_block(2, 4, block),
        ],
        out_shape=[
            jax.ShapeDtypeStruct((2 * block, width), BF16),
            vec,
            vec,
            jax.ShapeDtypeStruct((2, 4, block), F32),
        ],
        compiler_params=params("arbitrary"),
        cost_estimate=cost(4),
        name="down_other",
    )(act, weighted, sums, local, gm_sum, gamma, beta)


def down_mine_kernel(act, weighted, ratio, gamma, beta, mine):
    row = pl.ds(pl.program_id(0), 1)
    mine[...] = outer(mixed_of(act[0], gamma[row, :], ratio[row, :], beta[row, :]), weighted[...])


def down_mine(act, weighted, ratio, gamma, beta):
    _, pixels, block = act.shape
    width = weighted.shape[1]
    return pl.pallas_call(
        down_mine_kernel,
        grid=(2,),
        in_specs=[
            pl.BlockSpec((1, pixels, block), lambda h: (h, 0, 0)),
            whole_block(pixels, width),
            whole_block(4, block),
            whole_block(4, block),
            whole_block(4, block),
        ],
        out_specs=pl.BlockSpec((block, width), lambda h: (h, 0)),
        out_shape=jax.ShapeDtypeStruct((2 * block, width), BF16),
        compiler_params=params("arbitrary"),
        cost_estimate=cost(4),
        name="down_mine",
    )(act, weighted, ratio, gamma, beta)


def hidden_kernel(
    act, slope, gm, w_mine, w_other, normed, ratio, twice, gamma, gain, xhat, rstd,
    mine, other, grad_conv, first, last, gain_part, total,
):
    h = pl.program_id(0)
    row = pl.ds(h, 1)
    grad_act = gm[0] * (gamma[row, :] * ratio[row, :] + 1.0) + act[0] * twice[row, :]
    grad_hidden = (grad_act * slope[0]).astype(BF16)
    term = outer(grad_hidden, normed[...])

    @pl.when(h == 0)
    def _():
        total[...] = jnp.dot(grad_hidden, w_mine[...], preferred_element_type=F32)
        mine[...] = term

    @pl.when(h == 1)
    def _():
        total[...] += jnp.dot(grad_hidden, w_mine[...], preferred_element_type=F32)
        mine[...] = term

    @pl.when(h >= 2)
    def _():
        total[...] += jnp.dot(grad_hidden, w_other[...], preferred_element_type=F32)
        other[...] = term

    @pl.when(h == 3)
    def _():
        pixels, width = total.shape
        block = 64

        def one(t, carry):
            at = pl.ds(pl.multiple_of(t * block, block), block)
            g = total[at, :]
            hat = xhat[at, :]
            carry = carry + jnp.sum((g * hat).reshape(block // 8, 8, width), axis=0)
            g = g * gain[...]
            mean_g = jnp.sum(g, axis=-1, keepdims=True) / width
            mean_gh = jnp.sum(g * hat, axis=-1, keepdims=True) / width
            out = rstd[at, 0:1] * (g - mean_g - hat * mean_gh)
            grad_conv[at, :] = out

            @pl.when(t * block < first.shape[0])
            def _():
                first[at, :] = out.astype(BF16)

            @pl.when(t * block >= pixels - last.shape[0])
            def _():
                last[pl.ds(pl.multiple_of(t * block - (pixels - last.shape[0]), block), block), :] = out.astype(BF16)

            return carry

        gain_part[...] = lax.fori_loop(0, pixels // block, one, jnp.zeros((8, width), F32))


def hidden_grad(act, slope, gm, w_up, normed, ratio, twice, gamma, gain, xhat, rstd, edge):
    _, pixels, block = act.shape
    width = normed.shape[1]
    cols = pl.BlockSpec((1, pixels, block), lambda h: (h, 0, 0))
    vec = whole_block(4, block)
    mine, other = half_rows(block, width)
    term = jax.ShapeDtypeStruct((2 * block, width), BF16)
    return pl.pallas_call(
        hidden_kernel,
        grid=(4,),
        in_specs=[
            cols, cols, cols, mine, other, whole_block(pixels, width), vec, vec, vec,
            whole_block(1, width), whole_block(pixels, width), whole_block(pixels, LANES),
        ],
        out_specs=[
            mine, other, whole_block(pixels, width), whole_block(edge, width), whole_block(edge, width),
            whole_block(8, width),
        ],
        out_shape=[
            term,
            term,
            jax.ShapeDtypeStruct((pixels, width), F32),
            jax.ShapeDtypeStruct((edge, width), BF16),
            jax.ShapeDtypeStruct((edge, width), BF16),
            jax.ShapeDtypeStruct((8, width), F32),
        ],
        scratch_shapes=[pltpu.VMEM((pixels, width), F32)],
        compiler_params=params("arbitrary"),
        cost_estimate=cost(14),
        name="hidden_grad",
    )(act, slope, gm, *w_up, normed, ratio, twice, gamma, gain.reshape(1, width), xhat, rstd)


def taps_grad_kernel(feat, above, below, grad, ktaps, xs, gs):
    cols = feat.shape[1]

    def chunk(n, lanes):
        fill_padded(xs, above, 0, lanes)
        fill_padded(xs, feat, 3, lanes)
        fill_padded(xs, below, 7, lanes)
        gs[...] = grad[:, :, lanes]
        for j in range(7):
            sums = [jnp.zeros((TILE, LANES), F32) for _ in range(7)]
            for start in range(0, cols, TILE):
                g = [gs[o, start : start + TILE, :] for o in range(4)]
                for r in range(10):
                    x = xs[r, PAD - 3 + j + start : PAD - 3 + j + start + TILE, :]
                    for o in range(4):
                        if 0 <= r - o <= 6:
                            sums[r - o] = sums[r - o] + x * g[o]
            for i in range(7):
                ktaps[i, j : j + 1, lanes] = jnp.sum(sums[i], axis=0, keepdims=True)

    each_chunk(chunk)


def taps_grad(feat, above, below, grad):
    rows, cols, width = feat.shape
    return pl.pallas_call(
        taps_grad_kernel,
        grid=(pl.cdiv(width, CHUNKS * LANES),),
        in_specs=[
            lane_blocks(rows, cols),
            lane_blocks(3, cols),
            lane_blocks(3, cols),
            lane_blocks(rows, cols),
        ],
        out_specs=lane_blocks(7, 7),
        out_shape=jax.ShapeDtypeStruct((7, 7, width), F32),
        scratch_shapes=[
            pltpu.VMEM((rows + 6, cols + 2 * PAD, LANES), F32),
            pltpu.VMEM((rows, cols, LANES), F32),
        ],
        compiler_params=params("arbitrary"),
        cost_estimate=cost(1),
        name="taps_grad",
    )(feat, above, below, grad)


def all_pairs():
    return [(r, o, r - o) for r in range(10) for o in range(4) if 0 <= r - o <= 6]


def conv_back_kernel(grad, above, below, k_ref, upstream, weight, out, xs, taps):
    cols = grad.shape[1]

    def chunk(n, lanes):
        fill_padded(xs, above, 0, lanes)
        fill_padded(xs, grad, 3, lanes)
        fill_padded(xs, below, 7, lanes)
        spread_taps(taps, k_ref, True, lanes)
        for start in range(0, cols, GROUP * TILE):
            acc = [[None] * GROUP for _ in range(4)]
            for o in range(4):
                for b in range(GROUP):
                    at = tile_rows(start, b)
                    acc[o][b] = upstream[o, at, lanes].astype(F32) * weight[o, at, :]
            acc = taps_group(xs, taps, all_pairs(), start, acc)
            for o in range(4):
                for b in range(GROUP):
                    out[o, tile_rows(start, b), lanes] = acc[o][b]

    each_chunk(chunk)


def conv_back(grad, above, below, kernel, upstream, weight):
    rows, cols, width = grad.shape
    return pl.pallas_call(
        conv_back_kernel,
        grid=(pl.cdiv(width, CHUNKS * LANES),),
        in_specs=[
            lane_blocks(rows, cols),
            lane_blocks(3, cols),
            lane_blocks(3, cols),
            lane_blocks(7, 7),
            lane_blocks(rows, cols),
            whole_block(rows, cols, LANES),
        ],
        out_specs=lane_blocks(rows, cols),
        out_shape=jax.ShapeDtypeStruct((rows, cols, width), F32),
        scratch_shapes=[
            pltpu.VMEM((rows + 6, cols + 2 * PAD, LANES), F32),
            pltpu.VMEM((49, TILE, LANES), F32),
        ],
        compiler_params=params("arbitrary"),
        cost_estimate=cost(60),
        name="conv_back",
    )(grad, above, below, kernel, upstream, weight)


def chip_kernel(mine, other, vector, edge, out):
    width = mine.shape[2]
    for q in range(mine.shape[0]):
        high = (mine[q, :128, :].astype(F32) + other[q, :128, :].astype(F32)).astype(BF16)
        low = mine[q, 128:, :].astype(F32) + other[q, 128:, :].astype(F32)
        for s in range(8):
            out[q * 8 + s, :16, :width] = high[16 * s : 16 * (s + 1), :]
            rest = low[6 * s : 6 * (s + 1), :]
            if vector is not None:
                rest = jnp.concatenate([rest, vector[s]], axis=0)
                out[q * 8 + s, :16, width:] = edge[s, :16, :].astype(BF16)
                out[q * 8 + s, 16:, width:] = edge[s, 16:, :].astype(BF16)
            out[q * 8 + s, 16:, :width] = rest.astype(BF16)


def chip_sum(mine, other, vector=None, edge=None):
    owners, owned, width = mine.shape
    rows = pl.BlockSpec((owners // 2, owned, width), lambda q: (q, 0, 0))
    if vector is None:
        given, piece, lanes = [], owned // 8, width
        kernel = lambda mine, other, out: chip_kernel(mine, other, None, None, out)
    else:
        given, piece, lanes = [vector, edge], owned // 8 + 2, width + edge.shape[2]
        kernel = chip_kernel
    return pl.pallas_call(
        kernel,
        grid=(2,),
        in_specs=[rows, rows] + [pl.BlockSpec((8,) + v.shape[1:], lambda q: (q, 0, 0)) for v in given],
        out_specs=pl.BlockSpec((owners * 4, piece, lanes), lambda q: (q, 0, 0)),
        out_shape=jax.ShapeDtypeStruct((owners * 8, piece, lanes), BF16),
        compiler_params=params("arbitrary"),
        cost_estimate=cost(0.3),
        name="chip_sum",
    )(mine, other, *given)


BOTH = ("dp", "space")


def device(y, z, c, x, low):
    return (y * 8 + z * 2 + c) * 8 + x * 2 + low


OWNERS = [
    [device(y, z, c, x, low ^ y) for y in range(2) for z in range(4)]
    for c in range(2)
    for x in range(4)
    for low in range(2)
]
CORES = [
    [device(y, z, c, x, low) for y in range(2) for z in range(4) for x in range(4) for low in range(2)]
    for c in range(2)
]


def moved(move):
    return [
        (device(y, z, c, x, low), device(*move(y, z, c, x, low)))
        for y in range(2)
        for z in range(4)
        for c in range(2)
        for x in range(4)
        for low in range(2)
    ]


def to_other_core(value):
    return lax.ppermute(value, BOTH, moved(lambda y, z, c, x, low: (y, z, 1 - c, x, low)))


def to_other_half(value, cross):
    return lax.ppermute(value, BOTH, moved(lambda y, z, c, x, low: (1 - y, z, 1 - c if cross else c, x, low)))


def gather_mine(shard):
    return lax.all_to_all(jnp.broadcast_to(shard, (8,) + shard.shape), BOTH, 0, 0, axis_index_groups=OWNERS)


def with_other(mine):
    other = to_other_core(mine)
    return mine.reshape(-1, mine.shape[2]), other.reshape(-1, mine.shape[2])


def local_order(vector, owned):
    first, second = core_halves(vector.reshape(8, 2, owned), 1)
    return jnp.concatenate([first.reshape(2, -1), second.reshape(2, -1)], axis=0)


def core_halves(value, axis):
    c = lax.axis_index("dp") % 2
    low, high = lax.index_in_dim(value, 0, axis, False), lax.index_in_dim(value, 1, axis, False)
    return jnp.where(c == 0, low, high), jnp.where(c == 0, high, low)


def global_order(blocks, owned):
    n = blocks.shape[0]
    low, high = core_halves(blocks.reshape(n, 2, 8, owned), 1)
    return jnp.stack([low, high], axis=2).reshape(n, -1)


def sum_blocks(blocks):
    return jnp.sum(lax.all_to_all(blocks, BOTH, 0, 0, axis_index_groups=CORES).astype(F32), axis=0)


def exchange(value, axis):
    return lax.all_to_all(value, axis, 0, 0)


def everyone(value, axis):
    return exchange(jnp.broadcast_to(value, (lax.axis_size(axis),) + value.shape), axis)


def shift(rows, pairs):
    flat = rows.reshape(-1, 16, rows.shape[-1])
    return lax.ppermute(flat, "space", pairs).reshape(rows.shape)


def body(
    features, kernel, norm_gain, w_up, grn_gamma, grn_beta, w_down, upstream, labels, class_weight
):
    crops, rows, cols, width = features.shape
    feat, up = features[0], upstream[0]
    space = lax.axis_size("space")
    dp = lax.axis_size("dp")
    owned = w_up.shape[0]
    hid = owned * dp
    pixels = rows * cols
    rising = [(i, i + 1) for i in range(space - 1)]
    falling = [(j, i) for i, j in rising]
    above = shift(feat[rows - 3 :], rising)
    below = shift(feat[:3], falling)
    part = conv_own(feat, kernel)
    w_up_mine = gather_mine(w_up)
    w_up_mine, w_down, part, above, below = lax.optimization_barrier((w_up_mine, w_down, part, above, below))
    w_down_mine = gather_mine(w_down)
    gamma, beta = local_order(grn_gamma, owned), local_order(grn_beta, owned)

    classes = jnp.arange(class_weight.shape[0], dtype=jnp.int32)
    pixel_weight = jnp.sum(jnp.where(labels[0][..., None] == classes, class_weight, 0.0), axis=-1)
    weight = jnp.broadcast_to(pixel_weight[..., None], (rows, cols, LANES))
    weighted = (up.astype(F32) * pixel_weight[..., None]).astype(BF16).reshape(pixels, width)

    normed, xhat, rstd = conv_norm(part, above, below, kernel, norm_gain)
    w_up_all = with_other(w_up_mine)
    act, slope, sq = up_project(normed, w_up_all)
    w_down_mine, sq = lax.optimization_barrier((w_down_mine, sq))
    w_down_all = with_other(w_down_mine)
    gm, local, gm_sum = mixed_grad(weighted, w_down_all, act, sq)
    sums = everyone(local, "space")
    down_other_term, ratio, twice, parts = down_other(act, weighted, sums, local, gm_sum, gamma, beta)
    by_owner = lambda rows: rows.reshape(8, owned, width)
    came = to_other_core(by_owner(down_other_term))
    down_blocks = chip_sum(by_owner(down_mine(act, weighted, ratio, gamma, beta)), came)
    ratio, down_blocks = lax.optimization_barrier((ratio, down_blocks))
    down_rows = sum_blocks(down_blocks)
    up_mine, up_other, grad_conv, g_first, g_last, gain_part = hidden_grad(
        act, slope, gm, w_up_all, normed, ratio, twice, gamma, norm_gain, xhat, rstd, 3 * cols
    )
    grad_conv = grad_conv.reshape(rows, cols, width)
    g_above = shift(g_last.reshape(3, cols, width), rising)
    g_below = shift(g_first.reshape(3, cols, width), falling)
    kernel_part = taps_grad(feat, above, below, grad_conv)

    scale = 1.0 / math.sqrt(dp * space * pixels)
    vector = jnp.concatenate(
        [
            kernel_part.reshape(49, width),
            jnp.sum(gain_part, axis=0, keepdims=True),
            global_order(parts, owned).reshape(-1, width),
        ],
        axis=0,
    )
    lines = vector.shape[0]
    vector = jnp.pad(vector, ((0, -lines % 64), (0, 0))).reshape(16, 4, width)
    piece = owned // space
    lanes = 2 * width // piece
    edge = jnp.pad(vector[:, 2:].reshape(16, piece, lanes), ((0, 0), (0, 2), (0, 0)))
    up_blocks = chip_sum(by_owner(up_mine), to_other_core(by_owner(up_other)), vector[:, :2], edge)
    up_blocks, down_rows = lax.optimization_barrier((up_blocks, down_rows))
    up_rows = sum_blocks(up_blocks)
    grad_features = conv_back(grad_conv, g_above, g_below, kernel, up, weight)
    up_rows, grad_features = lax.optimization_barrier((up_rows, grad_features))

    vector = jnp.concatenate([up_rows[piece:, :width], up_rows[:piece, width:].reshape(2, width)], axis=0)
    here = vector + to_other_core(vector)
    there = to_other_half(vector, False) + to_other_half(vector, True)
    first = lax.axis_index("dp") < 8
    vector = jnp.concatenate([jnp.where(first, here, there), jnp.where(first, there, here)], axis=0)
    block = jnp.concatenate([up_rows[:piece, :width], down_rows], axis=1)
    block = jnp.concatenate([block, vector.reshape(4, 2 * width)], axis=0)
    block = everyone((scale * block).astype(BF16), "space").astype(F32)
    vector = jnp.transpose(block[:, piece:].reshape(space, 2, 4, width), (1, 0, 2, 3)).reshape(8 * space, width)
    kernel_sum = vector[:49].reshape(7, 7, width)
    gain_sum = vector[49]
    gamma_sum, beta_sum = vector[50:lines].reshape(2, hid)
    block = jnp.concatenate([block[:, :16].reshape(-1, 2 * width), block[:, 16:piece].reshape(-1, 2 * width)], axis=0)
    return (
        grad_features[None],
        kernel_sum,
        gain_sum,
        block[:, :width],
        gamma_sum,
        beta_sum,
        block[:, width:],
    )


def solution(mesh):
    return jax.shard_map(
        body,
        mesh=mesh,
        in_specs=(
            P("dp", "space", None, None),
            P(),
            P(),
            P("dp", None),
            P(),
            P(),
            P("dp", None),
            P("dp", "space", None, None),
            P("dp", "space", None),
            P(),
        ),
        out_specs=(P("dp", "space", None, None), P(), P(), P("dp", None), P(), P(), P("dp", None)),
        check_vma=False,
    )
```

```python
import functools
import math

import jax
import jax.numpy as jnp
from jax import lax
from jax.experimental import pallas as pl
from jax.experimental.pallas import tpu as pltpu
from jax.sharding import PartitionSpec as P

EPS_NORM = 1e-06
F32 = jnp.float32
BF16 = jnp.bfloat16
VMEM_LIMIT = 56 * 1024 * 1024
LANES = 128
PAD = 8
TILE = 8
GROUP = 4
CHUNKS = 3


def params(*semantics):
    return pltpu.CompilerParams(dimension_semantics=semantics, vmem_limit_bytes=VMEM_LIMIT)


def cost(micros):
    return pl.CostEstimate(flops=int(micros * 0.4e9), transcendentals=0, bytes_accessed=0)


def fill_padded(dst, src, first, lanes):
    rows, cols, _ = src.shape
    zeros = jnp.zeros((rows, PAD, LANES), F32)
    dst[first : first + rows, 0:PAD, :] = zeros
    dst[first : first + rows, PAD + cols : PAD + cols + PAD, :] = zeros
    dst[first : first + rows, PAD : PAD + cols, :] = src[:, :, lanes].astype(F32)


def spread_taps(dst, k_ref, flip, lanes):
    for i in range(7):
        for j in range(7):
            tap = k_ref[6 - i, 6 - j : 7 - j, lanes] if flip else k_ref[i, j : j + 1, lanes]
            dst[i * 7 + j] = jnp.broadcast_to(tap, (TILE, LANES))


def taps_group(src, taps, pairs, start, acc):
    rows = sorted({r for r, _, _ in pairs})
    for j in range(7):
        for r in rows:
            todo = [(o, i) for rr, o, i in pairs if rr == r]
            at = [start + TILE * b + PAD - 3 + j for b in range(GROUP)]
            xs = [src[r, p : p + TILE, :] for p in at]
            for o, i in todo:
                tap = taps[i * 7 + j]
                for b in range(GROUP):
                    acc[o][b] = acc[o][b] + xs[b] * tap
    return acc


def own_pairs():
    return [(s, o, s - o + 3) for s in range(4) for o in range(4)]


def halo_pairs():
    above = [(s, o, s - o) for s in range(3) for o in range(4) if 0 <= s - o <= 6]
    below = [(3 + s, o, s + 7 - o) for s in range(3) for o in range(4) if 0 <= s + 7 - o <= 6]
    return above + below


def each_chunk(body):
    def one(n, carry):
        body(n, pl.ds(pl.multiple_of(n * LANES, LANES), LANES))
        return carry

    lax.fori_loop(0, CHUNKS, one, 0)


def tile_rows(start, b):
    return slice(start + TILE * b, start + TILE * (b + 1))


def conv_own_kernel(feat, k_ref, out, xs, taps):
    cols = feat.shape[1]

    def chunk(n, lanes):
        fill_padded(xs, feat, 0, lanes)
        spread_taps(taps, k_ref, False, lanes)
        for start in range(0, cols, GROUP * TILE):
            acc = [[jnp.zeros((TILE, LANES), F32) for _ in range(GROUP)] for _ in range(4)]
            acc = taps_group(xs, taps, own_pairs(), start, acc)
            for o in range(4):
                for b in range(GROUP):
                    out[o, tile_rows(start, b), lanes] = acc[o][b]

    each_chunk(chunk)


def lane_blocks(rows, cols):
    return pl.BlockSpec((rows, cols, CHUNKS * LANES), lambda c: (0, 0, c))


def whole_block(*shape):
    return pl.BlockSpec(shape, lambda c: (0,) * len(shape))


def conv_own(feat, kernel):
    rows, cols, width = feat.shape
    return pl.pallas_call(
        conv_own_kernel,
        grid=(pl.cdiv(width, CHUNKS * LANES),),
        in_specs=[lane_blocks(rows, cols), lane_blocks(7, 7)],
        out_specs=lane_blocks(rows, cols),
        out_shape=jax.ShapeDtypeStruct((rows, cols, width), F32),
        scratch_shapes=[
            pltpu.VMEM((rows, cols + 2 * PAD, LANES), F32),
            pltpu.VMEM((49, TILE, LANES), F32),
        ],
        compiler_params=params("arbitrary"),
        cost_estimate=cost(5),
        name="conv_own",
    )(feat, kernel)


def conv_norm_kernel(width, steps, part, above, below, k_ref, gain, normed, xhat, rstd, xs, taps, conv):
    c = pl.program_id(0)
    cols = part.shape[1]

    def chunk(n, lanes):
        fill_padded(xs, above, 0, lanes)
        fill_padded(xs, below, 3, lanes)
        spread_taps(taps, k_ref, False, lanes)
        for start in range(0, cols, GROUP * TILE):
            acc = [[part[o, tile_rows(start, b), lanes] for b in range(GROUP)] for o in range(4)]
            acc = taps_group(xs, taps, halo_pairs(), start, acc)
            for o in range(4):
                for b in range(GROUP):
                    conv[c * CHUNKS + n, tile_rows(o * cols + start, b), :] = acc[o][b]

    each_chunk(chunk)

    @pl.when(c == steps - 1)
    def _():
        chunks = pl.cdiv(width, LANES)
        last = width - (chunks - 1) * LANES
        block = 64

        def one(t, carry):
            at = pl.multiple_of(t * block, block)
            parts = [conv[n, pl.ds(at, block), :] for n in range(chunks)]
            lane = lax.broadcasted_iota(jnp.int32, (block, LANES), 1)
            inside = lane < last
            parts[-1] = jnp.where(inside, parts[-1], 0.0)
            mean = jnp.sum(sum(parts[1:], parts[0]), axis=-1, keepdims=True) / width
            centred = [p - mean for p in parts]
            centred[-1] = jnp.where(inside, centred[-1], 0.0)
            squares = [p * p for p in centred]
            var = jnp.sum(sum(squares[1:], squares[0]), axis=-1, keepdims=True) / width
            scale = lax.rsqrt(var + EPS_NORM)
            rstd[pl.ds(at, block), :] = jnp.broadcast_to(scale, (block, LANES))
            for n in range(chunks):
                w = min(LANES, width - n * LANES)
                hat = centred[n] * scale
                g = gain[:, n * LANES : n * LANES + w]
                xhat[pl.ds(at, block), n * LANES : n * LANES + w] = hat[:, :w]
                normed[pl.ds(at, block), n * LANES : n * LANES + w] = (hat[:, :w] * g).astype(BF16)
            return carry

        lax.fori_loop(0, (4 * cols) // block, one, 0)


def conv_norm(part, above, below, kernel, gain):
    rows, cols, width = part.shape
    steps = pl.cdiv(width, CHUNKS * LANES)
    pixels = rows * cols
    return pl.pallas_call(
        functools.partial(conv_norm_kernel, width, steps),
        grid=(steps,),
        in_specs=[
            lane_blocks(rows, cols),
            lane_blocks(3, cols),
            lane_blocks(3, cols),
            lane_blocks(7, 7),
            whole_block(1, width),
        ],
        out_specs=[whole_block(pixels, width), whole_block(pixels, width), whole_block(pixels, LANES)],
        out_shape=[
            jax.ShapeDtypeStruct((pixels, width), BF16),
            jax.ShapeDtypeStruct((pixels, width), F32),
            jax.ShapeDtypeStruct((pixels, LANES), F32),
        ],
        scratch_shapes=[
            pltpu.VMEM((6, cols + 2 * PAD, LANES), F32),
            pltpu.VMEM((49, TILE, LANES), F32),
            pltpu.VMEM((steps * CHUNKS, pixels, LANES), F32),
        ],
        compiler_params=params("arbitrary"),
        cost_estimate=cost(7),
        name="conv_norm",
    )(part, above, below, kernel, gain.reshape(1, width))


IN_VMEM = pl.BlockSpec(memory_space=pltpu.VMEM)
STAY = pltpu.CompilerParams(vmem_limit_bytes=12 * 1024 * 1024)


def with_rows(h, mine, other, step):
    pl.when(h < 2)(lambda: step(mine))
    pl.when(h >= 2)(lambda: step(other))


def half_rows(block, width):
    mine = pl.BlockSpec((block, width), lambda h: (jnp.minimum(h, 1), 0))
    other = pl.BlockSpec((block, width), lambda h: (jnp.maximum(h - 2, 0), 0))
    return mine, other


def up_kernel(normed, w_mine, w_other, act_ref, slope_ref, sums):
    def step(w):
        nt = (((1,), (1,)), ((), ()))
        hidden = lax.dot_general(normed[...], w[...], nt, preferred_element_type=F32)
        cdf = 0.5 * (1.0 + lax.erf(hidden * (2.0**-0.5)))
        act = hidden * cdf
        slope_ref[0] = cdf + hidden * (jnp.exp(hidden * hidden * -0.5) * (1.0 / math.sqrt(2.0 * math.pi)))
        act_ref[0] = act
        sums[0] = jnp.sum((act * act).reshape(-1, 8, act.shape[1]), axis=0)

    with_rows(pl.program_id(0), w_mine, w_other, step)


def up_project(normed, w_up):
    pixels, width = normed.shape
    block = w_up[0].shape[0] // 2
    cols = pl.BlockSpec((1, pixels, block), lambda h: (h, 0, 0))
    big = jax.ShapeDtypeStruct((4, pixels, block), F32)
    return pl.pallas_call(
        up_kernel,
        grid=(4,),
        in_specs=[whole_block(pixels, width), *half_rows(block, width)],
        out_specs=[cols, cols, pl.BlockSpec((1, 8, block), lambda h: (h, 0, 0))],
        out_shape=[big, big, jax.ShapeDtypeStruct((4, 8, block), F32)],
        compiler_params=params("arbitrary"),
        cost_estimate=cost(9),
        name="up_project",
    )(normed, *w_up)


def mixed_kernel(weighted, w_mine, w_other, act_ref, sq, gm_ref, sums, gm_sum):
    h = pl.program_id(0)

    def step(w):
        nt = (((1,), (1,)), ((), ()))
        gm = lax.dot_general(weighted[...], w[...], nt, preferred_element_type=F32)
        gm_ref[0] = gm
        sums[pl.ds(h, 1), :] = jnp.sum(sq[0], axis=0, keepdims=True)
        sums[pl.ds(h + 4, 1), :] = jnp.sum(gm * act_ref[0], axis=0, keepdims=True)
        gm_sum[pl.ds(h, 1), :] = jnp.sum(gm, axis=0, keepdims=True)

    with_rows(h, w_mine, w_other, step)


def mixed_grad(weighted, w_down, act, sq):
    pixels, width = weighted.shape
    block = w_down[0].shape[0] // 2
    cols = pl.BlockSpec((1, pixels, block), lambda h: (h, 0, 0))
    return pl.pallas_call(
        mixed_kernel,
        grid=(4,),
        in_specs=[
            whole_block(pixels, width),
            *half_rows(block, width),
            cols,
            pl.BlockSpec((1, 8, block), lambda h: (h, 0, 0)),
        ],
        out_specs=[cols, whole_block(8, block), whole_block(4, block)],
        out_shape=[
            jax.ShapeDtypeStruct((4, pixels, block), F32),
            jax.ShapeDtypeStruct((8, block), F32),
            jax.ShapeDtypeStruct((4, block), F32),
        ],
        compiler_params=params("arbitrary"),
        cost_estimate=cost(8),
        name="mixed_grad",
    )(weighted, *w_down, act, sq)


def ratio_of(sq, dot, gamma):
    energy = jnp.sqrt(sq)
    hid = energy.shape[0] * energy.shape[1]
    total = lambda x: jnp.sum(jnp.sum(x, axis=1, keepdims=True), axis=0, keepdims=True)
    mean = total(energy) / hid + EPS_NORM
    grad_ratio = gamma * dot
    shared = total(grad_ratio * energy) / (mean * mean) / hid
    return energy / mean, (grad_ratio / mean - shared) / energy


def store_rows(half, i, value):
    block = half.shape[0] // 2
    half[pl.ds(pl.multiple_of(i * block, block), block), :] = value


def outer(left, right):
    return lax.dot_general(left, right, (((0,), (0,)), ((), ())), preferred_element_type=F32).astype(BF16)


def down_rows_of(half, first, act, weighted, gamma, ratio, beta):
    def one(i, carry):
        row = pl.ds(first + i, 1)
        a = act[first + i]
        mixed = (gamma[row, :] * a * ratio[row, :] + beta[row, :] + a).astype(BF16)
        store_rows(half, i, outer(mixed, weighted[...]))
        return carry

    lax.fori_loop(0, 2, one, 0)


def down_other_kernel(act, weighted, sums, local, gm_sum, gamma, beta, other, ratio, twice, parts):
    crop = jnp.sum(sums[...], axis=0)
    r, t = ratio_of(crop[:4], crop[4:], gamma[...])
    ratio[...] = r
    twice[...] = t
    parts[0] = local[4:, :] * r
    parts[1] = gm_sum[...]
    down_rows_of(other, 2, act, weighted, gamma, ratio, beta)


def down_other(act, weighted, sums, local, gm_sum, gamma, beta):
    _, pixels, block = act.shape
    width = weighted.shape[1]
    vec = jax.ShapeDtypeStruct((4, block), F32)
    return pl.pallas_call(
        down_other_kernel,
        in_specs=[IN_VMEM] * 7,
        out_specs=[IN_VMEM] * 4,
        out_shape=[
            jax.ShapeDtypeStruct((2 * block, width), BF16),
            vec,
            vec,
            jax.ShapeDtypeStruct((2, 4, block), F32),
        ],
        compiler_params=STAY,
        cost_estimate=cost(4),
        name="down_other",
    )(act, weighted, sums, local, gm_sum, gamma, beta)


def down_mine_kernel(act, weighted, ratio, gamma, beta, mine):
    down_rows_of(mine, 0, act, weighted, gamma, ratio, beta)


def down_mine(act, weighted, ratio, gamma, beta):
    _, pixels, block = act.shape
    width = weighted.shape[1]
    return pl.pallas_call(
        down_mine_kernel,
        in_specs=[IN_VMEM] * 5,
        out_specs=IN_VMEM,
        out_shape=jax.ShapeDtypeStruct((2 * block, width), BF16),
        compiler_params=STAY,
        cost_estimate=cost(4),
        name="down_mine",
    )(act, weighted, ratio, gamma, beta)


def hidden_kernel(
    act, slope, gm, w_mine, w_other, normed, ratio, twice, gamma, gain, xhat, rstd,
    mine, other, grad_conv, first, last, gain_part, total,
):
    h = pl.program_id(0)
    row = pl.ds(h, 1)
    grad_act = gm[0] * (gamma[row, :] * ratio[row, :] + 1.0) + act[0] * twice[row, :]
    grad_hidden = (grad_act * slope[0]).astype(BF16)
    term = outer(grad_hidden, normed[...])

    @pl.when(h == 0)
    def _():
        total[...] = jnp.dot(grad_hidden, w_mine[...], preferred_element_type=F32)
        mine[...] = term

    @pl.when(h == 1)
    def _():
        total[...] += jnp.dot(grad_hidden, w_mine[...], preferred_element_type=F32)
        mine[...] = term

    @pl.when(h >= 2)
    def _():
        total[...] += jnp.dot(grad_hidden, w_other[...], preferred_element_type=F32)
        other[...] = term

    @pl.when(h == 3)
    def _():
        pixels, width = total.shape
        block = 64

        def one(t, carry):
            at = pl.ds(pl.multiple_of(t * block, block), block)
            g = total[at, :]
            hat = xhat[at, :]
            carry = carry + jnp.sum((g * hat).reshape(block // 8, 8, width), axis=0)
            g = g * gain[...]
            mean_g = jnp.sum(g, axis=-1, keepdims=True) / width
            mean_gh = jnp.sum(g * hat, axis=-1, keepdims=True) / width
            out = rstd[at, 0:1] * (g - mean_g - hat * mean_gh)
            grad_conv[at, :] = out

            @pl.when(t * block < first.shape[0])
            def _():
                first[at, :] = out.astype(BF16)

            @pl.when(t * block >= pixels - last.shape[0])
            def _():
                last[pl.ds(pl.multiple_of(t * block - (pixels - last.shape[0]), block), block), :] = out.astype(BF16)

            return carry

        gain_part[...] = lax.fori_loop(0, pixels // block, one, jnp.zeros((8, width), F32))


def hidden_grad(act, slope, gm, w_up, normed, ratio, twice, gamma, gain, xhat, rstd, edge):
    _, pixels, block = act.shape
    width = normed.shape[1]
    cols = pl.BlockSpec((1, pixels, block), lambda h: (h, 0, 0))
    vec = whole_block(4, block)
    mine, other = half_rows(block, width)
    term = jax.ShapeDtypeStruct((2 * block, width), BF16)
    return pl.pallas_call(
        hidden_kernel,
        grid=(4,),
        in_specs=[
            cols, cols, cols, mine, other, whole_block(pixels, width), vec, vec, vec,
            whole_block(1, width), whole_block(pixels, width), whole_block(pixels, LANES),
        ],
        out_specs=[
            mine, other, whole_block(pixels, width), whole_block(edge, width), whole_block(edge, width),
            whole_block(8, width),
        ],
        out_shape=[
            term,
            term,
            jax.ShapeDtypeStruct((pixels, width), F32),
            jax.ShapeDtypeStruct((edge, width), BF16),
            jax.ShapeDtypeStruct((edge, width), BF16),
            jax.ShapeDtypeStruct((8, width), F32),
        ],
        scratch_shapes=[pltpu.VMEM((pixels, width), F32)],
        compiler_params=params("arbitrary"),
        cost_estimate=cost(14),
        name="hidden_grad",
    )(act, slope, gm, *w_up, normed, ratio, twice, gamma, gain.reshape(1, width), xhat, rstd)


def taps_grad_kernel(feat, above, below, grad, ktaps, xs, gs):
    cols = feat.shape[1]

    def chunk(n, lanes):
        fill_padded(xs, above, 0, lanes)
        fill_padded(xs, feat, 3, lanes)
        fill_padded(xs, below, 7, lanes)
        gs[...] = grad[:, :, lanes]
        for j in range(7):
            sums = [jnp.zeros((TILE, LANES), F32) for _ in range(7)]
            for start in range(0, cols, TILE):
                g = [gs[o, start : start + TILE, :] for o in range(4)]
                for r in range(10):
                    x = xs[r, PAD - 3 + j + start : PAD - 3 + j + start + TILE, :]
                    for o in range(4):
                        if 0 <= r - o <= 6:
                            sums[r - o] = sums[r - o] + x * g[o]
            for i in range(7):
                ktaps[i, j : j + 1, lanes] = jnp.sum(sums[i], axis=0, keepdims=True)

    each_chunk(chunk)


def taps_grad(feat, above, below, grad):
    rows, cols, width = feat.shape
    return pl.pallas_call(
        taps_grad_kernel,
        grid=(pl.cdiv(width, CHUNKS * LANES),),
        in_specs=[
            lane_blocks(rows, cols),
            lane_blocks(3, cols),
            lane_blocks(3, cols),
            lane_blocks(rows, cols),
        ],
        out_specs=lane_blocks(7, 7),
        out_shape=jax.ShapeDtypeStruct((7, 7, width), F32),
        scratch_shapes=[
            pltpu.VMEM((rows + 6, cols + 2 * PAD, LANES), F32),
            pltpu.VMEM((rows, cols, LANES), F32),
        ],
        compiler_params=params("arbitrary"),
        cost_estimate=cost(1),
        name="taps_grad",
    )(feat, above, below, grad)


def all_pairs():
    return [(r, o, r - o) for r in range(10) for o in range(4) if 0 <= r - o <= 6]


def conv_back_kernel(grad, above, below, k_ref, upstream, weight, out, xs, taps):
    cols = grad.shape[1]

    def chunk(n, lanes):
        fill_padded(xs, above, 0, lanes)
        fill_padded(xs, grad, 3, lanes)
        fill_padded(xs, below, 7, lanes)
        spread_taps(taps, k_ref, True, lanes)
        for start in range(0, cols, GROUP * TILE):
            acc = [[None] * GROUP for _ in range(4)]
            for o in range(4):
                for b in range(GROUP):
                    at = tile_rows(start, b)
                    acc[o][b] = upstream[o, at, lanes].astype(F32) * weight[o, at, :]
            acc = taps_group(xs, taps, all_pairs(), start, acc)
            for o in range(4):
                for b in range(GROUP):
                    out[o, tile_rows(start, b), lanes] = acc[o][b]

    each_chunk(chunk)


def conv_back(grad, above, below, kernel, upstream, weight):
    rows, cols, width = grad.shape
    return pl.pallas_call(
        conv_back_kernel,
        grid=(pl.cdiv(width, CHUNKS * LANES),),
        in_specs=[
            lane_blocks(rows, cols),
            lane_blocks(3, cols),
            lane_blocks(3, cols),
            lane_blocks(7, 7),
            lane_blocks(rows, cols),
            whole_block(rows, cols, LANES),
        ],
        out_specs=lane_blocks(rows, cols),
        out_shape=jax.ShapeDtypeStruct((rows, cols, width), F32),
        scratch_shapes=[
            pltpu.VMEM((rows + 6, cols + 2 * PAD, LANES), F32),
            pltpu.VMEM((49, TILE, LANES), F32),
        ],
        compiler_params=params("arbitrary"),
        cost_estimate=cost(60),
        name="conv_back",
    )(grad, above, below, kernel, upstream, weight)


def chip_kernel(mine, other, vector, edge, out):
    width = mine.shape[2]
    def one(q, carry):
        high = (mine[q, :128, :].astype(F32) + other[q, :128, :].astype(F32)).astype(BF16)
        low = mine[q, 128:, :].astype(F32) + other[q, 128:, :].astype(F32)
        for s in range(8):
            out[q * 8 + s, :16, :width] = high[16 * s : 16 * (s + 1), :]
            rest = low[6 * s : 6 * (s + 1), :]
            if vector is not None:
                at = q // 4 * 8 + s
                rest = jnp.concatenate([rest, vector[at]], axis=0)
                out[q * 8 + s, :16, width:] = edge[at, :16, :].astype(BF16)
                out[q * 8 + s, 16:, width:] = edge[at, 16:, :].astype(BF16)
            out[q * 8 + s, 16:, :width] = rest.astype(BF16)
        return carry

    lax.fori_loop(0, mine.shape[0], one, 0)


def chip_sum(mine, other, vector=None, edge=None):
    owners, owned, width = mine.shape
    if vector is None:
        given, piece, lanes = [], owned // 8, width
        kernel = lambda mine, other, out: chip_kernel(mine, other, None, None, out)
    else:
        given, piece, lanes = [vector, edge], owned // 8 + 2, width + edge.shape[2]
        kernel = chip_kernel
    return pl.pallas_call(
        kernel,
        in_specs=[IN_VMEM] * (2 + len(given)),
        out_specs=IN_VMEM,
        out_shape=jax.ShapeDtypeStruct((owners * 8, piece, lanes), BF16),
        compiler_params=STAY,
        cost_estimate=cost(0.3),
        name="chip_sum",
    )(mine, other, *given)


BOTH = ("dp", "space")


def device(y, z, c, x, low):
    return (y * 8 + z * 2 + c) * 8 + x * 2 + low


OWNERS = [
    [device(y, z, c, x, low ^ y) for y in range(2) for z in range(4)]
    for c in range(2)
    for x in range(4)
    for low in range(2)
]
CORES = [
    [device(y, z, c, x, low) for y in range(2) for z in range(4) for x in range(4) for low in range(2)]
    for c in range(2)
]


def moved(move):
    return [
        (device(y, z, c, x, low), device(*move(y, z, c, x, low)))
        for y in range(2)
        for z in range(4)
        for c in range(2)
        for x in range(4)
        for low in range(2)
    ]


def to_other_core(value):
    return lax.ppermute(value, BOTH, moved(lambda y, z, c, x, low: (y, z, 1 - c, x, low)))


def to_other_half(value, cross):
    return lax.ppermute(value, BOTH, moved(lambda y, z, c, x, low: (1 - y, z, 1 - c if cross else c, x, low)))


def gather_mine(shard):
    return lax.all_to_all(jnp.broadcast_to(shard, (8,) + shard.shape), BOTH, 0, 0, axis_index_groups=OWNERS)


def with_other(mine):
    other = to_other_core(mine)
    return mine.reshape(-1, mine.shape[2]), other.reshape(-1, mine.shape[2])


def local_order(vector, owned):
    first, second = core_halves(vector.reshape(8, 2, owned), 1)
    return jnp.concatenate([first.reshape(2, -1), second.reshape(2, -1)], axis=0)


def core_halves(value, axis):
    c = lax.axis_index("dp") % 2
    low, high = lax.index_in_dim(value, 0, axis, False), lax.index_in_dim(value, 1, axis, False)
    return jnp.where(c == 0, low, high), jnp.where(c == 0, high, low)


def global_order(blocks, owned):
    n = blocks.shape[0]
    low, high = core_halves(blocks.reshape(n, 2, 8, owned), 1)
    return jnp.stack([low, high], axis=2).reshape(n, -1)


def sum_blocks(blocks):
    return jnp.sum(lax.all_to_all(blocks, BOTH, 0, 0, axis_index_groups=CORES).astype(F32), axis=0)


def exchange(value, axis):
    return lax.all_to_all(value, axis, 0, 0)


def everyone(value, axis):
    return exchange(jnp.broadcast_to(value, (lax.axis_size(axis),) + value.shape), axis)


def shift(rows, pairs):
    flat = rows.reshape(-1, 16, rows.shape[-1])
    return lax.ppermute(flat, "space", pairs).reshape(rows.shape)


def body(
    features, kernel, norm_gain, w_up, grn_gamma, grn_beta, w_down, upstream, labels, class_weight
):
    crops, rows, cols, width = features.shape
    feat, up = features[0], upstream[0]
    space = lax.axis_size("space")
    dp = lax.axis_size("dp")
    owned = w_up.shape[0]
    hid = owned * dp
    pixels = rows * cols
    rising = [(i, i + 1) for i in range(space - 1)]
    falling = [(j, i) for i, j in rising]
    above = shift(feat[rows - 3 :], rising)
    below = shift(feat[:3], falling)
    part = conv_own(feat, kernel)
    w_up_mine = gather_mine(w_up)
    w_up_mine, w_down, part, above, below = lax.optimization_barrier((w_up_mine, w_down, part, above, below))
    w_down_mine = gather_mine(w_down)
    gamma, beta = local_order(grn_gamma, owned), local_order(grn_beta, owned)

    classes = jnp.arange(class_weight.shape[0], dtype=jnp.int32)
    pixel_weight = jnp.sum(jnp.where(labels[0][..., None] == classes, class_weight, 0.0), axis=-1)
    weight = jnp.broadcast_to(pixel_weight[..., None], (rows, cols, LANES))
    weighted = (up.astype(F32) * pixel_weight[..., None]).astype(BF16).reshape(pixels, width)

    normed, xhat, rstd = conv_norm(part, above, below, kernel, norm_gain)
    w_up_all = with_other(w_up_mine)
    act, slope, sq = up_project(normed, w_up_all)
    w_down_mine, sq = lax.optimization_barrier((w_down_mine, sq))
    w_down_all = with_other(w_down_mine)
    gm, local, gm_sum = mixed_grad(weighted, w_down_all, act, sq)
    sums = everyone(local, "space")
    down_other_term, ratio, twice, parts = down_other(act, weighted, sums, local, gm_sum, gamma, beta)
    by_owner = lambda rows: rows.reshape(8, owned, width)
    came = to_other_core(by_owner(down_other_term))
    down_blocks = chip_sum(by_owner(down_mine(act, weighted, ratio, gamma, beta)), came)
    ratio, down_blocks = lax.optimization_barrier((ratio, down_blocks))
    down_rows = sum_blocks(down_blocks)
    up_mine, up_other, grad_conv, g_first, g_last, gain_part = hidden_grad(
        act, slope, gm, w_up_all, normed, ratio, twice, gamma, norm_gain, xhat, rstd, 3 * cols
    )
    grad_conv = grad_conv.reshape(rows, cols, width)
    g_above = shift(g_last.reshape(3, cols, width), rising)
    g_below = shift(g_first.reshape(3, cols, width), falling)
    kernel_part = taps_grad(feat, above, below, grad_conv)

    scale = 1.0 / math.sqrt(dp * space * pixels)
    vector = jnp.concatenate(
        [
            kernel_part.reshape(49, width),
            jnp.sum(gain_part, axis=0, keepdims=True),
            global_order(parts, owned).reshape(-1, width),
        ],
        axis=0,
    )
    lines = vector.shape[0]
    vector = jnp.pad(vector, ((0, -lines % 64), (0, 0))).reshape(16, 4, width)
    piece = owned // space
    lanes = 2 * width // piece
    edge = jnp.pad(vector[:, 2:].reshape(16, piece, lanes), ((0, 0), (0, 2), (0, 0)))
    up_blocks = chip_sum(by_owner(up_mine), to_other_core(by_owner(up_other)), vector[:, :2], edge)
    up_blocks, down_rows = lax.optimization_barrier((up_blocks, down_rows))
    up_rows = sum_blocks(up_blocks)
    grad_features = conv_back(grad_conv, g_above, g_below, kernel, up, weight)
    up_rows, grad_features = lax.optimization_barrier((up_rows, grad_features))

    vector = jnp.concatenate([up_rows[piece:, :width], up_rows[:piece, width:].reshape(2, width)], axis=0)
    here = vector + to_other_core(vector)
    there = to_other_half(vector, False) + to_other_half(vector, True)
    first = lax.axis_index("dp") < 8
    vector = jnp.concatenate([jnp.where(first, here, there), jnp.where(first, there, here)], axis=0)
    block = jnp.concatenate([up_rows[:piece, :width], down_rows], axis=1)
    block = jnp.concatenate([block, vector.reshape(4, 2 * width)], axis=0)
    block = everyone((scale * block).astype(BF16), "space").astype(F32)
    vector = jnp.transpose(block[:, piece:].reshape(space, 2, 4, width), (1, 0, 2, 3)).reshape(8 * space, width)
    kernel_sum = vector[:49].reshape(7, 7, width)
    gain_sum = vector[49]
    gamma_sum, beta_sum = vector[50:lines].reshape(2, hid)
    block = jnp.concatenate([block[:, :16].reshape(-1, 2 * width), block[:, 16:piece].reshape(-1, 2 * width)], axis=0)
    return (
        grad_features[None],
        kernel_sum,
        gain_sum,
        block[:, :width],
        gamma_sum,
        beta_sum,
        block[:, width:],
    )


def solution(mesh):
    return jax.shard_map(
        body,
        mesh=mesh,
        in_specs=(
            P("dp", "space", None, None),
            P(),
            P(),
            P("dp", None),
            P(),
            P(),
            P("dp", None),
            P("dp", "space", None, None),
            P("dp", "space", None),
            P(),
        ),
        out_specs=(P("dp", "space", None, None), P(), P(), P("dp", None), P(), P(), P("dp", None)),
        check_vma=False,
    )
```

```python
import functools
import math

import jax
import jax.numpy as jnp
from jax import lax
from jax.experimental import pallas as pl
from jax.experimental.pallas import tpu as pltpu
from jax.sharding import PartitionSpec as P

EPS_NORM = 1e-06
F32 = jnp.float32
BF16 = jnp.bfloat16
VMEM_LIMIT = 56 * 1024 * 1024
LANES = 128
PAD = 8
TILE = 8
GROUP = 4
CHUNKS = 3


def params(*semantics):
    return pltpu.CompilerParams(dimension_semantics=semantics, vmem_limit_bytes=VMEM_LIMIT)


def cost(micros):
    return pl.CostEstimate(flops=int(micros * 0.4e9), transcendentals=0, bytes_accessed=0)


def fill_padded(dst, src, first, lanes):
    rows, cols, _ = src.shape
    zeros = jnp.zeros((rows, PAD, LANES), F32)
    dst[first : first + rows, 0:PAD, :] = zeros
    dst[first : first + rows, PAD + cols : PAD + cols + PAD, :] = zeros
    dst[first : first + rows, PAD : PAD + cols, :] = src[:, :, lanes].astype(F32)


def spread_taps(dst, k_ref, flip, lanes):
    for i in range(7):
        for j in range(7):
            tap = k_ref[6 - i, 6 - j : 7 - j, lanes] if flip else k_ref[i, j : j + 1, lanes]
            dst[i * 7 + j] = jnp.broadcast_to(tap, (TILE, LANES))


def taps_group(src, taps, pairs, start, acc):
    rows = sorted({r for r, _, _ in pairs})
    for j in range(7):
        for r in rows:
            todo = [(o, i) for rr, o, i in pairs if rr == r]
            at = [start + TILE * b + PAD - 3 + j for b in range(GROUP)]
            xs = [src[r, p : p + TILE, :] for p in at]
            for o, i in todo:
                tap = taps[i * 7 + j]
                for b in range(GROUP):
                    acc[o][b] = acc[o][b] + xs[b] * tap
    return acc


def own_pairs():
    return [(s, o, s - o + 3) for s in range(4) for o in range(4)]


def halo_pairs():
    above = [(s, o, s - o) for s in range(3) for o in range(4) if 0 <= s - o <= 6]
    below = [(3 + s, o, s + 7 - o) for s in range(3) for o in range(4) if 0 <= s + 7 - o <= 6]
    return above + below


def each_chunk(body):
    def one(n, carry):
        body(n, pl.ds(pl.multiple_of(n * LANES, LANES), LANES))
        return carry

    lax.fori_loop(0, CHUNKS, one, 0)


def tile_rows(start, b):
    return slice(start + TILE * b, start + TILE * (b + 1))


def conv_own_kernel(feat, k_ref, out, xs, taps):
    cols = feat.shape[1]

    def chunk(n, lanes):
        fill_padded(xs, feat, 0, lanes)
        spread_taps(taps, k_ref, False, lanes)
        for start in range(0, cols, GROUP * TILE):
            acc = [[jnp.zeros((TILE, LANES), F32) for _ in range(GROUP)] for _ in range(4)]
            acc = taps_group(xs, taps, own_pairs(), start, acc)
            for o in range(4):
                for b in range(GROUP):
                    out[o, tile_rows(start, b), lanes] = acc[o][b]

    each_chunk(chunk)


def lane_blocks(rows, cols):
    return pl.BlockSpec((rows, cols, CHUNKS * LANES), lambda c: (0, 0, c))


def whole_block(*shape):
    return pl.BlockSpec(shape, lambda c: (0,) * len(shape))


def conv_own(feat, kernel):
    rows, cols, width = feat.shape
    return pl.pallas_call(
        conv_own_kernel,
        grid=(pl.cdiv(width, CHUNKS * LANES),),
        in_specs=[lane_blocks(rows, cols), lane_blocks(7, 7)],
        out_specs=lane_blocks(rows, cols),
        out_shape=jax.ShapeDtypeStruct((rows, cols, width), F32),
        scratch_shapes=[
            pltpu.VMEM((rows, cols + 2 * PAD, LANES), F32),
            pltpu.VMEM((49, TILE, LANES), F32),
        ],
        compiler_params=params("arbitrary"),
        cost_estimate=cost(5),
        name="conv_own",
    )(feat, kernel)


def conv_norm_kernel(width, steps, part, above, below, k_ref, gain, normed, xhat, rstd, xs, taps, conv):
    c = pl.program_id(0)
    cols = part.shape[1]

    def chunk(n, lanes):
        fill_padded(xs, above, 0, lanes)
        fill_padded(xs, below, 3, lanes)
        spread_taps(taps, k_ref, False, lanes)
        for start in range(0, cols, GROUP * TILE):
            acc = [[part[o, tile_rows(start, b), lanes] for b in range(GROUP)] for o in range(4)]
            acc = taps_group(xs, taps, halo_pairs(), start, acc)
            for o in range(4):
                for b in range(GROUP):
                    conv[c * CHUNKS + n, tile_rows(o * cols + start, b), :] = acc[o][b]

    each_chunk(chunk)

    @pl.when(c == steps - 1)
    def _():
        chunks = pl.cdiv(width, LANES)
        last = width - (chunks - 1) * LANES
        block = 64

        def one(t, carry):
            at = pl.multiple_of(t * block, block)
            parts = [conv[n, pl.ds(at, block), :] for n in range(chunks)]
            lane = lax.broadcasted_iota(jnp.int32, (block, LANES), 1)
            inside = lane < last
            parts[-1] = jnp.where(inside, parts[-1], 0.0)
            mean = jnp.sum(sum(parts[1:], parts[0]), axis=-1, keepdims=True) / width
            centred = [p - mean for p in parts]
            centred[-1] = jnp.where(inside, centred[-1], 0.0)
            squares = [p * p for p in centred]
            var = jnp.sum(sum(squares[1:], squares[0]), axis=-1, keepdims=True) / width
            scale = lax.rsqrt(var + EPS_NORM)
            rstd[pl.ds(at, block), :] = jnp.broadcast_to(scale, (block, LANES))
            for n in range(chunks):
                w = min(LANES, width - n * LANES)
                hat = centred[n] * scale
                g = gain[:, n * LANES : n * LANES + w]
                xhat[pl.ds(at, block), n * LANES : n * LANES + w] = hat[:, :w]
                normed[pl.ds(at, block), n * LANES : n * LANES + w] = (hat[:, :w] * g).astype(BF16)
            return carry

        lax.fori_loop(0, (4 * cols) // block, one, 0)


def conv_norm(part, above, below, kernel, gain):
    rows, cols, width = part.shape
    steps = pl.cdiv(width, CHUNKS * LANES)
    pixels = rows * cols
    return pl.pallas_call(
        functools.partial(conv_norm_kernel, width, steps),
        grid=(steps,),
        in_specs=[
            lane_blocks(rows, cols),
            lane_blocks(3, cols),
            lane_blocks(3, cols),
            lane_blocks(7, 7),
            whole_block(1, width),
        ],
        out_specs=[whole_block(pixels, width), whole_block(pixels, width), whole_block(pixels, LANES)],
        out_shape=[
            jax.ShapeDtypeStruct((pixels, width), BF16),
            jax.ShapeDtypeStruct((pixels, width), F32),
            jax.ShapeDtypeStruct((pixels, LANES), F32),
        ],
        scratch_shapes=[
            pltpu.VMEM((6, cols + 2 * PAD, LANES), F32),
            pltpu.VMEM((49, TILE, LANES), F32),
            pltpu.VMEM((steps * CHUNKS, pixels, LANES), F32),
        ],
        compiler_params=params("arbitrary"),
        cost_estimate=cost(7),
        name="conv_norm",
    )(part, above, below, kernel, gain.reshape(1, width))


IN_VMEM = pl.BlockSpec(memory_space=pltpu.VMEM)
STAY = pltpu.CompilerParams(vmem_limit_bytes=12 * 1024 * 1024)


def with_rows(h, mine, other, step):
    pl.when(h < 2)(lambda: step(mine))
    pl.when(h >= 2)(lambda: step(other))


def half_rows(block, width):
    mine = pl.BlockSpec((block, width), lambda h: (jnp.minimum(h, 1), 0))
    other = pl.BlockSpec((block, width), lambda h: (jnp.maximum(h - 2, 0), 0))
    return mine, other


def up_kernel(normed, w_mine, w_other, act_ref, slope_ref, sums):
    def step(w):
        nt = (((1,), (1,)), ((), ()))
        hidden = lax.dot_general(normed[...], w[...], nt, preferred_element_type=F32)
        cdf = 0.5 * (1.0 + lax.erf(hidden * (2.0**-0.5)))
        act = hidden * cdf
        slope_ref[0] = cdf + hidden * (jnp.exp(hidden * hidden * -0.5) * (1.0 / math.sqrt(2.0 * math.pi)))
        act_ref[0] = act
        sums[0] = jnp.sum((act * act).reshape(-1, 8, act.shape[1]), axis=0)

    with_rows(pl.program_id(0), w_mine, w_other, step)


def up_project(normed, w_up):
    pixels, width = normed.shape
    block = w_up[0].shape[0] // 2
    cols = pl.BlockSpec((1, pixels, block), lambda h: (h, 0, 0))
    big = jax.ShapeDtypeStruct((4, pixels, block), F32)
    return pl.pallas_call(
        up_kernel,
        grid=(4,),
        in_specs=[whole_block(pixels, width), *half_rows(block, width)],
        out_specs=[cols, cols, pl.BlockSpec((1, 8, block), lambda h: (h, 0, 0))],
        out_shape=[big, big, jax.ShapeDtypeStruct((4, 8, block), F32)],
        compiler_params=params("arbitrary"),
        cost_estimate=cost(9),
        name="up_project",
    )(normed, *w_up)


def mixed_kernel(weighted, w_mine, w_other, act_ref, sq, gm_ref, sums, gm_sum):
    h = pl.program_id(0)

    def step(w):
        nt = (((1,), (1,)), ((), ()))
        gm = lax.dot_general(weighted[...], w[...], nt, preferred_element_type=F32)
        gm_ref[0] = gm
        square = jnp.sum(sq[0], axis=0, keepdims=True)
        dot = jnp.sum(gm * act_ref[0], axis=0, keepdims=True)
        for d in range(sums.shape[0]):
            sums[d, pl.ds(h, 1), :] = square
            sums[d, pl.ds(h + 4, 1), :] = dot
        gm_sum[pl.ds(h, 1), :] = jnp.sum(gm, axis=0, keepdims=True)

    with_rows(h, w_mine, w_other, step)


def mixed_grad(weighted, w_down, act, sq, members):
    pixels, width = weighted.shape
    block = w_down[0].shape[0] // 2
    cols = pl.BlockSpec((1, pixels, block), lambda h: (h, 0, 0))
    return pl.pallas_call(
        mixed_kernel,
        grid=(4,),
        in_specs=[
            whole_block(pixels, width),
            *half_rows(block, width),
            cols,
            pl.BlockSpec((1, 8, block), lambda h: (h, 0, 0)),
        ],
        out_specs=[cols, whole_block(members, 8, block), whole_block(4, block)],
        out_shape=[
            jax.ShapeDtypeStruct((4, pixels, block), F32),
            jax.ShapeDtypeStruct((members, 8, block), F32),
            jax.ShapeDtypeStruct((4, block), F32),
        ],
        compiler_params=params("arbitrary"),
        cost_estimate=cost(8),
        name="mixed_grad",
    )(weighted, *w_down, act, sq)


def ratio_of(sq, dot, gamma):
    energy = jnp.sqrt(sq)
    hid = energy.shape[0] * energy.shape[1]
    total = lambda x: jnp.sum(jnp.sum(x, axis=1, keepdims=True), axis=0, keepdims=True)
    mean = total(energy) / hid + EPS_NORM
    grad_ratio = gamma * dot
    shared = total(grad_ratio * energy) / (mean * mean) / hid
    return energy / mean, (grad_ratio / mean - shared) / energy


def store_rows(half, i, value):
    block = half.shape[0] // 2
    half[pl.ds(pl.multiple_of(i * block, block), block), :] = value


def outer(left, right):
    return lax.dot_general(left, right, (((0,), (0,)), ((), ())), preferred_element_type=F32).astype(BF16)


def down_rows_of(half, first, act, weighted, gamma, ratio, beta):
    def one(i, carry):
        row = pl.ds(first + i, 1)
        a = act[first + i]
        mixed = (gamma[row, :] * a * ratio[row, :] + beta[row, :] + a).astype(BF16)
        store_rows(half, i, outer(mixed, weighted[...]))
        return carry

    lax.fori_loop(0, 2, one, 0)


def down_other_kernel(act, weighted, sums, local, gm_sum, gamma, beta, other, ratio, twice, parts):
    crop = jnp.sum(sums[...], axis=0)
    r, t = ratio_of(crop[:4], crop[4:], gamma[...])
    ratio[...] = r
    twice[...] = t
    parts[0] = local[0, 4:, :] * r
    parts[1] = gm_sum[...]
    down_rows_of(other, 2, act, weighted, gamma, ratio, beta)


def down_other(act, weighted, sums, local, gm_sum, gamma, beta):
    _, pixels, block = act.shape
    width = weighted.shape[1]
    vec = jax.ShapeDtypeStruct((4, block), F32)
    return pl.pallas_call(
        down_other_kernel,
        in_specs=[IN_VMEM] * 7,
        out_specs=[IN_VMEM] * 4,
        out_shape=[
            jax.ShapeDtypeStruct((2 * block, width), BF16),
            vec,
            vec,
            jax.ShapeDtypeStruct((2, 4, block), F32),
        ],
        compiler_params=STAY,
        cost_estimate=cost(4),
        name="down_other",
    )(act, weighted, sums, local, gm_sum, gamma, beta)


def down_mine_kernel(act, weighted, ratio, gamma, beta, mine):
    down_rows_of(mine, 0, act, weighted, gamma, ratio, beta)


def down_mine(act, weighted, ratio, gamma, beta):
    _, pixels, block = act.shape
    width = weighted.shape[1]
    return pl.pallas_call(
        down_mine_kernel,
        in_specs=[IN_VMEM] * 5,
        out_specs=IN_VMEM,
        out_shape=jax.ShapeDtypeStruct((2 * block, width), BF16),
        compiler_params=STAY,
        cost_estimate=cost(4),
        name="down_mine",
    )(act, weighted, ratio, gamma, beta)


def hidden_kernel(
    act, slope, gm, w_mine, w_other, normed, ratio, twice, gamma, gain, xhat, rstd,
    mine, other, grad_conv, first, last, gain_part, total,
):
    h = pl.program_id(0)
    row = pl.ds(h, 1)
    grad_act = gm[0] * (gamma[row, :] * ratio[row, :] + 1.0) + act[0] * twice[row, :]
    grad_hidden = (grad_act * slope[0]).astype(BF16)
    term = outer(grad_hidden, normed[...])

    @pl.when(h == 0)
    def _():
        total[...] = jnp.dot(grad_hidden, w_mine[...], preferred_element_type=F32)
        mine[...] = term

    @pl.when(h == 1)
    def _():
        total[...] += jnp.dot(grad_hidden, w_mine[...], preferred_element_type=F32)
        mine[...] = term

    @pl.when(h >= 2)
    def _():
        total[...] += jnp.dot(grad_hidden, w_other[...], preferred_element_type=F32)
        other[...] = term

    @pl.when(h == 3)
    def _():
        pixels, width = total.shape
        block = 64

        def one(t, carry):
            at = pl.ds(pl.multiple_of(t * block, block), block)
            g = total[at, :]
            hat = xhat[at, :]
            carry = carry + jnp.sum((g * hat).reshape(block // 8, 8, width), axis=0)
            g = g * gain[...]
            mean_g = jnp.sum(g, axis=-1, keepdims=True) / width
            mean_gh = jnp.sum(g * hat, axis=-1, keepdims=True) / width
            out = rstd[at, 0:1] * (g - mean_g - hat * mean_gh)
            grad_conv[at, :] = out

            @pl.when(t * block < first.shape[0])
            def _():
                first[at, :] = out.astype(BF16)

            @pl.when(t * block >= pixels - last.shape[0])
            def _():
                last[pl.ds(pl.multiple_of(t * block - (pixels - last.shape[0]), block), block), :] = out.astype(BF16)

            return carry

        gain_part[...] = lax.fori_loop(0, pixels // block, one, jnp.zeros((8, width), F32))


def hidden_grad(act, slope, gm, w_up, normed, ratio, twice, gamma, gain, xhat, rstd, edge):
    _, pixels, block = act.shape
    width = normed.shape[1]
    cols = pl.BlockSpec((1, pixels, block), lambda h: (h, 0, 0))
    vec = whole_block(4, block)
    mine, other = half_rows(block, width)
    term = jax.ShapeDtypeStruct((2 * block, width), BF16)
    return pl.pallas_call(
        hidden_kernel,
        grid=(4,),
        in_specs=[
            cols, cols, cols, mine, other, whole_block(pixels, width), vec, vec, vec,
            whole_block(1, width), whole_block(pixels, width), whole_block(pixels, LANES),
        ],
        out_specs=[
            mine, other, whole_block(pixels, width), whole_block(edge, width), whole_block(edge, width),
            whole_block(8, width),
        ],
        out_shape=[
            term,
            term,
            jax.ShapeDtypeStruct((pixels, width), F32),
            jax.ShapeDtypeStruct((edge, width), BF16),
            jax.ShapeDtypeStruct((edge, width), BF16),
            jax.ShapeDtypeStruct((8, width), F32),
        ],
        scratch_shapes=[pltpu.VMEM((pixels, width), F32)],
        compiler_params=params("arbitrary"),
        cost_estimate=cost(14),
        name="hidden_grad",
    )(act, slope, gm, *w_up, normed, ratio, twice, gamma, gain.reshape(1, width), xhat, rstd)


def taps_grad_kernel(feat, above, below, grad, ktaps, xs, gs):
    cols = feat.shape[1]

    def chunk(n, lanes):
        fill_padded(xs, above, 0, lanes)
        fill_padded(xs, feat, 3, lanes)
        fill_padded(xs, below, 7, lanes)
        gs[...] = grad[:, :, lanes]
        for j in range(7):
            sums = [jnp.zeros((TILE, LANES), F32) for _ in range(7)]
            for start in range(0, cols, TILE):
                g = [gs[o, start : start + TILE, :] for o in range(4)]
                for r in range(10):
                    x = xs[r, PAD - 3 + j + start : PAD - 3 + j + start + TILE, :]
                    for o in range(4):
                        if 0 <= r - o <= 6:
                            sums[r - o] = sums[r - o] + x * g[o]
            for i in range(7):
                ktaps[i, j : j + 1, lanes] = jnp.sum(sums[i], axis=0, keepdims=True)

    each_chunk(chunk)


def taps_grad(feat, above, below, grad):
    rows, cols, width = feat.shape
    return pl.pallas_call(
        taps_grad_kernel,
        grid=(pl.cdiv(width, CHUNKS * LANES),),
        in_specs=[
            lane_blocks(rows, cols),
            lane_blocks(3, cols),
            lane_blocks(3, cols),
            lane_blocks(rows, cols),
        ],
        out_specs=lane_blocks(7, 7),
        out_shape=jax.ShapeDtypeStruct((7, 7, width), F32),
        scratch_shapes=[
            pltpu.VMEM((rows + 6, cols + 2 * PAD, LANES), F32),
            pltpu.VMEM((rows, cols, LANES), F32),
        ],
        compiler_params=params("arbitrary"),
        cost_estimate=cost(1),
        name="taps_grad",
    )(feat, above, below, grad)


def all_pairs():
    return [(r, o, r - o) for r in range(10) for o in range(4) if 0 <= r - o <= 6]


def conv_back_kernel(grad, above, below, k_ref, upstream, weight, out, xs, taps):
    cols = grad.shape[1]

    def chunk(n, lanes):
        fill_padded(xs, above, 0, lanes)
        fill_padded(xs, grad, 3, lanes)
        fill_padded(xs, below, 7, lanes)
        spread_taps(taps, k_ref, True, lanes)
        for start in range(0, cols, GROUP * TILE):
            acc = [[None] * GROUP for _ in range(4)]
            for o in range(4):
                for b in range(GROUP):
                    at = tile_rows(start, b)
                    acc[o][b] = upstream[o, at, lanes].astype(F32) * weight[o, at, :]
            acc = taps_group(xs, taps, all_pairs(), start, acc)
            for o in range(4):
                for b in range(GROUP):
                    out[o, tile_rows(start, b), lanes] = acc[o][b]

    each_chunk(chunk)


def conv_back(grad, above, below, kernel, upstream, weight):
    rows, cols, width = grad.shape
    return pl.pallas_call(
        conv_back_kernel,
        grid=(pl.cdiv(width, CHUNKS * LANES),),
        in_specs=[
            lane_blocks(rows, cols),
            lane_blocks(3, cols),
            lane_blocks(3, cols),
            lane_blocks(7, 7),
            lane_blocks(rows, cols),
            whole_block(rows, cols, LANES),
        ],
        out_specs=lane_blocks(rows, cols),
        out_shape=jax.ShapeDtypeStruct((rows, cols, width), F32),
        scratch_shapes=[
            pltpu.VMEM((rows + 6, cols + 2 * PAD, LANES), F32),
            pltpu.VMEM((49, TILE, LANES), F32),
        ],
        compiler_params=params("arbitrary"),
        cost_estimate=cost(60),
        name="conv_back",
    )(grad, above, below, kernel, upstream, weight)


def chip_kernel(mine, other, vector, edge, out):
    width = mine.shape[2]
    def one(q, carry):
        high = (mine[q, :128, :].astype(F32) + other[q, :128, :].astype(F32)).astype(BF16)
        low = mine[q, 128:, :].astype(F32) + other[q, 128:, :].astype(F32)
        for s in range(8):
            out[q * 8 + s, :16, :width] = high[16 * s : 16 * (s + 1), :]
            rest = low[6 * s : 6 * (s + 1), :]
            if vector is not None:
                at = q // 4 * 8 + s
                rest = jnp.concatenate([rest, vector[at]], axis=0)
                out[q * 8 + s, :16, width:] = edge[at, :16, :].astype(BF16)
                out[q * 8 + s, 16:, width:] = edge[at, 16:, :].astype(BF16)
            out[q * 8 + s, 16:, :width] = rest.astype(BF16)
        return carry

    lax.fori_loop(0, mine.shape[0], one, 0)


def chip_sum(mine, other, vector=None, edge=None):
    owners, owned, width = mine.shape
    if vector is None:
        given, piece, lanes = [], owned // 8, width
        kernel = lambda mine, other, out: chip_kernel(mine, other, None, None, out)
    else:
        given, piece, lanes = [vector, edge], owned // 8 + 2, width + edge.shape[2]
        kernel = chip_kernel
    return pl.pallas_call(
        kernel,
        in_specs=[IN_VMEM] * (2 + len(given)),
        out_specs=IN_VMEM,
        out_shape=jax.ShapeDtypeStruct((owners * 8, piece, lanes), BF16),
        compiler_params=STAY,
        cost_estimate=cost(0.3),
        name="chip_sum",
    )(mine, other, *given)


BOTH = ("dp", "space")


def device(y, z, c, x, low):
    return (y * 8 + z * 2 + c) * 8 + x * 2 + low


OWNERS = [
    [device(y, z, c, x, low ^ y) for y in range(2) for z in range(4)]
    for c in range(2)
    for x in range(4)
    for low in range(2)
]
CORES = [
    [device(y, z, c, x, low) for y in range(2) for z in range(4) for x in range(4) for low in range(2)]
    for c in range(2)
]


def moved(move):
    return [
        (device(y, z, c, x, low), device(*move(y, z, c, x, low)))
        for y in range(2)
        for z in range(4)
        for c in range(2)
        for x in range(4)
        for low in range(2)
    ]


def to_other_core(value):
    return lax.ppermute(value, BOTH, moved(lambda y, z, c, x, low: (y, z, 1 - c, x, low)))


def to_other_half(value, cross):
    return lax.ppermute(value, BOTH, moved(lambda y, z, c, x, low: (1 - y, z, 1 - c if cross else c, x, low)))


def copies(shard):
    return jnp.broadcast_to(shard, (8,) + shard.shape)


def gather_mine(shards):
    return lax.all_to_all(shards, BOTH, 0, 0, axis_index_groups=OWNERS)


def with_other(mine):
    other = to_other_core(mine)
    return mine.reshape(-1, mine.shape[2]), other.reshape(-1, mine.shape[2])


def local_order(vector, owned):
    first, second = core_halves(vector.reshape(8, 2, owned), 1)
    return jnp.concatenate([first.reshape(2, -1), second.reshape(2, -1)], axis=0)


def core_halves(value, axis):
    c = lax.axis_index("dp") % 2
    low, high = lax.index_in_dim(value, 0, axis, False), lax.index_in_dim(value, 1, axis, False)
    return jnp.where(c == 0, low, high), jnp.where(c == 0, high, low)


def global_order(blocks, owned):
    n = blocks.shape[0]
    low, high = core_halves(blocks.reshape(n, 2, 8, owned), 1)
    return jnp.stack([low, high], axis=2).reshape(n, -1)


def sum_blocks(blocks):
    return jnp.sum(lax.all_to_all(blocks, BOTH, 0, 0, axis_index_groups=CORES).astype(F32), axis=0)


def exchange(value, axis):
    return lax.all_to_all(value, axis, 0, 0)


def everyone(value, axis):
    return exchange(jnp.broadcast_to(value, (lax.axis_size(axis),) + value.shape), axis)


def shift(rows, pairs):
    flat = rows.reshape(-1, 16, rows.shape[-1])
    return lax.ppermute(flat, "space", pairs).reshape(rows.shape)


def body(
    features, kernel, norm_gain, w_up, grn_gamma, grn_beta, w_down, upstream, labels, class_weight
):
    crops, rows, cols, width = features.shape
    feat, up = features[0], upstream[0]
    space = lax.axis_size("space")
    dp = lax.axis_size("dp")
    owned = w_up.shape[0]
    hid = owned * dp
    pixels = rows * cols
    rising = [(i, i + 1) for i in range(space - 1)]
    falling = [(j, i) for i, j in rising]
    above = shift(feat[rows - 3 :], rising)
    below = shift(feat[:3], falling)
    w_up_mine = gather_mine(copies(w_up))
    inner, w_down = lax.optimization_barrier((feat, copies(w_down)))
    part = conv_own(inner, kernel)
    w_up_mine, w_down, part, above, below = lax.optimization_barrier((w_up_mine, w_down, part, above, below))
    w_down_mine = gather_mine(w_down)
    gamma, beta = local_order(grn_gamma, owned), local_order(grn_beta, owned)

    classes = jnp.arange(class_weight.shape[0], dtype=jnp.int32)
    pixel_weight = jnp.sum(jnp.where(labels[0][..., None] == classes, class_weight, 0.0), axis=-1)
    weight = jnp.broadcast_to(pixel_weight[..., None], (rows, cols, LANES))
    weighted = (up.astype(F32) * pixel_weight[..., None]).astype(BF16).reshape(pixels, width)

    normed, xhat, rstd = conv_norm(part, above, below, kernel, norm_gain)
    w_up_all = with_other(w_up_mine)
    act, slope, sq = up_project(normed, w_up_all)
    w_down_mine, sq = lax.optimization_barrier((w_down_mine, sq))
    w_down_all = with_other(w_down_mine)
    gm, local, gm_sum = mixed_grad(weighted, w_down_all, act, sq, space)
    sums = exchange(local, "space")
    down_other_term, ratio, twice, parts = down_other(act, weighted, sums, local, gm_sum, gamma, beta)
    by_owner = lambda rows: rows.reshape(8, owned, width)
    came = to_other_core(by_owner(down_other_term))
    down_blocks = chip_sum(by_owner(down_mine(act, weighted, ratio, gamma, beta)), came)
    ratio, down_blocks = lax.optimization_barrier((ratio, down_blocks))
    down_rows = sum_blocks(down_blocks)
    up_mine, up_other, grad_conv, g_first, g_last, gain_part = hidden_grad(
        act, slope, gm, w_up_all, normed, ratio, twice, gamma, norm_gain, xhat, rstd, 3 * cols
    )
    grad_conv = grad_conv.reshape(rows, cols, width)
    g_above = shift(g_last.reshape(3, cols, width), rising)
    g_below = shift(g_first.reshape(3, cols, width), falling)
    kernel_part = taps_grad(feat, above, below, grad_conv)

    scale = 1.0 / math.sqrt(dp * space * pixels)
    vector = jnp.concatenate(
        [
            kernel_part.reshape(49, width),
            jnp.sum(gain_part, axis=0, keepdims=True),
            global_order(parts, owned).reshape(-1, width),
        ],
        axis=0,
    )
    lines = vector.shape[0]
    vector = jnp.pad(vector, ((0, -lines % 64), (0, 0))).reshape(16, 4, width)
    piece = owned // space
    lanes = 2 * width // piece
    edge = jnp.pad(vector[:, 2:].reshape(16, piece, lanes), ((0, 0), (0, 2), (0, 0)))
    up_blocks = chip_sum(by_owner(up_mine), to_other_core(by_owner(up_other)), vector[:, :2], edge)
    up_blocks, down_rows = lax.optimization_barrier((up_blocks, down_rows))
    up_rows = sum_blocks(up_blocks)
    grad_features = conv_back(grad_conv, g_above, g_below, kernel, up, weight)
    up_rows, grad_features = lax.optimization_barrier((up_rows, grad_features))

    vector = jnp.concatenate([up_rows[piece:, :width], up_rows[:piece, width:].reshape(2, width)], axis=0)
    here = vector + to_other_core(vector)
    there = to_other_half(vector, False) + to_other_half(vector, True)
    first = lax.axis_index("dp") < 8
    vector = jnp.concatenate([jnp.where(first, here, there), jnp.where(first, there, here)], axis=0)
    block = jnp.concatenate([up_rows[:piece, :width], down_rows], axis=1)
    block = jnp.concatenate([block, vector.reshape(4, 2 * width)], axis=0)
    block = everyone((scale * block).astype(BF16), "space").astype(F32)
    vector = jnp.transpose(block[:, piece:].reshape(space, 2, 4, width), (1, 0, 2, 3)).reshape(8 * space, width)
    kernel_sum = vector[:49].reshape(7, 7, width)
    gain_sum = vector[49]
    gamma_sum, beta_sum = vector[50:lines].reshape(2, hid)
    block = jnp.concatenate([block[:, :16].reshape(-1, 2 * width), block[:, 16:piece].reshape(-1, 2 * width)], axis=0)
    return (
        grad_features[None],
        kernel_sum,
        gain_sum,
        block[:, :width],
        gamma_sum,
        beta_sum,
        block[:, width:],
    )


def solution(mesh):
    return jax.shard_map(
        body,
        mesh=mesh,
        in_specs=(
            P("dp", "space", None, None),
            P(),
            P(),
            P("dp", None),
            P(),
            P(),
            P("dp", None),
            P("dp", "space", None, None),
            P("dp", "space", None),
            P(),
        ),
        out_specs=(P("dp", "space", None, None), P(), P(), P("dp", None), P(), P(), P("dp", None)),
        check_vma=False,
    )
```

```python
import functools
import math

import jax
import jax.numpy as jnp
from jax import lax
from jax.experimental import pallas as pl
from jax.experimental.pallas import tpu as pltpu
from jax.sharding import PartitionSpec as P

EPS_NORM = 1e-06
F32 = jnp.float32
BF16 = jnp.bfloat16
VMEM_LIMIT = 56 * 1024 * 1024
LANES = 128
PAD = 8
TILE = 8
GROUP = 4
CHUNKS = 3


def params(*semantics):
    return pltpu.CompilerParams(dimension_semantics=semantics, vmem_limit_bytes=VMEM_LIMIT)


def cost(micros):
    return pl.CostEstimate(flops=int(micros * 0.4e9), transcendentals=0, bytes_accessed=0)


def fill_padded(dst, src, first, lanes):
    rows, cols, _ = src.shape
    zeros = jnp.zeros((rows, PAD, LANES), F32)
    dst[first : first + rows, 0:PAD, :] = zeros
    dst[first : first + rows, PAD + cols : PAD + cols + PAD, :] = zeros
    dst[first : first + rows, PAD : PAD + cols, :] = src[:, :, lanes].astype(F32)


def spread_taps(dst, k_ref, flip, lanes):
    for i in range(7):
        for j in range(7):
            tap = k_ref[6 - i, 6 - j : 7 - j, lanes] if flip else k_ref[i, j : j + 1, lanes]
            dst[i * 7 + j] = jnp.broadcast_to(tap, (TILE, LANES))


def taps_group(src, taps, pairs, start, acc):
    rows = sorted({r for r, _, _ in pairs})
    for j in range(7):
        for r in rows:
            todo = [(o, i) for rr, o, i in pairs if rr == r]
            at = [start + TILE * b + PAD - 3 + j for b in range(GROUP)]
            xs = [src[r, p : p + TILE, :] for p in at]
            for o, i in todo:
                tap = taps[i * 7 + j]
                for b in range(GROUP):
                    acc[o][b] = acc[o][b] + xs[b] * tap
    return acc


def own_pairs():
    return [(s, o, s - o + 3) for s in range(4) for o in range(4)]


def halo_pairs():
    above = [(s, o, s - o) for s in range(3) for o in range(4) if 0 <= s - o <= 6]
    below = [(3 + s, o, s + 7 - o) for s in range(3) for o in range(4) if 0 <= s + 7 - o <= 6]
    return above + below


def each_chunk(body):
    def one(n, carry):
        body(n, pl.ds(pl.multiple_of(n * LANES, LANES), LANES))
        return carry

    lax.fori_loop(0, CHUNKS, one, 0)


def tile_rows(start, b):
    return slice(start + TILE * b, start + TILE * (b + 1))


def conv_own_kernel(feat, k_ref, out, xs, taps):
    cols = feat.shape[1]

    def chunk(n, lanes):
        fill_padded(xs, feat, 0, lanes)
        spread_taps(taps, k_ref, False, lanes)
        for start in range(0, cols, GROUP * TILE):
            acc = [[jnp.zeros((TILE, LANES), F32) for _ in range(GROUP)] for _ in range(4)]
            acc = taps_group(xs, taps, own_pairs(), start, acc)
            for o in range(4):
                for b in range(GROUP):
                    out[o, tile_rows(start, b), lanes] = acc[o][b]

    each_chunk(chunk)


def lane_blocks(rows, cols):
    return pl.BlockSpec((rows, cols, CHUNKS * LANES), lambda c: (0, 0, c))


def whole_block(*shape):
    return pl.BlockSpec(shape, lambda c: (0,) * len(shape))


def conv_own(feat, kernel):
    rows, cols, width = feat.shape
    return pl.pallas_call(
        conv_own_kernel,
        grid=(pl.cdiv(width, CHUNKS * LANES),),
        in_specs=[lane_blocks(rows, cols), lane_blocks(7, 7)],
        out_specs=lane_blocks(rows, cols),
        out_shape=jax.ShapeDtypeStruct((rows, cols, width), F32),
        scratch_shapes=[
            pltpu.VMEM((rows, cols + 2 * PAD, LANES), F32),
            pltpu.VMEM((49, TILE, LANES), F32),
        ],
        compiler_params=params("arbitrary"),
        cost_estimate=cost(5),
        name="conv_own",
    )(feat, kernel)


def conv_norm_kernel(width, steps, part, above, below, k_ref, gain, normed, xhat, rstd, xs, taps, conv):
    c = pl.program_id(0)
    cols = part.shape[1]

    def chunk(n, lanes):
        fill_padded(xs, above, 0, lanes)
        fill_padded(xs, below, 3, lanes)
        spread_taps(taps, k_ref, False, lanes)
        for start in range(0, cols, GROUP * TILE):
            acc = [[part[o, tile_rows(start, b), lanes] for b in range(GROUP)] for o in range(4)]
            acc = taps_group(xs, taps, halo_pairs(), start, acc)
            for o in range(4):
                for b in range(GROUP):
                    conv[c * CHUNKS + n, tile_rows(o * cols + start, b), :] = acc[o][b]

    each_chunk(chunk)

    @pl.when(c == steps - 1)
    def _():
        chunks = pl.cdiv(width, LANES)
        last = width - (chunks - 1) * LANES
        block = 64

        def one(t, carry):
            at = pl.multiple_of(t * block, block)
            parts = [conv[n, pl.ds(at, block), :] for n in range(chunks)]
            lane = lax.broadcasted_iota(jnp.int32, (block, LANES), 1)
            inside = lane < last
            parts[-1] = jnp.where(inside, parts[-1], 0.0)
            mean = jnp.sum(sum(parts[1:], parts[0]), axis=-1, keepdims=True) / width
            centred = [p - mean for p in parts]
            centred[-1] = jnp.where(inside, centred[-1], 0.0)
            squares = [p * p for p in centred]
            var = jnp.sum(sum(squares[1:], squares[0]), axis=-1, keepdims=True) / width
            scale = lax.rsqrt(var + EPS_NORM)
            rstd[pl.ds(at, block), :] = jnp.broadcast_to(scale, (block, LANES))
            for n in range(chunks):
                w = min(LANES, width - n * LANES)
                hat = centred[n] * scale
                g = gain[:, n * LANES : n * LANES + w]
                xhat[pl.ds(at, block), n * LANES : n * LANES + w] = hat[:, :w]
                normed[pl.ds(at, block), n * LANES : n * LANES + w] = (hat[:, :w] * g).astype(BF16)
            return carry

        lax.fori_loop(0, (4 * cols) // block, one, 0)


def conv_norm(part, above, below, kernel, gain):
    rows, cols, width = part.shape
    steps = pl.cdiv(width, CHUNKS * LANES)
    pixels = rows * cols
    return pl.pallas_call(
        functools.partial(conv_norm_kernel, width, steps),
        grid=(steps,),
        in_specs=[
            lane_blocks(rows, cols),
            lane_blocks(3, cols),
            lane_blocks(3, cols),
            lane_blocks(7, 7),
            whole_block(1, width),
        ],
        out_specs=[whole_block(pixels, width), whole_block(pixels, width), whole_block(pixels, LANES)],
        out_shape=[
            jax.ShapeDtypeStruct((pixels, width), BF16),
            jax.ShapeDtypeStruct((pixels, width), F32),
            jax.ShapeDtypeStruct((pixels, LANES), F32),
        ],
        scratch_shapes=[
            pltpu.VMEM((6, cols + 2 * PAD, LANES), F32),
            pltpu.VMEM((49, TILE, LANES), F32),
            pltpu.VMEM((steps * CHUNKS, pixels, LANES), F32),
        ],
        compiler_params=params("arbitrary"),
        cost_estimate=cost(7),
        name="conv_norm",
    )(part, above, below, kernel, gain.reshape(1, width))


IN_VMEM = pl.BlockSpec(memory_space=pltpu.VMEM)
STAY = pltpu.CompilerParams(vmem_limit_bytes=12 * 1024 * 1024)


def with_rows(h, mine, other, step):
    pl.when(h < 2)(lambda: step(mine))
    pl.when(h >= 2)(lambda: step(other))


def half_rows(block, width):
    mine = pl.BlockSpec((block, width), lambda h: (jnp.minimum(h, 1), 0))
    other = pl.BlockSpec((block, width), lambda h: (jnp.maximum(h - 2, 0), 0))
    return mine, other


def up_kernel(normed, w_mine, w_other, act_ref, slope_ref, sums):
    def step(w):
        nt = (((1,), (1,)), ((), ()))
        hidden = lax.dot_general(normed[...], w[...], nt, preferred_element_type=F32)
        cdf = 0.5 * (1.0 + lax.erf(hidden * (2.0**-0.5)))
        act = hidden * cdf
        slope_ref[0] = cdf + hidden * (jnp.exp(hidden * hidden * -0.5) * (1.0 / math.sqrt(2.0 * math.pi)))
        act_ref[0] = act
        sums[0] = jnp.sum((act * act).reshape(-1, 8, act.shape[1]), axis=0)

    with_rows(pl.program_id(0), w_mine, w_other, step)


def up_project(normed, w_up):
    pixels, width = normed.shape
    block = w_up[0].shape[0] // 2
    cols = pl.BlockSpec((1, pixels, block), lambda h: (h, 0, 0))
    big = jax.ShapeDtypeStruct((4, pixels, block), F32)
    return pl.pallas_call(
        up_kernel,
        grid=(4,),
        in_specs=[whole_block(pixels, width), *half_rows(block, width)],
        out_specs=[cols, cols, pl.BlockSpec((1, 8, block), lambda h: (h, 0, 0))],
        out_shape=[big, big, jax.ShapeDtypeStruct((4, 8, block), F32)],
        compiler_params=params("arbitrary"),
        cost_estimate=cost(9),
        name="up_project",
    )(normed, *w_up)


def mixed_kernel(weighted, w_mine, w_other, act_ref, sq, gm_ref, sums, gm_sum):
    h = pl.program_id(0)

    def step(w):
        nt = (((1,), (1,)), ((), ()))
        gm = lax.dot_general(weighted[...], w[...], nt, preferred_element_type=F32)
        gm_ref[0] = gm
        square = jnp.sum(sq[0], axis=0, keepdims=True)
        dot = jnp.sum(gm * act_ref[0], axis=0, keepdims=True)
        for d in range(sums.shape[0]):
            sums[d, pl.ds(h, 1), :] = square
            sums[d, pl.ds(h + 4, 1), :] = dot
        gm_sum[pl.ds(h, 1), :] = jnp.sum(gm, axis=0, keepdims=True)

    with_rows(h, w_mine, w_other, step)


def mixed_grad(weighted, w_down, act, sq, members):
    pixels, width = weighted.shape
    block = w_down[0].shape[0] // 2
    cols = pl.BlockSpec((1, pixels, block), lambda h: (h, 0, 0))
    return pl.pallas_call(
        mixed_kernel,
        grid=(4,),
        in_specs=[
            whole_block(pixels, width),
            *half_rows(block, width),
            cols,
            pl.BlockSpec((1, 8, block), lambda h: (h, 0, 0)),
        ],
        out_specs=[cols, whole_block(members, 8, block), whole_block(4, block)],
        out_shape=[
            jax.ShapeDtypeStruct((4, pixels, block), F32),
            jax.ShapeDtypeStruct((members, 8, block), F32),
            jax.ShapeDtypeStruct((4, block), F32),
        ],
        compiler_params=params("arbitrary"),
        cost_estimate=cost(8),
        name="mixed_grad",
    )(weighted, *w_down, act, sq)


def ratio_of(sq, dot, gamma):
    energy = jnp.sqrt(sq)
    hid = energy.shape[0] * energy.shape[1]
    total = lambda x: jnp.sum(jnp.sum(x, axis=1, keepdims=True), axis=0, keepdims=True)
    mean = total(energy) / hid + EPS_NORM
    grad_ratio = gamma * dot
    shared = total(grad_ratio * energy) / (mean * mean) / hid
    return energy / mean, (grad_ratio / mean - shared) / energy


def store_rows(half, i, value):
    block = half.shape[0] // 2
    half[pl.ds(pl.multiple_of(i * block, block), block), :] = value


def outer(left, right):
    return lax.dot_general(left, right, (((0,), (0,)), ((), ())), preferred_element_type=F32).astype(BF16)


def down_rows_of(half, first, act, weighted, gamma, ratio, beta):
    def one(i, carry):
        row = pl.ds(first + i, 1)
        a = act[first + i]
        mixed = (gamma[row, :] * a * ratio[row, :] + beta[row, :] + a).astype(BF16)
        store_rows(half, i, outer(mixed, weighted[...]))
        return carry

    lax.fori_loop(0, 2, one, 0)


def down_other_kernel(act, weighted, sums, local, gm_sum, gamma, beta, other, ratio, twice, parts):
    crop = jnp.sum(sums[...], axis=0)
    r, t = ratio_of(crop[:4], crop[4:], gamma[...])
    ratio[...] = r
    twice[...] = t
    parts[0] = local[0, 4:, :] * r
    parts[1] = gm_sum[...]
    down_rows_of(other, 2, act, weighted, gamma, ratio, beta)


def down_other(act, weighted, sums, local, gm_sum, gamma, beta):
    _, pixels, block = act.shape
    width = weighted.shape[1]
    vec = jax.ShapeDtypeStruct((4, block), F32)
    return pl.pallas_call(
        down_other_kernel,
        in_specs=[IN_VMEM] * 7,
        out_specs=[IN_VMEM] * 4,
        out_shape=[
            jax.ShapeDtypeStruct((2 * block, width), BF16),
            vec,
            vec,
            jax.ShapeDtypeStruct((2, 4, block), F32),
        ],
        compiler_params=STAY,
        cost_estimate=cost(4),
        name="down_other",
    )(act, weighted, sums, local, gm_sum, gamma, beta)


def down_mine_kernel(act, weighted, ratio, gamma, beta, mine):
    down_rows_of(mine, 0, act, weighted, gamma, ratio, beta)


def down_mine(act, weighted, ratio, gamma, beta):
    _, pixels, block = act.shape
    width = weighted.shape[1]
    return pl.pallas_call(
        down_mine_kernel,
        in_specs=[IN_VMEM] * 5,
        out_specs=IN_VMEM,
        out_shape=jax.ShapeDtypeStruct((2 * block, width), BF16),
        compiler_params=STAY,
        cost_estimate=cost(4),
        name="down_mine",
    )(act, weighted, ratio, gamma, beta)


def hidden_kernel(
    act, slope, gm, w_mine, w_other, normed, ratio, twice, gamma, gain, xhat, rstd,
    mine, other, grad_conv, first, last, gain_part, total,
):
    h = pl.program_id(0)
    row = pl.ds(h, 1)
    grad_act = gm[0] * (gamma[row, :] * ratio[row, :] + 1.0) + act[0] * twice[row, :]
    grad_hidden = (grad_act * slope[0]).astype(BF16)
    term = outer(grad_hidden, normed[...])

    @pl.when(h == 0)
    def _():
        total[...] = jnp.dot(grad_hidden, w_mine[...], preferred_element_type=F32)
        mine[...] = term

    @pl.when(h == 1)
    def _():
        total[...] += jnp.dot(grad_hidden, w_mine[...], preferred_element_type=F32)
        mine[...] = term

    @pl.when(h >= 2)
    def _():
        total[...] += jnp.dot(grad_hidden, w_other[...], preferred_element_type=F32)
        other[...] = term

    @pl.when(h == 3)
    def _():
        pixels, width = total.shape
        block = 64

        def one(t, carry):
            at = pl.ds(pl.multiple_of(t * block, block), block)
            g = total[at, :]
            hat = xhat[at, :]
            carry = carry + jnp.sum((g * hat).reshape(block // 8, 8, width), axis=0)
            g = g * gain[...]
            mean_g = jnp.sum(g, axis=-1, keepdims=True) / width
            mean_gh = jnp.sum(g * hat, axis=-1, keepdims=True) / width
            out = rstd[at, 0:1] * (g - mean_g - hat * mean_gh)
            grad_conv[at, :] = out

            @pl.when(t * block < first.shape[0])
            def _():
                first[at, :] = out.astype(BF16)

            @pl.when(t * block >= pixels - last.shape[0])
            def _():
                last[pl.ds(pl.multiple_of(t * block - (pixels - last.shape[0]), block), block), :] = out.astype(BF16)

            return carry

        gain_part[...] = lax.fori_loop(0, pixels // block, one, jnp.zeros((8, width), F32))


def hidden_grad(act, slope, gm, w_up, normed, ratio, twice, gamma, gain, xhat, rstd, edge):
    _, pixels, block = act.shape
    width = normed.shape[1]
    cols = pl.BlockSpec((1, pixels, block), lambda h: (h, 0, 0))
    vec = whole_block(4, block)
    mine, other = half_rows(block, width)
    term = jax.ShapeDtypeStruct((2 * block, width), BF16)
    return pl.pallas_call(
        hidden_kernel,
        grid=(4,),
        in_specs=[
            cols, cols, cols, mine, other, whole_block(pixels, width), vec, vec, vec,
            whole_block(1, width), whole_block(pixels, width), whole_block(pixels, LANES),
        ],
        out_specs=[
            mine, other, whole_block(pixels, width), whole_block(edge, width), whole_block(edge, width),
            whole_block(8, width),
        ],
        out_shape=[
            term,
            term,
            jax.ShapeDtypeStruct((pixels, width), F32),
            jax.ShapeDtypeStruct((edge, width), BF16),
            jax.ShapeDtypeStruct((edge, width), BF16),
            jax.ShapeDtypeStruct((8, width), F32),
        ],
        scratch_shapes=[pltpu.VMEM((pixels, width), F32)],
        compiler_params=params("arbitrary"),
        cost_estimate=cost(14),
        name="hidden_grad",
    )(act, slope, gm, *w_up, normed, ratio, twice, gamma, gain.reshape(1, width), xhat, rstd)


def taps_grad_kernel(feat, above, below, grad, ktaps, xs, gs):
    cols = feat.shape[1]

    def chunk(n, lanes):
        fill_padded(xs, above, 0, lanes)
        fill_padded(xs, feat, 3, lanes)
        fill_padded(xs, below, 7, lanes)
        gs[...] = grad[:, :, lanes]
        for j in range(7):
            sums = [jnp.zeros((TILE, LANES), F32) for _ in range(7)]
            for start in range(0, cols, TILE):
                g = [gs[o, start : start + TILE, :] for o in range(4)]
                for r in range(10):
                    x = xs[r, PAD - 3 + j + start : PAD - 3 + j + start + TILE, :]
                    for o in range(4):
                        if 0 <= r - o <= 6:
                            sums[r - o] = sums[r - o] + x * g[o]
            for i in range(7):
                ktaps[i, j : j + 1, lanes] = jnp.sum(sums[i], axis=0, keepdims=True)

    each_chunk(chunk)


def taps_grad(feat, above, below, grad):
    rows, cols, width = feat.shape
    return pl.pallas_call(
        taps_grad_kernel,
        grid=(pl.cdiv(width, CHUNKS * LANES),),
        in_specs=[
            lane_blocks(rows, cols),
            lane_blocks(3, cols),
            lane_blocks(3, cols),
            lane_blocks(rows, cols),
        ],
        out_specs=lane_blocks(7, 7),
        out_shape=jax.ShapeDtypeStruct((7, 7, width), F32),
        scratch_shapes=[
            pltpu.VMEM((rows + 6, cols + 2 * PAD, LANES), F32),
            pltpu.VMEM((rows, cols, LANES), F32),
        ],
        compiler_params=params("arbitrary"),
        cost_estimate=cost(1),
        name="taps_grad",
    )(feat, above, below, grad)


def all_pairs():
    return [(r, o, r - o) for r in range(10) for o in range(4) if 0 <= r - o <= 6]


def conv_back_kernel(grad, above, below, k_ref, upstream, weight, out, xs, taps):
    cols = grad.shape[1]

    def chunk(n, lanes):
        fill_padded(xs, above, 0, lanes)
        fill_padded(xs, grad, 3, lanes)
        fill_padded(xs, below, 7, lanes)
        spread_taps(taps, k_ref, True, lanes)
        for start in range(0, cols, GROUP * TILE):
            acc = [[None] * GROUP for _ in range(4)]
            for o in range(4):
                for b in range(GROUP):
                    at = tile_rows(start, b)
                    acc[o][b] = upstream[o, at, lanes].astype(F32) * weight[o, at, :]
            acc = taps_group(xs, taps, all_pairs(), start, acc)
            for o in range(4):
                for b in range(GROUP):
                    out[o, tile_rows(start, b), lanes] = acc[o][b]

    each_chunk(chunk)


def conv_back(grad, above, below, kernel, upstream, weight):
    rows, cols, width = grad.shape
    return pl.pallas_call(
        conv_back_kernel,
        grid=(pl.cdiv(width, CHUNKS * LANES),),
        in_specs=[
            lane_blocks(rows, cols),
            lane_blocks(3, cols),
            lane_blocks(3, cols),
            lane_blocks(7, 7),
            lane_blocks(rows, cols),
            whole_block(rows, cols, LANES),
        ],
        out_specs=lane_blocks(rows, cols),
        out_shape=jax.ShapeDtypeStruct((rows, cols, width), F32),
        scratch_shapes=[
            pltpu.VMEM((rows + 6, cols + 2 * PAD, LANES), F32),
            pltpu.VMEM((49, TILE, LANES), F32),
        ],
        compiler_params=params("arbitrary"),
        cost_estimate=cost(60),
        name="conv_back",
    )(grad, above, below, kernel, upstream, weight)


def chip_kernel(mine, other, vector, edge, out):
    width = mine.shape[2]
    def one(q, carry):
        high = (mine[q, :128, :].astype(F32) + other[q, :128, :].astype(F32)).astype(BF16)
        low = mine[q, 128:, :].astype(F32) + other[q, 128:, :].astype(F32)
        for s in range(8):
            out[q * 8 + s, :16, :width] = high[16 * s : 16 * (s + 1), :]
            rest = low[6 * s : 6 * (s + 1), :]
            if vector is not None:
                at = q // 4 * 8 + s
                rest = jnp.concatenate([rest, vector[at]], axis=0)
                out[q * 8 + s, :16, width:] = edge[at, :16, :].astype(BF16)
                out[q * 8 + s, 16:, width:] = edge[at, 16:, :].astype(BF16)
            out[q * 8 + s, 16:, :width] = rest.astype(BF16)
        return carry

    lax.fori_loop(0, mine.shape[0], one, 0)


def chip_sum(mine, other, vector=None, edge=None):
    owners, owned, width = mine.shape
    if vector is None:
        given, piece, lanes = [], owned // 8, width
        kernel = lambda mine, other, out: chip_kernel(mine, other, None, None, out)
    else:
        given, piece, lanes = [vector, edge], owned // 8 + 2, width + edge.shape[2]
        kernel = chip_kernel
    return pl.pallas_call(
        kernel,
        in_specs=[IN_VMEM] * (2 + len(given)),
        out_specs=IN_VMEM,
        out_shape=jax.ShapeDtypeStruct((owners * 8, piece, lanes), BF16),
        compiler_params=STAY,
        cost_estimate=cost(0.3),
        name="chip_sum",
    )(mine, other, *given)


BOTH = ("dp", "space")


def device(y, z, c, x, low):
    return (y * 8 + z * 2 + c) * 8 + x * 2 + low


OWNERS = [
    [device(y, z, c, x, low ^ y) for y in range(2) for z in range(4)]
    for c in range(2)
    for x in range(4)
    for low in range(2)
]
CORES = [
    [device(y, z, c, x, low) for y in range(2) for z in range(4) for x in range(4) for low in range(2)]
    for c in range(2)
]


def moved(move):
    return [
        (device(y, z, c, x, low), device(*move(y, z, c, x, low)))
        for y in range(2)
        for z in range(4)
        for c in range(2)
        for x in range(4)
        for low in range(2)
    ]


def to_other_core(value):
    return lax.ppermute(value, BOTH, moved(lambda y, z, c, x, low: (y, z, 1 - c, x, low)))


def to_other_half(value):
    return lax.ppermute(value, BOTH, moved(lambda y, z, c, x, low: (1 - y, z, c, x, low)))


def copies(shard):
    return jnp.broadcast_to(shard, (8,) + shard.shape)


def gather_mine(shards):
    return lax.all_to_all(shards, BOTH, 0, 0, axis_index_groups=OWNERS)


def with_other(mine):
    other = to_other_core(mine)
    return mine.reshape(-1, mine.shape[2]), other.reshape(-1, mine.shape[2])


def local_order(vector, owned):
    first, second = core_halves(vector.reshape(8, 2, owned), 1)
    return jnp.concatenate([first.reshape(2, -1), second.reshape(2, -1)], axis=0)


def core_halves(value, axis):
    c = lax.axis_index("dp") % 2
    low, high = lax.index_in_dim(value, 0, axis, False), lax.index_in_dim(value, 1, axis, False)
    return jnp.where(c == 0, low, high), jnp.where(c == 0, high, low)


def global_order(blocks, owned):
    n = blocks.shape[0]
    low, high = core_halves(blocks.reshape(n, 2, 8, owned), 1)
    return jnp.stack([low, high], axis=2).reshape(n, -1)


def sum_blocks(blocks):
    return jnp.sum(lax.all_to_all(blocks, BOTH, 0, 0, axis_index_groups=CORES).astype(F32), axis=0)


def exchange(value, axis):
    return lax.all_to_all(value, axis, 0, 0)


def everyone(value, axis):
    return exchange(jnp.broadcast_to(value, (lax.axis_size(axis),) + value.shape), axis)


def shift(rows, pairs):
    flat = rows.reshape(-1, 16, rows.shape[-1])
    return lax.ppermute(flat, "space", pairs).reshape(rows.shape)


def body(
    features, kernel, norm_gain, w_up, grn_gamma, grn_beta, w_down, upstream, labels, class_weight
):
    crops, rows, cols, width = features.shape
    feat, up = features[0], upstream[0]
    space = lax.axis_size("space")
    dp = lax.axis_size("dp")
    owned = w_up.shape[0]
    hid = owned * dp
    pixels = rows * cols
    rising = [(i, i + 1) for i in range(space - 1)]
    falling = [(j, i) for i, j in rising]
    above = shift(feat[rows - 3 :], rising)
    below = shift(feat[:3], falling)
    w_up_mine = gather_mine(copies(w_up))
    inner, w_down = lax.optimization_barrier((feat, copies(w_down)))
    part = conv_own(inner, kernel)
    w_up_mine, w_down, part, above, below = lax.optimization_barrier((w_up_mine, w_down, part, above, below))
    w_down_mine = gather_mine(w_down)
    gamma, beta = local_order(grn_gamma, owned), local_order(grn_beta, owned)

    classes = jnp.arange(class_weight.shape[0], dtype=jnp.int32)
    pixel_weight = jnp.sum(jnp.where(labels[0][..., None] == classes, class_weight, 0.0), axis=-1)
    weight = jnp.broadcast_to(pixel_weight[..., None], (rows, cols, LANES))
    weighted = (up.astype(F32) * pixel_weight[..., None]).astype(BF16).reshape(pixels, width)

    normed, xhat, rstd = conv_norm(part, above, below, kernel, norm_gain)
    w_up_all = with_other(w_up_mine)
    act, slope, sq = up_project(normed, w_up_all)
    w_down_mine, sq = lax.optimization_barrier((w_down_mine, sq))
    w_down_all = with_other(w_down_mine)
    gm, local, gm_sum = mixed_grad(weighted, w_down_all, act, sq, space)
    sums = exchange(local, "space")
    down_other_term, ratio, twice, parts = down_other(act, weighted, sums, local, gm_sum, gamma, beta)
    by_owner = lambda rows: rows.reshape(8, owned, width)
    came = to_other_core(by_owner(down_other_term))
    down_blocks = chip_sum(by_owner(down_mine(act, weighted, ratio, gamma, beta)), came)
    ratio, down_blocks = lax.optimization_barrier((ratio, down_blocks))
    down_rows = sum_blocks(down_blocks)
    up_mine, up_other, grad_conv, g_first, g_last, gain_part = hidden_grad(
        act, slope, gm, w_up_all, normed, ratio, twice, gamma, norm_gain, xhat, rstd, 3 * cols
    )
    grad_conv = grad_conv.reshape(rows, cols, width)
    g_above = shift(g_last.reshape(3, cols, width), rising)
    g_below = shift(g_first.reshape(3, cols, width), falling)
    kernel_part = taps_grad(feat, above, below, grad_conv)

    scale = 1.0 / math.sqrt(dp * space * pixels)
    vector = jnp.concatenate(
        [
            kernel_part.reshape(49, width),
            jnp.sum(gain_part, axis=0, keepdims=True),
            global_order(parts, owned).reshape(-1, width),
        ],
        axis=0,
    )
    lines = vector.shape[0]
    vector = jnp.pad(vector, ((0, -lines % 64), (0, 0)))
    vector = (vector + to_other_core(vector)).reshape(16, 4, width)
    piece = owned // space
    lanes = 2 * width // piece
    edge = jnp.pad(vector[:, 2:].reshape(16, piece, lanes), ((0, 0), (0, 2), (0, 0)))
    up_blocks = chip_sum(by_owner(up_mine), to_other_core(by_owner(up_other)), vector[:, :2], edge)
    up_blocks, down_rows = lax.optimization_barrier((up_blocks, down_rows))
    up_rows = sum_blocks(up_blocks)
    grad_features = conv_back(grad_conv, g_above, g_below, kernel, up, weight)
    up_rows, grad_features = lax.optimization_barrier((up_rows, grad_features))

    vector = jnp.concatenate([up_rows[piece:, :width], up_rows[:piece, width:].reshape(2, width)], axis=0)
    there = to_other_half(vector)
    first = lax.axis_index("dp") < 8
    vector = jnp.concatenate([jnp.where(first, vector, there), jnp.where(first, there, vector)], axis=0)
    block = jnp.concatenate([up_rows[:piece, :width], down_rows], axis=1)
    block = jnp.concatenate([block, vector.reshape(4, 2 * width)], axis=0)
    block = everyone((scale * block).astype(BF16), "space").astype(F32)
    vector = jnp.transpose(block[:, piece:].reshape(space, 2, 4, width), (1, 0, 2, 3)).reshape(8 * space, width)
    kernel_sum = vector[:49].reshape(7, 7, width)
    gain_sum = vector[49]
    gamma_sum, beta_sum = vector[50:lines].reshape(2, hid)
    block = jnp.concatenate([block[:, :16].reshape(-1, 2 * width), block[:, 16:piece].reshape(-1, 2 * width)], axis=0)
    return (
        grad_features[None],
        kernel_sum,
        gain_sum,
        block[:, :width],
        gamma_sum,
        beta_sum,
        block[:, width:],
    )


def solution(mesh):
    return jax.shard_map(
        body,
        mesh=mesh,
        in_specs=(
            P("dp", "space", None, None),
            P(),
            P(),
            P("dp", None),
            P(),
            P(),
            P("dp", None),
            P("dp", "space", None, None),
            P("dp", "space", None),
            P(),
        ),
        out_specs=(P("dp", "space", None, None), P(), P(), P("dp", None), P(), P(), P("dp", None)),
        check_vma=False,
    )
```
